32 devices in a mesh: wide: 16 (over z, y, x), narrow: 2 (over core).
Axes of the slice: x: 2, y: 2, z: 4, core: 2. Of those that a mesh axis runs over, the one named last changes fastest.
Arguments:
- tokens: bfloat16 [16384, 640], P(('wide', 'narrow')), may hold values from -6 to 6
- lengths: int32 [32], P(('wide', 'narrow')), may hold values from 0 to 512, as said below
- w_qkv: bfloat16 [2, 1228800], P(None, ('wide', 'narrow')), may hold values from -0.25 to 0.25
- w_out: bfloat16 [2, 409600], P(None, ('wide', 'narrow')), may hold values from -0.625 to 0.625
- w_up: bfloat16 [2, 1638400], P(None, ('wide', 'narrow')), may hold values from -0.25 to 0.25
- w_down: bfloat16 [2, 1638400], P(None, ('wide', 'narrow')), may hold values from -0.125 to 0.125
- gains: bfloat16 [2560], P(('wide', 'narrow')), may hold values from 0.5 to 1.5
- biases: bfloat16 [14080], P(('wide', 'narrow')), may hold values from -1.25 to 1.25
- cotangent: bfloat16 [16384, 640], P(('wide', 'narrow')), may hold values from -6 to 6
Outputs:
- output: bfloat16 [16384, 640], P(('wide', 'narrow'))
- grad_tokens: bfloat16 [16384, 640], P(('wide', 'narrow'))
- grad_w_qkv: float32 [2, 1228800], P(None, ('wide', 'narrow'))
- grad_w_out: float32 [2, 409600], P(None, ('wide', 'narrow'))
- grad_w_up: float32 [2, 1638400], P(None, ('wide', 'narrow'))
- grad_w_down: float32 [2, 1638400], P(None, ('wide', 'narrow'))
- grad_gains: float32 [2560], P(('wide', 'narrow'))
- grad_biases: float32 [14080], P(('wide', 'narrow'))
The draws below stay inside these ranges and needn't reach their ends.
Inputs may be any that keep to these rules, and one draw needn't show every extreme that they name: `lengths`: 1 slots, drawn from the seed, hold no crop (length 0); every other slot holds a crop of 128 to 512 residues, and at least one crop has exactly 512.
All inputs are finite; a program needn't handle non-finite values.
Results may differ from the reference program's by a relative error of at most 0.014.
Values may be sent and summed in bfloat16 or wider, within the bound.
No kernel may reach another device: no remote copies, remote signals or barrier semaphores. Data moves between devices by JAX's collectives and lax.ppermute only.
A program may use at most 256 MiB of HBM per device.

```python
import jax
import jax.numpy as jnp
from jax import lax

D = 640
HEADS = 20
HEAD_DIM = 32
FF = 2560
LAYERS = 2
LEN = 512
SLOTS = 32
TOKENS = 16384
MIN_LEN = 128
EMPTY = 1


def draw_lengths(key, part):
    key = jax.random.fold_in(key, 11)
    key_base, key_order = jax.random.split(key)
    lengths_drawn = jax.random.randint(key_base, (SLOTS,), MIN_LEN, LEN + 1)
    slot_order = jax.random.permutation(key_order, SLOTS)
    slot_rank = jnp.zeros((SLOTS,), jnp.int32).at[slot_order].set(jnp.arange(SLOTS, dtype=jnp.int32))
    lengths_drawn = jnp.where(slot_rank == EMPTY, LEN, lengths_drawn)
    return jnp.where(slot_rank < EMPTY, 0, lengths_drawn).astype(jnp.int32)


def shard_levels(stream_key, extent, pieces, low, largest):
    def one(position, shards_of):
        heights = jax.random.uniform(jax.random.fold_in(jax.random.fold_in(stream_key, 6), position), (shards_of,), jnp.float32, low / len(pieces), largest / len(pieces))
        return jnp.repeat(jnp.exp(heights), extent[position] // shards_of).reshape((-1,) + (1,) * (len(extent) - position - 1))

    level = one(*pieces[0])
    for cut in pieces[1:]:
        level = level * one(*cut)
    return level


def scatter_about(rng, shape, width, reach, pieces=(), kind=jnp.bfloat16):
    entries = jax.random.normal(rng, shape, jnp.float32) * width
    if len(pieces) > 0:
        entries = shard_levels(rng, shape, pieces, -0.22, 0.18) * entries
    return jnp.clip(entries, min=-reach, max=reach).astype(kind)


def setup_inputs(seed: int = 0) -> dict:
    splits = jax.random.split(jax.random.key(seed), 10)
    tokens = scatter_about(splits[0], (TOKENS, D), 1.0, 6.0, ((0, 32),))
    lengths = draw_lengths(jax.random.fold_in(splits[9], 71), 0)
    w_qkv = scatter_about(splits[2], (LAYERS, 3 * D * D), D ** -0.5, 0.25, ((1, 32),))
    w_out = scatter_about(splits[3], (LAYERS, D * D), (D // 8) ** -0.5, 0.625, ((1, 32),))
    w_up = scatter_about(splits[4], (LAYERS, D * FF), D ** -0.5, 0.25, ((1, 32),))
    w_down = scatter_about(splits[5], (LAYERS, FF * D), FF ** -0.5, 0.125, ((1, 32),))
    gains = jnp.clip(1.0 + 0.1 * jax.random.normal(splits[6], (LAYERS * 2 * D,), jnp.float32), 0.5, 1.5).astype(jnp.bfloat16)
    biases = scatter_about(splits[7], (LAYERS * (7 * D + FF),), 0.2, 1.25, ((0, 32),))
    cotangent = scatter_about(splits[8], (TOKENS, D), 1.0, 6.0, ((0, 32),))
    return {"tokens": tokens, "lengths": lengths, "w_qkv": w_qkv, "w_out": w_out, "w_up": w_up, "w_down": w_down, "gains": gains, "biases": biases, "cotangent": cotangent}


@jax.custom_vjp
def low(v):
    return lax.optimization_barrier(v.astype(jnp.bfloat16)).astype(jnp.float32)

@jax.custom_vjp
def low_back(v):
    return v

def low_keep(v):
    return (low(v), None)

def low_pass(kept, grad):
    return (grad,)

def back_keep(v):
    return (v, None)

def back_low(kept, grad):
    return (low(grad),)
low.defvjp(low_keep, low_pass)
low_back.defvjp(back_keep, back_low)
EPSILON = 1e-05
MASKED = -1000000000.0

def rotary_tables(length, head_dim):
    half_dim = head_dim // 2
    steps_up = jnp.arange(half_dim, dtype=jnp.float32) * (2.0 / head_dim)
    inverse = 1.0 / 10000.0 ** steps_up
    angles = jnp.arange(length, dtype=jnp.float32)[:, None] * inverse[None, :]
    cosine_table = jnp.concatenate([jnp.cos(angles), jnp.cos(angles)], 1)
    sine_table = jnp.concatenate([jnp.sin(angles), jnp.sin(angles)], 1)
    return (cosine_table, sine_table)

def rotate(tensor, cosine_table, sine_table):
    half_dim = tensor.shape[-1] // 2
    turned = jnp.concatenate([-tensor[..., half_dim:], tensor[..., :half_dim]], -1)
    return tensor * cosine_table[:, None, :] + turned * sine_table[:, None, :]

def layer_norm(stream, gain, shift):
    average = lax.optimization_barrier(jnp.mean(stream, -1, keepdims=True))
    centered = stream - average
    variance = lax.optimization_barrier(jnp.mean(centered * centered, -1, keepdims=True))
    return centered * lax.rsqrt(variance + EPSILON) * gain + shift

def gelu_value(hidden_pre):
    return 0.5 * hidden_pre * (1.0 + lax.erf(hidden_pre * 0.7071067811865476))

def product(left, right):
    return jnp.dot(left, right, precision=lax.Precision.HIGHEST)

def unpack_layer(w_qkv, w_out, w_up, w_down, gains, biases, layer_index):
    gain_rows = gains.reshape(LAYERS, 2, D)[layer_index]
    bias_row = biases.reshape(LAYERS, 7 * D + FF)[layer_index]
    return (w_qkv[layer_index].reshape(D, 3 * D), w_out[layer_index].reshape(D, D), w_up[layer_index].reshape(D, FF), w_down[layer_index].reshape(FF, D), gain_rows[0], gain_rows[1], bias_row[:D], bias_row[D:4 * D], bias_row[4 * D:5 * D], bias_row[5 * D:6 * D], bias_row[6 * D:6 * D + FF], bias_row[6 * D + FF:])

def ref_layer(stream, keys_live, params, cosine_table, sine_table):
    w_qkv_full, w_out_full, w_up_full, w_down_full, gain_attn, gain_ffn, shift_attn, bias_qkv, bias_out, shift_ffn, bias_up, bias_down = params
    length = stream.shape[0]
    normed_attn = low(layer_norm(stream, gain_attn, shift_attn))
    projected = low_back(product(normed_attn, w_qkv_full) + bias_qkv)
    queries = projected[:, :D].reshape(length, HEADS, HEAD_DIM) * HEAD_DIM ** (-0.5)
    keys_plain = projected[:, D:2 * D].reshape(length, HEADS, HEAD_DIM)
    value_rows = low(projected[:, 2 * D:].reshape(length, HEADS, HEAD_DIM))
    rotated_queries = low(low_back(rotate(queries, cosine_table, sine_table)))
    rotated_keys = low(low_back(rotate(keys_plain, cosine_table, sine_table)))
    attention_scores = low_back(jnp.einsum('vap,jap->avj', rotated_queries, rotated_keys, precision=lax.Precision.HIGHEST))
    attention_scores = jnp.where(keys_live[None, None, :], attention_scores, MASKED)
    attention_probs = low(low_back(jax.nn.softmax(attention_scores, axis=-1)))
    attention_mixture = jnp.einsum('fos,sfc->ofc', attention_probs, value_rows, precision=lax.Precision.HIGHEST)
    attention_mixture = low(low_back(attention_mixture.reshape(length, D)))
    middle = stream + low_back(product(attention_mixture, w_out_full) + bias_out)
    normed_ffn = low(layer_norm(middle, gain_ffn, shift_ffn))
    hidden_pre = low_back(product(normed_ffn, w_up_full) + bias_up)
    hidden_act = low(low_back(gelu_value(hidden_pre)))
    return middle + low_back(product(hidden_act, w_down_full) + bias_down)

def forward(tokens32, lengths, weights):
    cosine_table, sine_table = rotary_tables(LEN, HEAD_DIM)
    layers_params = [unpack_layer(*weights, layer_index) for layer_index in range(LAYERS)]
    keys_live = jnp.arange(LEN, dtype=jnp.int32)[None, :] < lengths[:, None]

    def one_crop(stream, live_row):
        for params in layers_params:
            stream = ref_layer(stream, live_row, params, cosine_table, sine_table)
        return stream * live_row[:, None].astype(stream.dtype)
    batched = jax.checkpoint(jax.vmap(one_crop))
    crops = tokens32.reshape(SLOTS // 8, 8, LEN, D)
    live_groups = keys_live.reshape(SLOTS // 8, 8, LEN)
    result = lax.map(lambda crop_pair: batched(crop_pair[0], crop_pair[1]), (crops, live_groups))
    return result.reshape(TOKENS, D)

def reference(tokens, lengths, w_qkv, w_out, w_up, w_down, gains, biases, cotangent):
    inputs32 = tuple((member.astype(jnp.float32) for member in (tokens, w_qkv, w_out, w_up, w_down, gains, biases)))

    def forward_all(tokens32, *weights):
        return forward(tokens32, lengths, weights)
    output, pullback = jax.vjp(forward_all, *inputs32)
    gradients = pullback(cotangent.astype(jnp.float32))
    return (output.astype(jnp.bfloat16), gradients[0].astype(jnp.bfloat16), gradients[1], gradients[2], gradients[3], gradients[4], gradients[5], gradients[6])
```

```python
import functools

import jax
import jax.numpy as jnp
import numpy as np
from jax import lax
from jax.experimental import pallas as pl
from jax.experimental.pallas import tpu as pltpu
from jax.sharding import PartitionSpec as P

D = 640
HEADS = 20
HEAD_DIM = 32
FF = 2560
LAYERS = 2
EPSILON = 1e-05
MASKED = -1e9
LANES = 128
GROUPS = D // LANES
PER_GROUP = LANES // HEAD_DIM
BLOCKS = FF // D
PIECE = 80
VECS = 16
ROWS = 256
AXES = ("wide", "narrow")
VMEM_LIMIT = 56 * 1024 * 1024
f32, bf16 = jnp.float32, jnp.bfloat16

GAIN_A, GAIN_F, SHIFT_A, BIAS_QKV, BIAS_OUT, SHIFT_F, BIAS_UP, BIAS_DOWN = 0, 1, 2, 3, 6, 7, 8, 12


def rotary_tables(length):
    half = HEAD_DIM // 2
    inverse = 1.0 / 10000.0 ** (np.arange(half) * (2.0 / HEAD_DIM))
    angles = np.arange(length)[:, None] * inverse[None, :]
    cos = np.tile(np.cos(angles), (1, 2 * PER_GROUP))
    sine = np.sin(angles)
    none = np.zeros_like(sine)
    ahead = np.tile(np.concatenate([-sine, none], 1), (1, PER_GROUP))
    behind = np.tile(np.concatenate([none, sine], 1), (1, PER_GROUP))
    return np.stack([cos, ahead, behind]).astype(np.float32)


def dot(left, right):
    return jnp.dot(left, right, preferred_element_type=f32)


def dot_nt(left, right):
    return lax.dot_general(left, right, (((1,), (1,)), ((), ())), preferred_element_type=f32)


def dot_tn(left, right):
    return lax.dot_general(left, right, (((0,), (0,)), ((), ())), preferred_element_type=f32)


def rolled(value, table, rows, sign):
    half = HEAD_DIM // 2
    turned = pltpu.roll(value, LANES - half, 1) * table[1, rows, :] + pltpu.roll(value, half, 1) * table[2, rows, :]
    return value * table[0, rows, :] + (turned if sign > 0 else -turned)


def unit_of(value):
    centered = value - jnp.mean(value, -1, keepdims=True)
    inverse = lax.rsqrt(jnp.mean(centered * centered, -1, keepdims=True) + EPSILON)
    return centered * inverse, inverse


def norm_back(grad, unit, inverse, gain):
    scaled = grad * gain
    return inverse * (scaled - jnp.mean(scaled, -1, keepdims=True) - unit * jnp.mean(scaled * unit, -1, keepdims=True))


def column_sum(value):
    return jnp.sum(value, 0, keepdims=True)


def gelu_parts(value):
    scaled = jnp.abs(value) * 0.7071067811865476
    t = 1.0 / (1.0 + 0.3275911 * scaled)
    bell = jnp.exp(-scaled * scaled)
    series = t * (0.127414796 + t * (-0.142248368 + t * (0.7107068705 + t * (-0.7265760135 + t * 0.5307027145))))
    tail = series * bell
    return jnp.where(value >= 0.0, 1.0 - tail, tail), bell * 0.3989422804014327


def three_parts(value):
    first = value.astype(bf16)
    rest = value - first.astype(f32)
    second = rest.astype(bf16)
    third = (rest - second.astype(f32)).astype(bf16)
    return first, second, third


def spread(value):
    lane = lax.broadcasted_iota(jnp.int32, value.shape, 1) % HEAD_DIM
    first, second, third = three_parts(value)
    tail = jnp.where(lane == 3, 1.0, 0.0)
    out = jnp.where(lane == 2, third.astype(f32), tail)
    out = jnp.where(lane == 1, second.astype(f32), out)
    return jnp.where(lane == 0, first.astype(f32), out).astype(bf16)


def row_loop(length, step, body):
    def run(i, carry):
        body(pl.ds(pl.multiple_of(i * step, step), step), i)
        return carry

    lax.fori_loop(0, length // step, run, 0)


def place(coords, piece, kz):
    kx, kn, ky = piece // 4, piece // 2 % 2, piece % 2
    z, y, x, n = coords[0] ^ kz, coords[1] ^ ky, coords[2] ^ kx, coords[3] ^ kn
    return z, y, x, n


def quarter_copies(coords, pieces, whole, sems):
    copies = []
    for piece in range(8):
        for kz in range(4):
            z, y, x, n = place(coords, piece, kz)
            rows = pl.ds(pl.multiple_of((2 * z + y) * PIECE, PIECE), PIECE)
            columns = pl.ds(pl.multiple_of((2 * x + n) * D, D), D)
            copies.append(
                pltpu.make_async_copy(
                    pieces[piece].at[kz, pl.ds(0, PIECE)], whole.at[rows, columns], sems.at[4 * piece + kz]
                )
            )
    return copies


def row_copies(coords, pieces, whole, sems):
    copies = []
    for piece in range(8):
        for kz in range(4):
            z, y, x, n = place(coords, piece, kz)
            rows = pl.ds(pl.multiple_of((8 * z + 4 * y + 2 * x + n) * PIECE, PIECE), PIECE)
            copies.append(pltpu.make_async_copy(pieces[piece].at[kz], whole.at[rows], sems.at[4 * piece + kz]))
    return copies


def head_masks():
    lane = lax.broadcasted_iota(jnp.int32, (1, LANES), 1)
    return [(lane // HEAD_DIM == head).astype(f32).astype(bf16) for head in range(PER_GROUP)]


def key_tail(length, live, head):
    lane = lax.broadcasted_iota(jnp.int32, (length, LANES), 1)
    row = lax.broadcasted_iota(jnp.int32, (length, LANES), 0)
    base = head * HEAD_DIM
    ones = jnp.where((lane >= base) & (lane < base + 3), 1.0, 0.0)
    return jnp.where((lane == base + 3) & (row >= live), MASKED, ones).astype(bf16)


def attn_fwd_kernel(coords, x_ref, vec_ref, table_ref, *refs):
    pieces, refs = refs[:8], refs[8:]
    a_ref, qkv_ref, o_ref, lse_ref, m_ref, b_ref, w_ref, key_ref, val_ref, sems = refs
    length = x_ref.shape[0]
    copies = quarter_copies(coords, pieces, w_ref, sems)
    for copy in copies:
        copy.start()

    def norm(rows, _):
        unit, _ = unit_of(x_ref[rows, :].astype(f32))
        a_ref[rows, :] = (unit * vec_ref[GAIN_A : GAIN_A + 1, :] + vec_ref[SHIFT_A : SHIFT_A + 1, :]).astype(bf16)

    row_loop(length, 128, norm)
    for copy in copies:
        copy.wait()

    def project(rows, _):
        normed = a_ref[rows, :]
        for part in range(3):
            out = dot(normed, w_ref[:, part * D : (part + 1) * D]) + vec_ref[BIAS_QKV + part : BIAS_QKV + part + 1, :]
            if part == 0:
                out = out * HEAD_DIM**-0.5
            for group in range(GROUPS):
                piece = out[:, group * LANES : (group + 1) * LANES]
                if part < 2:
                    piece = rolled(piece, table_ref, rows, 1)
                qkv_ref[rows, part * D + group * LANES : part * D + (group + 1) * LANES] = piece.astype(bf16)

    row_loop(length, ROWS, project)
    live = coords[4]
    masks = head_masks()
    for head in range(PER_GROUP):
        key_ref[head, :, LANES:] = key_tail(length, live, head)
        val_ref[head, :, LANES:] = jnp.broadcast_to(masks[head], (length, LANES))

    def group_step(group, carry):
        at = [pl.ds(pl.multiple_of(part * D + group * LANES, LANES), LANES) for part in range(3)]
        for head in range(PER_GROUP):
            key_ref[head, :, :LANES] = qkv_ref[:, at[1]] * masks[head]
            val_ref[head, :, :LANES] = qkv_ref[:, at[2]] * masks[head]

        def rows_step(rows, _):
            lane = lax.broadcasted_iota(jnp.int32, (ROWS, LANES), 1)
            tail = jnp.where(lane % HEAD_DIM == 3, 1.0, 0.0).astype(bf16)
            query = jnp.concatenate([qkv_ref[rows, at[0]], tail], 1)
            total = jnp.zeros((ROWS, 2 * LANES), f32)
            tops = jnp.zeros((ROWS, LANES), f32)
            for head in range(PER_GROUP):
                scores = dot_nt(query, key_ref[head])
                top = jnp.max(scores, -1, keepdims=True)
                total = total + dot(jnp.exp(scores - top).astype(bf16), val_ref[head])
                tops = jnp.where(lane // HEAD_DIM == head, top, tops)
            o_ref[rows, at[0]] = (total[:, :LANES] / total[:, LANES:]).astype(bf16)
            lse_ref[rows, at[0]] = spread(-(tops + jnp.log(total[:, LANES:])))

        row_loop(length, ROWS, rows_step)
        return carry

    lax.fori_loop(0, GROUPS, group_step, 0)

    def after(rows, _):
        middle = x_ref[rows, :].astype(f32) + (dot(o_ref[rows, :], w_ref[:, 3 * D :]) + vec_ref[BIAS_OUT : BIAS_OUT + 1, :])
        m_ref[rows, :] = middle
        unit, _ = unit_of(middle)
        b_ref[rows, :] = (unit * vec_ref[GAIN_F : GAIN_F + 1, :] + vec_ref[SHIFT_F : SHIFT_F + 1, :]).astype(bf16)

    row_loop(length, ROWS, after)


def ffn_fwd_kernel(last, coords, m_ref, b_ref, vec_ref, *refs):
    up_pieces, down_pieces, refs = refs[:8], refs[8:16], refs[16:]
    y_ref, z_ref, slope_ref, up_ref, down_ref, up_sems, down_sems = refs
    length = m_ref.shape[0]
    copies = quarter_copies(coords, up_pieces, up_ref, up_sems)
    copies_down = row_copies(coords, down_pieces, down_ref, down_sems)
    for copy in copies + copies_down:
        copy.start()
    for copy in copies + copies_down:
        copy.wait()

    def step(rows, i):
        normed = b_ref[rows, :]
        for block in range(BLOCKS):
            columns = slice(block * D, (block + 1) * D)
            pre = dot(normed, up_ref[:, columns]) + vec_ref[BIAS_UP + block : BIAS_UP + block + 1, :]
            cdf, bell = gelu_parts(pre)
            z_ref[rows, columns] = (pre * cdf).astype(bf16)
            slope_ref[rows, columns] = (cdf + pre * bell).astype(bf16)
        out = m_ref[rows, :] + (dot(z_ref[rows, :], down_ref[...]) + vec_ref[BIAS_DOWN : BIAS_DOWN + 1, :])
        if last:
            row = lax.broadcasted_iota(jnp.int32, (ROWS, 1), 0) + i * ROWS
            out = jnp.where(row < coords[4], out, 0.0)
        y_ref[rows, :] = out.astype(y_ref.dtype)

    row_loop(length, ROWS, step)


def ffn_bwd_kernel(first, coords, g_ref, z_ref, slope_ref, m_ref, vec_ref, *refs):
    up_pieces, down_pieces, refs = refs[:8], refs[8:16], refs[16:]
    gb_ref, gu_ref, gm_ref, gmb_ref, sums_ref, up_ref, down_ref, up_sems, down_sems = refs
    length = m_ref.shape[0]
    copies = quarter_copies(coords, up_pieces, up_ref, up_sems)
    copies_down = row_copies(coords, down_pieces, down_ref, down_sems)
    for copy in copies_down + copies:
        copy.start()
    for copy in copies_down + copies:
        copy.wait()
    sums_ref[...] = jnp.zeros_like(sums_ref)

    def add(row, value):
        sums_ref[row : row + 1, :] += column_sum(value)

    def step(rows, i):
        grad = g_ref[rows, :].astype(f32)
        if first:
            row = lax.broadcasted_iota(jnp.int32, (ROWS, 1), 0) + i * ROWS
            grad = jnp.where(row < coords[4], grad, 0.0)
        low = grad.astype(bf16)
        gb_ref[rows, :] = low
        add(BIAS_DOWN, low.astype(f32))
        for block in range(BLOCKS):
            columns = slice(block * D, (block + 1) * D)
            back = dot_nt(low, down_ref[columns, :]) * slope_ref[rows, columns].astype(f32)
            part = back.astype(bf16)
            gu_ref[rows, columns] = part
            add(BIAS_UP + block, part.astype(f32))
        normed_grad = dot_nt(gu_ref[rows, :], up_ref[...])
        unit, inverse = unit_of(m_ref[rows, :])
        add(GAIN_F, normed_grad * unit)
        add(SHIFT_F, normed_grad)
        middle = grad + norm_back(normed_grad, unit, inverse, vec_ref[GAIN_F : GAIN_F + 1, :])
        gm_ref[rows, :] = middle
        low = middle.astype(bf16)
        gmb_ref[rows, :] = low
        add(BIAS_OUT, low.astype(f32))

    row_loop(length, ROWS, step)


def attn_bwd_kernel(coords, gm_ref, gmb_ref, qkv_ref, o_ref, lse_ref, x_ref, vec_ref, table_ref, *refs):
    pieces, refs = refs[:8], refs[8:]
    gpm_ref, gx_ref, sums_ref, w_ref, go_ref, key_ref, val_ref, q_ref, g_ref, dq_ref, sems = refs
    length = x_ref.shape[0]
    copies = quarter_copies(coords, pieces, w_ref, sems)
    for copy in copies:
        copy.start()
    for copy in copies:
        copy.wait()
    sums_ref[...] = jnp.zeros_like(sums_ref)

    def add(row, value):
        sums_ref[row : row + 1, :] += column_sum(value)

    def first(rows, _):
        low = gmb_ref[rows, :]
        gpm_ref[rows, 3 * D :] = low
        go_ref[rows, :] = dot_nt(low, w_ref[:, 3 * D :]).astype(bf16)

    row_loop(length, ROWS, first)
    live = coords[4]
    masks = head_masks()
    head_of = lax.broadcasted_iota(jnp.int32, (LANES, LANES), 0) // HEAD_DIM
    same = (head_of == lax.broadcasted_iota(jnp.int32, (LANES, LANES), 1) // HEAD_DIM).astype(f32).astype(bf16)
    for head in range(PER_GROUP):
        key_ref[head, :, LANES:] = key_tail(length, live, head)
        val_ref[head, :, LANES:] = key_tail(length, length, head)

    def group_step(group, carry):
        at = [pl.ds(pl.multiple_of(part * D + group * LANES, LANES), LANES) for part in range(3)]
        grad = go_ref[:, at[0]]
        query = qkv_ref[:, at[0]]
        product = grad.astype(f32) * o_ref[:, at[0]].astype(f32)
        high = product.astype(bf16)
        rest = (product - high.astype(f32)).astype(bf16)
        deltas = dot(high, same) + dot(rest, same)
        for head in range(PER_GROUP):
            key_ref[head, :, :LANES] = qkv_ref[:, at[1]] * masks[head]
            val_ref[head, :, :LANES] = qkv_ref[:, at[2]] * masks[head]
            q_ref[head] = query * masks[head]
            g_ref[head] = grad * masks[head]
        query_wide = jnp.concatenate([query, lse_ref[:, at[0]]], 1)
        grad_wide = jnp.concatenate([grad, spread(-deltas)], 1)
        dq_ref[...] = jnp.zeros_like(dq_ref)

        def rows_step(rows, _):
            dk = jnp.zeros((ROWS, LANES), f32)
            dv = jnp.zeros((ROWS, LANES), f32)
            for head in range(PER_GROUP):
                key = key_ref[head, rows, :]
                probs = jnp.exp(dot_nt(key, query_wide))
                scores = (probs * dot_nt(val_ref[head, rows, :], grad_wide)).astype(bf16)
                dv = dv + dot(probs.astype(bf16), g_ref[head])
                dk = dk + dot(scores, q_ref[head])
                dq_ref[...] += dot_tn(scores, key[:, :LANES])
            dk = rolled(dk.astype(bf16).astype(f32), table_ref, rows, -1)
            gpm_ref[rows, at[1]] = dk.astype(bf16)
            gpm_ref[rows, at[2]] = dv.astype(bf16)

        row_loop(length, ROWS, rows_step)

        def last_step(rows, _):
            dq = rolled(dq_ref[rows, :].astype(bf16).astype(f32), table_ref, rows, -1) * HEAD_DIM**-0.5
            gpm_ref[rows, at[0]] = dq.astype(bf16)

        row_loop(length, ROWS, last_step)
        return carry

    lax.fori_loop(0, GROUPS, group_step, 0)

    def after(rows, _):
        for part in range(3):
            add(BIAS_QKV + part, gpm_ref[rows, part * D : (part + 1) * D].astype(f32))
        normed_grad = dot_nt(gpm_ref[rows, : 3 * D], w_ref[:, : 3 * D])
        unit, inverse = unit_of(x_ref[rows, :].astype(f32))
        add(GAIN_A, normed_grad * unit)
        add(SHIFT_A, normed_grad)
        out = gm_ref[rows, :] + norm_back(normed_grad, unit, inverse, vec_ref[GAIN_A : GAIN_A + 1, :])
        gx_ref[rows, :] = out.astype(gx_ref.dtype)

    row_loop(length, ROWS, after)


def emit(coords, outs, second, kn, kx, ky, kz, value):
    core_ref, a_ref, b_ref, keep_ref = outs
    rows = slice(0, PIECE)
    ka, kb = (kx, ky) if second == "y" else (ky, kx)
    if kn:
        core_ref[ka, kb, kz, rows] = value
    elif ka:
        a_ref[kb, kz, rows] = value
    elif kb:
        b_ref[kz, rows] = value
    else:
        keep_ref[kz, rows] = value


def quarter_grad_kernel(second, coords, left_ref, right_ref, *refs):
    outs, (flip_ref, tmp_ref) = refs[-6:-2], refs[-2:]
    count = flip_ref.shape[0]
    for i in range(count):
        flip_ref[i] = (left_ref[i] if count > 1 else left_ref[...]).T
    for kn in (1, 0):
        for kx in (1, 0):
            quarter = 2 * (coords[2] ^ kx) + (coords[3] ^ kn)
            columns = pl.ds(pl.multiple_of(quarter * D, D), D)
            left = flip_ref[quarter // 3] if count > 1 else flip_ref[0]
            tmp_ref[...] = dot(left, right_ref[:, columns])
            for ky in range(2):
                for kz in range(4):
                    group = 2 * (coords[0] ^ kz) + (coords[1] ^ ky)
                    value = tmp_ref[pl.ds(pl.multiple_of(group * PIECE, PIECE), PIECE), :].astype(bf16)
                    emit(coords, outs, second, kn, kx, ky, kz, value)


def row_grad_kernel(second, coords, left_ref, right_ref, *refs):
    outs, (tmp_ref,) = refs[:4], refs[4:]
    for block in range(BLOCKS):
        columns = slice(block * D, (block + 1) * D)
        tmp_ref[columns, :] = dot(left_ref[:, columns].T, right_ref[...])
    for kn in (1, 0):
        for kx in (1, 0):
            for ky in range(2):
                for kz in range(4):
                    z, y, x, n = coords[0] ^ kz, coords[1] ^ ky, coords[2] ^ kx, coords[3] ^ kn
                    start = pl.multiple_of((8 * z + 4 * y + 2 * x + n) * PIECE, PIECE)
                    emit(coords, outs, second, kn, kx, ky, kz, tmp_ref[pl.ds(start, PIECE), :].astype(bf16))


def call(kernel, ins, outs, scratch, name, flops, exps=0):
    moved = sum(a.size * a.dtype.itemsize for a, _ in ins) + sum(int(np.prod(s)) * jnp.dtype(t).itemsize for s, t in outs)
    return pl.pallas_call(
        kernel,
        out_shape=[jax.ShapeDtypeStruct(s, t) for s, t in outs],
        in_specs=[pl.BlockSpec(memory_space=space) for _, space in ins],
        out_specs=[pl.BlockSpec(memory_space=pltpu.VMEM)] * len(outs),
        scratch_shapes=scratch,
        compiler_params=pltpu.CompilerParams(vmem_limit_bytes=VMEM_LIMIT),
        cost_estimate=pl.CostEstimate(flops=int(flops), bytes_accessed=int(moved), transcendentals=int(exps)),
        name=name,
    )(*[a for a, _ in ins])


V, S, H = pltpu.VMEM, pltpu.SMEM, pl.ANY
SEMS = pltpu.SemaphoreType.DMA


def attn_fwd(coords, x, vec, table, pieces):
    n = x.shape[0]
    ins = [(coords, S), (x, V), (vec, V), (table, V)] + [(p, H) for p in pieces]
    outs = [((n, D), bf16), ((n, 3 * D), bf16), ((n, D), bf16), ((n, D), bf16), ((n, D), f32), ((n, D), bf16)]
    scratch = [V((D, FF), bf16), V((PER_GROUP, n, 2 * LANES), bf16), V((PER_GROUP, n, 2 * LANES), bf16), SEMS((32,))]
    return call(attn_fwd_kernel, ins, outs, scratch, "attn_fwd", 2 * n * D * FF + 4 * n * n * D, HEADS * n * n)


def ffn_fwd(coords, m, b, vec, up, down, last):
    n = m.shape[0]
    ins = [(coords, S), (m, V), (b, V), (vec, V)] + [(p, H) for p in up + down]
    outs = [((n, D), bf16 if last else f32), ((n, FF), bf16), ((n, FF), bf16)]
    scratch = [V((D, FF), bf16), V((FF, D), bf16), SEMS((32,)), SEMS((32,))]
    return call(functools.partial(ffn_fwd_kernel, last), ins, outs, scratch, "ffn_fwd", 4 * n * D * FF, 2 * n * FF)


def ffn_bwd(coords, g, z, slope, m, vec, up, down, first):
    n = m.shape[0]
    ins = [(coords, S), (g, V), (z, V), (slope, V), (m, V), (vec, V)] + [(p, H) for p in up + down]
    outs = [((n, D), bf16), ((n, FF), bf16), ((n, D), f32), ((n, D), bf16), ((VECS, D), f32)]
    scratch = [V((D, FF), bf16), V((FF, D), bf16), SEMS((32,)), SEMS((32,))]
    return call(functools.partial(ffn_bwd_kernel, first), ins, outs, scratch, "ffn_bwd", 4 * n * D * FF, 0)


def attn_bwd(coords, gm, gmb, qkv, o, lse, x, vec, table, pieces, last):
    n = x.shape[0]
    ins = [(coords, S)] + [(a, V) for a in (gm, gmb, qkv, o, lse, x, vec, table)] + [(p, H) for p in pieces]
    outs = [((n, FF), bf16), ((n, D), bf16 if last else f32), ((VECS, D), f32)]
    wide, thin = V((PER_GROUP, n, 2 * LANES), bf16), V((PER_GROUP, n, LANES), bf16)
    scratch = [V((D, FF), bf16), V((n, D), bf16), wide, wide, thin, thin, V((n, LANES), f32), SEMS((32,))]
    return call(attn_bwd_kernel, ins, outs, scratch, "attn_bwd", 2 * n * D * FF + 10 * n * n * D, HEADS * n * n)


def grad_outs(rows):
    return [((2, 2, 4, rows, D), bf16), ((2, 4, rows, D), bf16), ((4, rows, D), bf16), ((4, rows, D), bf16)]


def quarter_grad(coords, left, right, second):
    count = left.shape[0] if left.ndim == 3 else 1
    n = right.shape[0]
    scratch = [V((count, D, n), bf16), V((D, D), f32)]
    ins = [(coords, S), (left, V), (right, V)]
    return call(functools.partial(quarter_grad_kernel, second), ins, grad_outs(PIECE), scratch, "quarter_grad", 2 * n * D * FF)


def row_grad(coords, left, right, second):
    n = right.shape[0]
    ins = [(coords, S), (left, V), (right, V)]
    return call(functools.partial(row_grad_kernel, second), ins, grad_outs(PIECE), [V((FF, D), f32)], "row_grad", 2 * n * D * FF)


def swap(axis_name, bit):
    size = lax.axis_size(axis_name)
    pairs = [(i, i ^ bit) for i in range(size)]
    return lambda value: lax.ppermute(value, axis_name, pairs)


NARROW = ("narrow", 1)
LINK = {"x": ("wide", 1), "y": ("wide", 2)}


def relative(values, bits):
    for place_of, bit in enumerate(reversed(bits)):
        step = 1 << place_of
        values = [jnp.where(bit > 0, values[i ^ step], values[i]) for i in range(len(values))]
    return values


def gather_blocks(block, first):
    second = "x" if first == "y" else "y"
    zs = jnp.stack([block] + [swap("wide", 4 * k)(block) for k in (1, 2, 3)])
    near = {0: zs, 1: swap(*LINK[first])(zs)}
    far = {k: swap(*LINK[second])(near[k]) for k in (0, 1)}
    pieces = [None] * 8
    for kx in range(2):
        for ky in range(2):
            ka, kb = (kx, ky) if first == "x" else (ky, kx)
            held = far[ka] if kb else near[ka]
            pieces[4 * kx + ky] = held
            pieces[4 * kx + 2 + ky] = swap(*NARROW)(held)
    return pieces


def add(*terms):
    return functools.reduce(lambda p, q: p + q, [t.astype(f32) for t in terms])


def scatter_blocks(sends, second):
    first = "x" if second == "y" else "y"
    core, a, b, keep = sends
    core = swap(*NARROW)(core)
    a = swap(*LINK[first])(add(a, core[1]).astype(bf16))
    b = swap(*LINK[second])(add(b, core[0, 1], a[1]).astype(bf16))
    total = add(keep, core[0, 0], a[0], b)
    return add(total[0], *[swap("wide", 4 * k)(total[k].astype(bf16)) for k in (1, 2, 3)])


def regroup(parts, bits):
    mine = relative(parts, bits)
    return relative([mine[0]] + [swap(AXES, k)(mine[k]) for k in (1, 2, 3)], bits)


def vector_tables(gains, biases):
    gains = gains.astype(f32).reshape(LAYERS, 2, D)
    biases = biases.astype(f32).reshape(LAYERS, 11, D)
    return jnp.concatenate([gains, biases, jnp.zeros((LAYERS, VECS - 13, D), f32)], 1)


def whole_pieces(matrix, by_rows):
    if by_rows:
        cut = matrix.reshape(4, 2, 2, 2, PIECE, D)
        return [cut[:, ky, kx, kn] for kx in range(2) for kn in range(2) for ky in range(2)]
    cut = matrix.reshape(4, 2, PIECE, 4, D)
    return [cut[:, ky, :, 2 * kx + kn] for kx in range(2) for kn in range(2) for ky in range(2)]


def whole_grad(sends, second, by_rows):
    core, a, b, keep = sends
    kept = jnp.stack([jnp.stack([keep, b]), a])
    cut = jnp.stack([kept, core])
    if second == "x":
        cut = jnp.swapaxes(cut, 1, 2)
    if by_rows:
        return jnp.transpose(cut, (3, 2, 1, 0, 4, 5)).reshape(FF, D)
    return jnp.transpose(cut, (3, 2, 4, 1, 0, 5)).reshape(D, FF)


FIRST = {("attn", 0): "y", ("up", 0): "x", ("down", 0): "y", ("attn", 1): "x", ("up", 1): "y", ("down", 1): "x"}
NAMES = ("attn", "up", "down")


def fetch(w_qkv, w_out, w_up, w_down, gains, biases, bits):
    rows = D // 32
    z1, z0, y, x, n = bits
    attn = [jnp.concatenate([w_qkv[l].reshape(rows, 3 * D), w_out[l].reshape(rows, D)], 1) for l in range(LAYERS)]
    ups = [w_up[l].reshape(rows, FF) for l in range(LAYERS)]
    cut = jnp.stack([attn[0], ups[0], attn[1], ups[1]])
    parts = [cut[:, :, s * D : (s + 1) * D] for s in range(4)]
    blocks = jnp.concatenate(regroup(parts, [x, n]), 1)
    mine = jnp.concatenate([gains, biases])
    width = mine.shape[0]
    tail = jnp.zeros((16, D), bf16).at[0, :width].set(mine)
    shards = {
        ("attn", 0): jnp.concatenate([blocks[0], tail]),
        ("up", 0): blocks[1],
        ("attn", 1): blocks[2],
        ("up", 1): blocks[3],
        ("down", 0): w_down[0].reshape(PIECE, D),
        ("down", 1): w_down[1].reshape(PIECE, D),
    }
    weights = {(name, l): gather_blocks(shards[name, l], FIRST[name, l]) for l in range(LAYERS) for name in NAMES}
    cut = jnp.stack([p[:, PIECE, :width] for p in weights["attn", 0]]).reshape(2, 2, 2, 2, 2, width)
    cut = jnp.transpose(cut, (3, 4, 2, 0, 1, 5))
    for axis, bit in enumerate(bits):
        cut = jnp.where(bit > 0, jnp.flip(cut, axis), cut)
    cut = cut.reshape(32, width)
    return weights, vector_tables(cut[:, : gains.shape[0]].reshape(-1), cut[:, gains.shape[0] :].reshape(-1))


def fetch_plain(w_qkv, w_out, w_up, w_down, gains, biases):
    def whole(value, rows):
        return lax.all_gather(value, AXES, axis=0, tiled=True).reshape(rows, -1)

    weights = {}
    for l in range(LAYERS):
        attn = jnp.concatenate([whole(w_qkv[l], D), whole(w_out[l], D)], 1)
        weights["attn", l] = whole_pieces(attn, False)
        weights["up", l] = whole_pieces(whole(w_up[l], D), False)
        weights["down", l] = whole_pieces(whole(w_down[l], FF), True)
    return weights, vector_tables(whole(gains, 1)[0], whole(biases, 1)[0])


def body(tokens, lengths, w_qkv, w_out, w_up, w_down, gains, biases, cotangent):
    length = tokens.shape[0] // lengths.shape[0]
    devices = lax.axis_size(AXES)
    fast = lax.axis_size("wide") == 16 and lax.axis_size("narrow") == 2
    wide, narrow = lax.axis_index("wide"), lax.axis_index("narrow")
    bits = [(wide >> 3) & 1, (wide >> 2) & 1, (wide >> 1) & 1, wide & 1, narrow]
    if fast:
        at = [wide >> 2, bits[2], bits[3], bits[4]]
        weights, vectors = fetch(w_qkv, w_out, w_up, w_down, gains, biases, bits)
    else:
        at = [jnp.int32(0)] * 4
        weights, vectors = fetch_plain(w_qkv, w_out, w_up, w_down, gains, biases)
    coords = jnp.stack([jnp.asarray(c, jnp.int32) for c in at + [lengths[0]]])
    table = jnp.asarray(rotary_tables(length))

    x = tokens
    kept = []
    for l in range(LAYERS):
        last = l == LAYERS - 1
        a, qkv, o, lse, m, b = attn_fwd(coords, x, vectors[l], table, weights["attn", l])
        y, z, slope = ffn_fwd(coords, m, b, vectors[l], weights["up", l], weights["down", l], last)
        kept.append((x, a, qkv, o, lse, m, b, z, slope))
        x = y
    output = x

    grad = cotangent
    sends, sums = {}, [None] * LAYERS
    for l in reversed(range(LAYERS)):
        x, a, qkv, o, lse, m, b, z, slope = kept[l]
        gb, gu, gm, gmb, sums_f = ffn_bwd(
            coords, grad, z, slope, m, vectors[l], weights["up", l], weights["down", l], l == LAYERS - 1
        )
        sends["down", l] = row_grad(coords, z, gb, FIRST["down", l])
        sends["up", l] = quarter_grad(coords, b, gu, FIRST["up", l])
        gpm, grad, sums_a = attn_bwd(coords, gm, gmb, qkv, o, lse, x, vectors[l], table, weights["attn", l], l == 0)
        sends["attn", l] = quarter_grad(coords, jnp.stack([a, o]), gpm, FIRST["attn", l])
        sums[l] = sums_f + sums_a
    sums = jnp.stack(sums)
    gain_sums, bias_sums = sums[:, :2].reshape(devices, -1), sums[:, 2:13].reshape(devices, -1)

    if not fast:
        outs = []
        for name, parts in (("attn", (3 * D, D)), ("up", (FF,)), ("down", (D,))):
            layers = [whole_grad(sends[name, l], FIRST[name, l], name == "down").astype(f32) for l in range(LAYERS)]
            start = 0
            for width in parts:
                cut = jnp.stack([g[:, start : start + width].reshape(-1) for g in layers])
                outs.append(lax.psum_scatter(cut, AXES, scatter_dimension=1, tiled=True))
                start += width
        small = [lax.psum_scatter(v.reshape(-1), AXES, scatter_dimension=0, tiled=True) for v in (gain_sums, bias_sums)]
        return (output, grad, *outs, *small)

    small = jnp.concatenate([gain_sums, bias_sums], 1)
    width = small.shape[1]
    small = small.reshape(2, 2, 2, 2, 2, width)
    for axis, bit in enumerate(bits):
        small = jnp.where(bit > 0, jnp.flip(small, axis), small)
    small = jnp.transpose(small, (4, 3, 2, 0, 1, 5)).reshape(2, 2, 2, 4, 1, width)
    if FIRST["attn", 0] == "x":
        small = jnp.swapaxes(small, 1, 2)
    small = jnp.pad(small, ((0, 0),) * 4 + ((0, 15), (0, D - width))).astype(bf16)
    ends = (small[1], small[0, 1], small[0, 0, 1], small[0, 0, 0])
    sends["attn", 0] = [jnp.concatenate([s, e], -2) for s, e in zip(sends["attn", 0], ends, strict=True)]
    sums = {key: scatter_blocks(value, FIRST[key]) for key, value in sends.items()}
    mine = sums["attn", 0][PIECE, :width]
    rows = D // 32
    shares = {}
    for keys in ((("up", 1), ("attn", 1), ("up", 0)), (("attn", 0),)):
        cut = jnp.stack([sums[key][:PIECE] for key in keys])
        parts = [cut[:, s * rows : (s + 1) * rows] for s in range(4)]
        whole = jnp.concatenate(regroup(parts, bits[3:]), 2)
        for i, key in enumerate(keys):
            shares[key] = whole[i]
    outs = (
        jnp.stack([shares["attn", l][:, : 3 * D].reshape(-1) for l in range(LAYERS)]),
        jnp.stack([shares["attn", l][:, 3 * D :].reshape(-1) for l in range(LAYERS)]),
        jnp.stack([shares["up", l].reshape(-1) for l in range(LAYERS)]),
        jnp.stack([sums["down", l].reshape(-1) for l in range(LAYERS)]),
    )
    return (output, grad, *outs, mine[: gains.shape[0]], mine[gains.shape[0] :])


def solution(mesh):
    both = P(AXES)
    flat = P(None, AXES)
    rows = P(AXES, None)
    return jax.shard_map(
        body,
        mesh=mesh,
        in_specs=(rows, both, flat, flat, flat, flat, both, both, rows),
        out_specs=(rows, rows, flat, flat, flat, flat, both, both),
        check_vma=False,
    )
```

```python
import functools

import jax
import jax.numpy as jnp
import numpy as np
from jax import lax
from jax.experimental import pallas as pl
from jax.experimental.pallas import tpu as pltpu
from jax.sharding import PartitionSpec as P

D = 640
HEADS = 20
HEAD_DIM = 32
FF = 2560
LAYERS = 2
EPSILON = 1e-05
MASKED = -1e9
LANES = 128
GROUPS = D // LANES
PER_GROUP = LANES // HEAD_DIM
BLOCKS = FF // D
PIECE = 80
VECS = 16
ROWS = 256
AXES = ("wide", "narrow")
VMEM_LIMIT = 56 * 1024 * 1024
f32, bf16 = jnp.float32, jnp.bfloat16

GAIN_A, GAIN_F, SHIFT_A, BIAS_QKV, BIAS_OUT, SHIFT_F, BIAS_UP, BIAS_DOWN = 0, 1, 2, 3, 6, 7, 8, 12


def rotary_tables(length):
    half = HEAD_DIM // 2
    inverse = 1.0 / 10000.0 ** (np.arange(half) * (2.0 / HEAD_DIM))
    angles = np.arange(length)[:, None] * inverse[None, :]
    cos = np.tile(np.cos(angles), (1, 2 * PER_GROUP))
    sine = np.sin(angles)
    none = np.zeros_like(sine)
    ahead = np.tile(np.concatenate([-sine, none], 1), (1, PER_GROUP))
    behind = np.tile(np.concatenate([none, sine], 1), (1, PER_GROUP))
    return np.stack([cos, ahead, behind]).astype(np.float32)


def dot(left, right):
    return jnp.dot(left, right, preferred_element_type=f32)


def dot_nt(left, right):
    return lax.dot_general(left, right, (((1,), (1,)), ((), ())), preferred_element_type=f32)


def dot_tn(left, right):
    return lax.dot_general(left, right, (((0,), (0,)), ((), ())), preferred_element_type=f32)


def rolled(value, table, rows, sign):
    half = HEAD_DIM // 2
    turned = pltpu.roll(value, LANES - half, 1) * table[1, rows, :] + pltpu.roll(value, half, 1) * table[2, rows, :]
    return value * table[0, rows, :] + (turned if sign > 0 else -turned)


def unit_of(value):
    centered = value - jnp.mean(value, -1, keepdims=True)
    inverse = lax.rsqrt(jnp.mean(centered * centered, -1, keepdims=True) + EPSILON)
    return centered * inverse, inverse


def norm_back(grad, unit, inverse, gain):
    scaled = grad * gain
    return inverse * (scaled - jnp.mean(scaled, -1, keepdims=True) - unit * jnp.mean(scaled * unit, -1, keepdims=True))


def column_sum(value):
    return jnp.sum(value, 0, keepdims=True)


def gelu_parts(value):
    scaled = jnp.abs(value) * 0.7071067811865476
    t = 1.0 / (1.0 + 0.3275911 * scaled)
    bell = jnp.exp(-scaled * scaled)
    series = t * (0.127414796 + t * (-0.142248368 + t * (0.7107068705 + t * (-0.7265760135 + t * 0.5307027145))))
    tail = series * bell
    return jnp.where(value >= 0.0, 1.0 - tail, tail), bell * 0.3989422804014327


def three_parts(value):
    first = value.astype(bf16)
    rest = value - first.astype(f32)
    second = rest.astype(bf16)
    third = (rest - second.astype(f32)).astype(bf16)
    return first, second, third


def spread(value):
    lane = lax.broadcasted_iota(jnp.int32, value.shape, 1) % HEAD_DIM
    first, second, third = three_parts(value)
    tail = jnp.where(lane == 3, 1.0, 0.0)
    out = jnp.where(lane == 2, third.astype(f32), tail)
    out = jnp.where(lane == 1, second.astype(f32), out)
    return jnp.where(lane == 0, first.astype(f32), out).astype(bf16)


def row_loop(length, step, body):
    def run(i, carry):
        body(pl.ds(pl.multiple_of(i * step, step), step), i)
        return carry

    lax.fori_loop(0, length // step, run, 0)


def blocks_of(coords, first):
    for kb in range(2):
        for kn in range(2):
            for ka in range(2):
                for kz in range(4):
                    kx, ky = (ka, kb) if first == "x" else (kb, ka)
                    yield 2 * kb + kn, 4 * ka + kz, coords[0] ^ kz, coords[1] ^ ky, coords[2] ^ kx, coords[3] ^ kn


def quarter_copies(coords, first, pieces, whole, sems):
    copies = []
    for piece, block, z, y, x, n in blocks_of(coords, first):
        rows = pl.ds(pl.multiple_of((2 * z + y) * PIECE, PIECE), PIECE)
        columns = pl.ds(pl.multiple_of((2 * x + n) * D, D), D)
        copies.append(
            pltpu.make_async_copy(
                pieces[piece].at[block, pl.ds(0, PIECE)], whole.at[rows, columns], sems.at[8 * piece + block]
            )
        )
    return copies


def row_copies(coords, first, pieces, whole, sems):
    copies = []
    for piece, block, z, y, x, n in blocks_of(coords, first):
        rows = pl.ds(pl.multiple_of((8 * z + 4 * y + 2 * x + n) * PIECE, PIECE), PIECE)
        copies.append(pltpu.make_async_copy(pieces[piece].at[block], whole.at[rows], sems.at[8 * piece + block]))
    return copies


def head_masks():
    lane = lax.broadcasted_iota(jnp.int32, (1, LANES), 1)
    return [(lane // HEAD_DIM == head).astype(f32).astype(bf16) for head in range(PER_GROUP)]


def key_tail(length, live, head):
    lane = lax.broadcasted_iota(jnp.int32, (length, LANES), 1)
    row = lax.broadcasted_iota(jnp.int32, (length, LANES), 0)
    base = head * HEAD_DIM
    ones = jnp.where((lane >= base) & (lane < base + 3), 1.0, 0.0)
    return jnp.where((lane == base + 3) & (row >= live), MASKED, ones).astype(bf16)


def attn_fwd_kernel(first, coords, x_ref, vec_ref, table_ref, *refs):
    pieces, refs = refs[:4], refs[4:]
    at_ref, qkv_ref, o_ref, ot_ref, lse_ref, m_ref, b_ref, bt_ref, a_ref, w_ref, key_ref, val_ref, sems = refs
    length = x_ref.shape[0]
    copies = quarter_copies(coords, first, pieces, w_ref, sems)
    for copy in copies:
        copy.start()

    def norm(rows, _):
        unit, _ = unit_of(x_ref[rows, :].astype(f32))
        a_ref[rows, :] = (unit * vec_ref[GAIN_A : GAIN_A + 1, :] + vec_ref[SHIFT_A : SHIFT_A + 1, :]).astype(bf16)

    row_loop(length, 128, norm)
    for copy in copies:
        copy.wait()

    def project(rows, _):
        normed = a_ref[rows, :]
        for part in range(3):
            out = dot(normed, w_ref[:, part * D : (part + 1) * D]) + vec_ref[BIAS_QKV + part : BIAS_QKV + part + 1, :]
            if part == 0:
                out = out * HEAD_DIM**-0.5
            for group in range(GROUPS):
                piece = out[:, group * LANES : (group + 1) * LANES]
                if part < 2:
                    piece = rolled(piece, table_ref, rows, 1)
                qkv_ref[rows, part * D + group * LANES : part * D + (group + 1) * LANES] = piece.astype(bf16)

    row_loop(length, ROWS, project)
    live = coords[4]
    masks = head_masks()
    for head in range(PER_GROUP):
        key_ref[head, :, LANES:] = key_tail(length, live, head)
        val_ref[head, :, LANES:] = jnp.broadcast_to(masks[head], (length, LANES))

    def group_step(group, carry):
        at = [pl.ds(pl.multiple_of(part * D + group * LANES, LANES), LANES) for part in range(3)]
        for head in range(PER_GROUP):
            key_ref[head, :, :LANES] = qkv_ref[:, at[1]] * masks[head]
            val_ref[head, :, :LANES] = qkv_ref[:, at[2]] * masks[head]

        def rows_step(rows, _):
            lane = lax.broadcasted_iota(jnp.int32, (ROWS, LANES), 1)
            tail = jnp.where(lane % HEAD_DIM == 3, 1.0, 0.0).astype(bf16)
            query = jnp.concatenate([qkv_ref[rows, at[0]], tail], 1)
            total = jnp.zeros((ROWS, 2 * LANES), f32)
            tops = jnp.zeros((ROWS, LANES), f32)
            for head in range(PER_GROUP):
                scores = dot_nt(query, key_ref[head])
                top = jnp.max(scores, -1, keepdims=True)
                total = total + dot(jnp.exp(scores - top).astype(bf16), val_ref[head])
                tops = jnp.where(lane // HEAD_DIM == head, top, tops)
            o_ref[rows, at[0]] = (total[:, :LANES] / total[:, LANES:]).astype(bf16)
            lse_ref[rows, at[0]] = spread(-(tops + jnp.log(total[:, LANES:])))

        row_loop(length, ROWS, rows_step)
        return carry

    lax.fori_loop(0, GROUPS, group_step, 0)

    def after(rows, _):
        middle = x_ref[rows, :].astype(f32) + (dot(o_ref[rows, :], w_ref[:, 3 * D :]) + vec_ref[BIAS_OUT : BIAS_OUT + 1, :])
        m_ref[rows, :] = middle
        unit, _ = unit_of(middle)
        b_ref[rows, :] = (unit * vec_ref[GAIN_F : GAIN_F + 1, :] + vec_ref[SHIFT_F : SHIFT_F + 1, :]).astype(bf16)

    row_loop(length, ROWS, after)
    at_ref[...] = a_ref[...].T
    ot_ref[...] = o_ref[...].T
    bt_ref[...] = b_ref[...].T


def ffn_fwd_kernel(first, last, coords, m_ref, b_ref, vec_ref, *refs):
    up_pieces, down_pieces, refs = refs[:4], refs[4:8], refs[8:]
    y_ref, zt_ref, slope_ref, z_ref, up_ref, down_ref, up_sems, down_sems = refs
    length = m_ref.shape[0]
    copies = quarter_copies(coords, first[0], up_pieces, up_ref, up_sems)
    copies_down = row_copies(coords, first[1], down_pieces, down_ref, down_sems)
    for copy in copies + copies_down:
        copy.start()
    for copy in copies + copies_down:
        copy.wait()

    def step(rows, i):
        normed = b_ref[rows, :]
        for block in range(BLOCKS):
            columns = slice(block * D, (block + 1) * D)
            pre = dot(normed, up_ref[:, columns]) + vec_ref[BIAS_UP + block : BIAS_UP + block + 1, :]
            cdf, bell = gelu_parts(pre)
            z_ref[rows, columns] = (pre * cdf).astype(bf16)
            slope_ref[rows, columns] = (cdf + pre * bell).astype(bf16)
        out = m_ref[rows, :] + (dot(z_ref[rows, :], down_ref[...]) + vec_ref[BIAS_DOWN : BIAS_DOWN + 1, :])
        if last:
            row = lax.broadcasted_iota(jnp.int32, (ROWS, 1), 0) + i * ROWS
            out = jnp.where(row < coords[4], out, 0.0)
        y_ref[rows, :] = out.astype(y_ref.dtype)

    row_loop(length, ROWS, step)
    for block in range(BLOCKS):
        columns = slice(block * D, (block + 1) * D)
        zt_ref[columns, :] = z_ref[:, columns].T


def ffn_bwd_kernel(first, top, coords, g_ref, slope_ref, m_ref, vec_ref, *refs):
    up_pieces, down_pieces, refs = refs[:4], refs[4:8], refs[8:]
    gb_ref, gu_ref, gm_ref, gmb_ref, sums_ref, up_ref, down_ref, up_sems, down_sems = refs
    length = m_ref.shape[0]
    copies = quarter_copies(coords, first[0], up_pieces, up_ref, up_sems)
    copies_down = row_copies(coords, first[1], down_pieces, down_ref, down_sems)
    for copy in copies_down + copies:
        copy.start()
    for copy in copies_down + copies:
        copy.wait()
    sums_ref[...] = jnp.zeros_like(sums_ref)

    def add(row, value):
        sums_ref[row : row + 1, :] += column_sum(value)

    def step(rows, i):
        grad = g_ref[rows, :].astype(f32)
        if top:
            row = lax.broadcasted_iota(jnp.int32, (ROWS, 1), 0) + i * ROWS
            grad = jnp.where(row < coords[4], grad, 0.0)
        low = grad.astype(bf16)
        gb_ref[rows, :] = low
        add(BIAS_DOWN, low.astype(f32))
        for block in range(BLOCKS):
            columns = slice(block * D, (block + 1) * D)
            back = dot_nt(low, down_ref[columns, :]) * slope_ref[rows, columns].astype(f32)
            part = back.astype(bf16)
            gu_ref[rows, columns] = part
            add(BIAS_UP + block, part.astype(f32))
        normed_grad = dot_nt(gu_ref[rows, :], up_ref[...])
        unit, inverse = unit_of(m_ref[rows, :])
        add(GAIN_F, normed_grad * unit)
        add(SHIFT_F, normed_grad)
        middle = grad + norm_back(normed_grad, unit, inverse, vec_ref[GAIN_F : GAIN_F + 1, :])
        gm_ref[rows, :] = middle
        low = middle.astype(bf16)
        gmb_ref[rows, :] = low
        add(BIAS_OUT, low.astype(f32))

    row_loop(length, ROWS, step)


def attn_bwd_kernel(first, coords, gmb_ref, qkv_ref, o_ref, lse_ref, table_ref, *refs):
    pieces, refs = refs[:4], refs[4:]
    gpm_ref, w_ref, go_ref, key_ref, val_ref, q_ref, g_ref, dq_ref, sems = refs
    length = gmb_ref.shape[0]
    copies = quarter_copies(coords, first, pieces, w_ref, sems)
    for copy in copies:
        copy.start()
    for copy in copies:
        copy.wait()

    def back(rows, _):
        low = gmb_ref[rows, :]
        gpm_ref[rows, 3 * D :] = low
        go_ref[rows, :] = dot_nt(low, w_ref[:, 3 * D :]).astype(bf16)

    row_loop(length, ROWS, back)
    live = coords[4]
    masks = head_masks()
    head_of = lax.broadcasted_iota(jnp.int32, (LANES, LANES), 0) // HEAD_DIM
    same = (head_of == lax.broadcasted_iota(jnp.int32, (LANES, LANES), 1) // HEAD_DIM).astype(f32).astype(bf16)
    for head in range(PER_GROUP):
        key_ref[head, :, LANES:] = key_tail(length, live, head)
        val_ref[head, :, LANES:] = key_tail(length, length, head)

    def group_step(group, carry):
        at = [pl.ds(pl.multiple_of(part * D + group * LANES, LANES), LANES) for part in range(3)]
        grad = go_ref[:, at[0]]
        query = qkv_ref[:, at[0]]
        product = grad.astype(f32) * o_ref[:, at[0]].astype(f32)
        high = product.astype(bf16)
        rest = (product - high.astype(f32)).astype(bf16)
        deltas = dot(high, same) + dot(rest, same)
        for head in range(PER_GROUP):
            key_ref[head, :, :LANES] = qkv_ref[:, at[1]] * masks[head]
            val_ref[head, :, :LANES] = qkv_ref[:, at[2]] * masks[head]
            q_ref[head] = query * masks[head]
            g_ref[head] = grad * masks[head]
        query_wide = jnp.concatenate([query, lse_ref[:, at[0]]], 1)
        grad_wide = jnp.concatenate([grad, spread(-deltas)], 1)
        dq_ref[...] = jnp.zeros_like(dq_ref)

        def rows_step(rows, _):
            dk = jnp.zeros((ROWS, LANES), f32)
            dv = jnp.zeros((ROWS, LANES), f32)
            for head in range(PER_GROUP):
                key = key_ref[head, rows, :]
                probs = jnp.exp(dot_nt(key, query_wide))
                scores = (probs * dot_nt(val_ref[head, rows, :], grad_wide)).astype(bf16)
                dv = dv + dot(probs.astype(bf16), g_ref[head])
                dk = dk + dot(scores, q_ref[head])
                dq_ref[...] += dot_tn(scores, key[:, :LANES])
            dk = rolled(dk.astype(bf16).astype(f32), table_ref, rows, -1)
            gpm_ref[rows, at[1]] = dk.astype(bf16)
            gpm_ref[rows, at[2]] = dv.astype(bf16)

        row_loop(length, ROWS, rows_step)

        def last_step(rows, _):
            dq = rolled(dq_ref[rows, :].astype(bf16).astype(f32), table_ref, rows, -1) * HEAD_DIM**-0.5
            gpm_ref[rows, at[0]] = dq.astype(bf16)

        row_loop(length, ROWS, last_step)
        return carry

    lax.fori_loop(0, GROUPS, group_step, 0)


def attn_after_kernel(first, coords, gpm_ref, gm_ref, x_ref, vec_ref, *refs):
    pieces, refs = refs[:4], refs[4:]
    gx_ref, sums_ref, w_ref, sems = refs
    length = x_ref.shape[0]
    copies = quarter_copies(coords, first, pieces, w_ref, sems)
    for copy in copies:
        copy.start()
    for copy in copies:
        copy.wait()
    sums_ref[...] = jnp.zeros_like(sums_ref)

    def add(row, value):
        sums_ref[row : row + 1, :] += column_sum(value)

    def after(rows, _):
        for part in range(3):
            add(BIAS_QKV + part, gpm_ref[rows, part * D : (part + 1) * D].astype(f32))
        normed_grad = dot_nt(gpm_ref[rows, : 3 * D], w_ref[:, : 3 * D])
        unit, inverse = unit_of(x_ref[rows, :].astype(f32))
        add(GAIN_A, normed_grad * unit)
        add(SHIFT_A, normed_grad)
        out = gm_ref[rows, :] + norm_back(normed_grad, unit, inverse, vec_ref[GAIN_A : GAIN_A + 1, :])
        gx_ref[rows, :] = out.astype(gx_ref.dtype)

    row_loop(length, ROWS, after)


def grads_kernel(plan, phase, coords, *refs):
    items, inputs, halves = plan
    offset = halves[0]
    ins, rest = refs[:inputs], refs[inputs:]
    left_ref, rest = rest[-1], rest[:-1]
    for kind, lefts, right, cuts in items:
        if kind == "rest":
            block = ins[right]

            def value_of(kx, ky, kz, block=block):
                return block[phase, kx, ky, kz]

            put(rest, phase, offset, value_of, cuts)
            continue
        if kind == "down":
            for kx in range(2):
                for ky in range(2):
                    for kz in range(4):
                        z, y, x, n = coords[0] ^ kz, coords[1] ^ ky, coords[2] ^ kx, coords[3] ^ phase
                        start = pl.multiple_of((8 * z + 4 * y + 2 * x + n) * PIECE, PIECE)
                        to = (8 * kx + 4 * ky + kz) * PIECE
                        left_ref[to : to + PIECE, :] = ins[lefts[0]][pl.ds(start, PIECE), :]
            for kx in range(2):
                whole = dot(left_ref[kx * D : (kx + 1) * D, :], ins[right][...]).astype(bf16)
                put(rest, phase, offset, functools.partial(block_of, whole), cuts, kx)
            continue
        for i, left in enumerate(lefts):
            for ky in range(2):
                for kz in range(4):
                    start = pl.multiple_of((2 * (coords[0] ^ kz) + (coords[1] ^ ky)) * PIECE, PIECE)
                    to = i * D + (4 * ky + kz) * PIECE
                    left_ref[to : to + PIECE, :] = ins[left][pl.ds(start, PIECE), :]
        for kx in range(2):
            quarter = 2 * (coords[2] ^ kx) + (coords[3] ^ phase)
            columns = pl.ds(pl.multiple_of(quarter * D, D), D)
            if len(lefts) > 1:
                left = left_ref[pl.ds(pl.multiple_of(quarter // 3 * D, D), D), :]
            else:
                left = left_ref[:D, :]
            whole = dot(left, ins[right][:, columns]).astype(bf16)
            put(rest, phase, offset, functools.partial(block_of, whole), cuts, kx)


def block_of(whole, kx, ky, kz):
    start = (4 * ky + kz) * PIECE
    return whole[start : start + PIECE]


def put(outs, phase, offset, value_of, cuts, only=None):
    for kx in range(2) if only is None else (only,):
        for ky in range(2):
            for kz in range(4):
                value = value_of(kx, ky, kz)
                for half, to, start, rows in cuts:
                    ka, kb = (ky, kx) if half else (kx, ky)
                    begin = to + (offset if phase and half else 0)
                    part, at = value[start : start + rows], slice(begin, begin + rows)
                    if phase:
                        outs[0][ka, kb, kz, at] = part
                    elif ka:
                        outs[3 * half][kb, kz, at] = part
                    elif kb:
                        outs[3 * half + 1][kz, at] = part
                    else:
                        outs[3 * half + 2][kz, at] = part


def call(kernel, ins, outs, scratch, name, flops, exps=0):
    moved = sum(a.size * a.dtype.itemsize for a, _ in ins) + sum(int(np.prod(s)) * jnp.dtype(t).itemsize for s, t in outs)
    return pl.pallas_call(
        kernel,
        out_shape=[jax.ShapeDtypeStruct(s, t) for s, t in outs],
        in_specs=[pl.BlockSpec(memory_space=space) for _, space in ins],
        out_specs=[pl.BlockSpec(memory_space=pltpu.VMEM)] * len(outs),
        scratch_shapes=scratch,
        compiler_params=pltpu.CompilerParams(vmem_limit_bytes=VMEM_LIMIT),
        cost_estimate=pl.CostEstimate(flops=int(flops), bytes_accessed=int(moved), transcendentals=int(exps)),
        name=name,
    )(*[a for a, _ in ins])


V, S, H = pltpu.VMEM, pltpu.SMEM, pl.ANY
SEMS = pltpu.SemaphoreType.DMA


def attn_fwd(coords, x, vec, table, weight):
    pieces, first = weight
    n = x.shape[0]
    ins = [(coords, S), (x, V), (vec, V), (table, V)] + [(p, H) for p in pieces]
    outs = [((D, n), bf16), ((n, 3 * D), bf16), ((n, D), bf16), ((D, n), bf16), ((n, D), bf16)]
    outs += [((n, D), f32), ((n, D), bf16), ((D, n), bf16)]
    wide = V((PER_GROUP, n, 2 * LANES), bf16)
    scratch = [V((n, D), bf16), V((D, FF), bf16), wide, wide, SEMS((32,))]
    kernel = functools.partial(attn_fwd_kernel, first)
    out = call(kernel, ins, outs, scratch, "attn_fwd", 2 * n * D * FF + 4 * n * n * D, HEADS * n * n)
    return dict(zip(("at", "qkv", "o", "ot", "lse", "m", "b", "bt"), out, strict=True)) | {"x": x}


def ffn_fwd(coords, kept, vec, up, down, last):
    m, b = kept["m"], kept["b"]
    n = m.shape[0]
    ins = [(coords, S), (m, V), (b, V), (vec, V)] + [(p, H) for p in up[0] + down[0]]
    outs = [((n, D), bf16 if last else f32), ((FF, n), bf16), ((n, FF), bf16)]
    scratch = [V((n, FF), bf16), V((D, FF), bf16), V((FF, D), bf16), SEMS((32,)), SEMS((32,))]
    kernel = functools.partial(ffn_fwd_kernel, (up[1], down[1]), last)
    y, zt, slope = call(kernel, ins, outs, scratch, "ffn_fwd", 4 * n * D * FF, 2 * n * FF)
    return y, {"zt": zt, "slope": slope}


def ffn_bwd(coords, g, kept, vec, up, down, top):
    slope, m = kept["slope"], kept["m"]
    n = m.shape[0]
    ins = [(coords, S), (g, V), (slope, V), (m, V), (vec, V)] + [(p, H) for p in up[0] + down[0]]
    outs = [((n, D), bf16), ((n, FF), bf16), ((n, D), f32), ((n, D), bf16), ((VECS, D), f32)]
    scratch = [V((D, FF), bf16), V((FF, D), bf16), SEMS((32,)), SEMS((32,))]
    kernel = functools.partial(ffn_bwd_kernel, (up[1], down[1]), top)
    out = call(kernel, ins, outs, scratch, "ffn_bwd", 4 * n * D * FF, 0)
    return dict(zip(("gb", "gu", "gm", "gmb", "sums"), out, strict=True))


def attn_bwd(coords, gmb, kept, table, weight):
    pieces, first = weight
    n = gmb.shape[0]
    ins = [(coords, S)] + [(a, V) for a in (gmb, kept["qkv"], kept["o"], kept["lse"], table)] + [(p, H) for p in pieces]
    wide, thin = V((PER_GROUP, n, 2 * LANES), bf16), V((PER_GROUP, n, LANES), bf16)
    scratch = [V((D, FF), bf16), V((n, D), bf16), wide, wide, thin, thin, V((n, LANES), f32), SEMS((32,))]
    kernel = functools.partial(attn_bwd_kernel, first)
    return call(kernel, ins, [((n, FF), bf16)], scratch, "attn_bwd", 2 * n * D * D + 10 * n * n * D, HEADS * n * n)[0]


def attn_after(coords, back, kept, vec, weight, last):
    gpm, gm, x = back["gpm"], back["gm"], kept["x"]
    pieces, first = weight
    n = x.shape[0]
    ins = [(coords, S)] + [(a, V) for a in (gpm, gm, x, vec)] + [(p, H) for p in pieces]
    outs = [((n, D), bf16 if last else f32), ((VECS, D), f32)]
    kernel = functools.partial(attn_after_kernel, first)
    return call(kernel, ins, outs, [V((D, FF), bf16), SEMS((32,))], "attn_after", 6 * n * D * D, 0)


def grads(coords, items, halves, phase):
    arrays, plan, flops = [], [], 0
    for kind, lefts, right, cuts in items:
        index = list(range(len(arrays), len(arrays) + len(lefts)))
        arrays += [*lefts, right]
        plan.append((kind, index, index[-1] + 1 if lefts else len(arrays) - 1, cuts))
        if lefts:
            flops += right.shape[0] * D * FF
    if phase:
        outs = [((2, 2, 4, sum(halves), D), bf16)]
    else:
        outs = [((*lead, rows, D), bf16) for rows in halves for lead in ((2, 4), (4,), (4,))]
    n = arrays[0].shape[1]
    kernel = functools.partial(grads_kernel, (plan, len(arrays), halves), phase)
    ins = [(coords, S)] + [(a, V) for a in arrays]
    return call(kernel, ins, outs, [V((2 * D, n), bf16)], "grads", flops, 0)


def swap(axis_name, bit):
    size = lax.axis_size(axis_name)
    pairs = [(i, i ^ bit) for i in range(size)]
    return lambda value: lax.ppermute(value, axis_name, pairs)


def mate(value):
    return swap("narrow", 1)(value)


def along(axis, value):
    return swap("wide", {"x": 1, "y": 2, "z0": 4, "z1": 8}[axis])(value)


def other(axis):
    return "x" if axis == "y" else "y"


def together(*values):
    return lax.optimization_barrier(values)


def relative(values, bits):
    for place_of, bit in enumerate(reversed(bits)):
        step = 1 << place_of
        values = [jnp.where(bit > 0, values[i ^ step], values[i]) for i in range(len(values))]
    return values


def add(*terms):
    return functools.reduce(lambda p, q: p + q, [t.astype(f32) for t in terms])


def regroup(parts, bits):
    mine = relative(parts, bits)
    return relative([mine[0]] + [swap(AXES, k)(mine[k]) for k in (1, 2, 3)], bits)


def vector_tables(gains, biases):
    gains = gains.astype(f32).reshape(LAYERS, 2, D)
    biases = biases.astype(f32).reshape(LAYERS, 11, D)
    return jnp.concatenate([gains, biases, jnp.zeros((LAYERS, VECS - 13, D), f32)], 1)


FIRST = {("attn", 0): "y", ("down", 0): "x", ("up", 0): "y", ("attn", 1): "x", ("up", 1): "y", ("down", 1): "x"}
LOTS = (
    ((80, 80), {("down", 1): ((0, 0, 0, 80),), ("up", 1): ((1, 0, 0, 80),)}),
    (
        (128, 112),
        {("attn", 1): ((0, 0, 0, 80),), ("down", 0): ((1, 0, 0, 80),), ("up", 0): ((0, 80, 0, 48), (1, 80, 48, 32))},
    ),
    ((48, 48), {("attn", 0): ((0, 0, 0, 48), (1, 0, 48, 32)), ("rest", 0): ((1, 32, 0, 16),)}),
)


def whole_pieces(matrix, by_rows, first):
    if by_rows:
        cut = jnp.transpose(matrix.reshape(4, 2, 2, 2, PIECE, D), (3, 2, 1, 0, 4, 5))
    else:
        cut = jnp.transpose(matrix.reshape(4, 2, PIECE, 2, 2, D), (4, 3, 1, 0, 2, 5))
    if first == "x":
        cut = jnp.swapaxes(cut, 1, 2)
    return [cut[kn, kb].reshape(8, PIECE, D) for kb in range(2) for kn in range(2)]


def whole_block(kept, core, halves, cuts):
    parts = {}
    for half in range(2):
        a, b, k = kept[3 * half : 3 * half + 3]
        rows = slice(halves[0], None) if half else slice(0, halves[0])
        cut = jnp.stack([jnp.stack([jnp.stack([k, b]), a]), core[:, :, :, rows]])
        parts[half] = jnp.swapaxes(cut, 1, 2) if half else cut
    return jnp.concatenate([parts[half][..., to : to + rows, :] for half, to, _, rows in cuts], -2)


def fetch_plain(w_qkv, w_out, w_up, w_down, gains, biases):
    def whole(value, rows):
        return lax.all_gather(value, AXES, axis=0, tiled=True).reshape(rows, -1)

    weights = {}
    for l in range(LAYERS):
        attn = jnp.concatenate([whole(w_qkv[l], D), whole(w_out[l], D)], 1)
        for name, matrix in (("attn", attn), ("up", whole(w_up[l], D)), ("down", whole(w_down[l], FF))):
            first = FIRST[name, l]
            weights[name, l] = (whole_pieces(matrix, name == "down", first), first)
    return weights, vector_tables(whole(gains, 1)[0], whole(biases, 1)[0])


class Lot:
    def __init__(self, halves):
        self.halves = halves

    def cut(self, core, half):
        return core[..., self.halves[0] :, :] if half else core[..., : self.halves[0], :]

    def first(self, core, kept):
        self.kept = kept
        self.core = [self.cut(core, half) for half in range(2)]
        return [add(kept[3 * half], self.core[half][1]).astype(bf16) for half in range(2)]

    def send_first(self, values):
        return along("x", values[0]), along("y", values[1])

    def second(self, got):
        self.got = got
        return [add(self.kept[3 * h + 1], self.core[h][0, 1], got[h][1]).astype(bf16) for h in range(2)]

    def send_second(self, values):
        return along("y", values[0]), along("x", values[1])

    def third(self, got):
        total = [add(self.kept[3 * h + 2], self.core[h][0, 0], self.got[h][0], got[h]) for h in range(2)]
        self.total = jnp.concatenate([t[:2] for t in total], 1)
        return jnp.concatenate([t[2:].astype(bf16) for t in total], 1)

    def fourth(self, got):
        total = add(self.total, got)
        self.total = total[0]
        return total[1].astype(bf16)

    def last(self, got):
        return add(self.total, got)


def stage(*groups):
    flat, tree = jax.tree.flatten(groups)
    return jax.tree.unflatten(tree, lax.optimization_barrier(flat))


def device_bits():
    wide = lax.axis_index("wide")
    return [(wide >> 3) & 1, (wide >> 2) & 1, (wide >> 1) & 1, wide & 1, lax.axis_index("narrow")]


def coordinates(values):
    return jnp.stack([jnp.asarray(v, jnp.int32) for v in values])


def layer_grads(sums):
    both = jnp.stack(sums)
    return both[:, :2].reshape(-1), both[:, 2:13].reshape(-1)


def gradient_blocks(coords, lot, kept, back, phase):
    items = []
    for (name, l), cuts in LOTS[lot][1].items():
        if name == "attn":
            items.append(("attn", [kept[l]["at"], kept[l]["ot"]], back[l]["gpm"], cuts))
        elif name == "up":
            items.append(("up", [kept[l]["bt"]], back[l]["gu"], cuts))
        elif name == "down":
            items.append(("down", [kept[l]["zt"]], back[l]["gb"], cuts))
        elif "rest" in back[l]:
            items.append(("rest", [], back[l]["rest"], cuts))
    halves = LOTS[lot][0]
    outs = grads(coords, items, halves if "rest" in back[0] or lot < 2 else (48, 32), phase)
    return outs[0] if phase else outs


def shares_of(parts, bits):
    rows = D // 32
    cut = jnp.stack(parts)
    whole = jnp.concatenate(regroup([cut[:, s * rows : (s + 1) * rows] for s in range(4)], bits[3:]), 2)
    return [whole[i] for i in range(len(parts))]


def body(tokens, lengths, w_qkv, w_out, w_up, w_down, gains, biases, cotangent):
    args = (tokens, lengths, w_qkv, w_out, w_up, w_down, gains, biases, cotangent)
    if lax.axis_size("wide") == 16 and lax.axis_size("narrow") == 2:
        return staged(*args)
    return plain(*args)


def plain(tokens, lengths, w_qkv, w_out, w_up, w_down, gains, biases, cotangent):
    length = tokens.shape[0] // lengths.shape[0]
    coords = coordinates([0, 0, 0, 0, lengths[0]])
    table = jnp.asarray(rotary_tables(length))
    weights, vectors = fetch_plain(w_qkv, w_out, w_up, w_down, gains, biases)
    kept, back, x = [], [{}, {}], tokens
    for l in range(LAYERS):
        held = attn_fwd(coords, x, vectors[l], table, weights["attn", l])
        x, more = ffn_fwd(coords, held, vectors[l], weights["up", l], weights["down", l], l == LAYERS - 1)
        kept.append(held | more)
    output, grad, sums = x, cotangent, [None] * LAYERS
    for l in reversed(range(LAYERS)):
        last = l == 0
        back[l] = ffn_bwd(coords, grad, kept[l], vectors[l], weights["up", l], weights["down", l], not last)
        back[l]["gpm"] = attn_bwd(coords, back[l]["gmb"], kept[l], table, weights["attn", l])
        grad, more = attn_after(coords, back[l], kept[l], vectors[l], weights["attn", l], last)
        sums[l] = back[l]["sums"] + more
    matrices = {}
    for lot, (halves, cuts) in enumerate(LOTS):
        core, rest = [gradient_blocks(coords, lot, kept, back, phase) for phase in (1, 0)]
        for key, where in cuts.items():
            if key[0] != "rest":
                cut = whole_block(rest, core, halves, where)
                order = (3, 2, 1, 0, 4, 5) if key[0] == "down" else (3, 2, 4, 1, 0, 5)
                matrices[key] = jnp.transpose(cut, order).reshape((FF, D) if key[0] == "down" else (D, FF)).astype(f32)
    outs = []
    for name, begin, end in (("attn", 0, 3 * D), ("attn", 3 * D, FF), ("up", 0, FF), ("down", 0, D)):
        cut = jnp.stack([matrices[name, l][:, begin:end].reshape(-1) for l in range(LAYERS)])
        outs.append(lax.psum_scatter(cut, AXES, scatter_dimension=1, tiled=True))
    outs += [lax.psum_scatter(v, AXES, scatter_dimension=0, tiled=True) for v in layer_grads(sums)]
    return (output, grad, *outs)


def staged(tokens, lengths, w_qkv, w_out, w_up, w_down, gains, biases, cotangent):
    length = tokens.shape[0] // lengths.shape[0]
    bits = device_bits()
    coords = coordinates([lax.axis_index("wide") >> 2, *bits[2:], lengths[0]])
    table = jnp.asarray(rotary_tables(length))
    rows = D // 32
    kept, back = [{}, {}], [{}, {}]

    flat = []
    for l in range(LAYERS):
        flat.append(jnp.concatenate([w_qkv[l].reshape(rows, 3 * D), w_out[l].reshape(rows, D)], 1))
        flat.append(w_up[l].reshape(rows, FF))
    flat = jnp.stack(flat)
    down0, down1 = [w_down[l].reshape(PIECE, D) for l in range(LAYERS)]
    down_t = jnp.stack([down0, along("z0", down0)])
    down_u = along("z1", down_t)
    attn0, up0, attn1, up1 = jnp.concatenate(regroup([flat[:, :, s * D : (s + 1) * D] for s in range(4)], bits[3:]), 1)
    small = jnp.concatenate([gains, biases])
    width = small.shape[0]
    attn0 = jnp.concatenate([attn0, jnp.zeros((16, D), bf16).at[0, :width].set(small)])
    attn_z = jnp.stack([attn0] + [swap("wide", k)(attn0) for k in (4, 8, 12)])
    down_z = jnp.concatenate([down_t, down_u])

    names = ((("attn", 0), ("down", 0)), (("up", 0), ("attn", 1)), (("up", 1), ("down", 1)))
    pairs = [None, jnp.stack([up0, attn1]), jnp.stack([up1, down1])]

    def hop(p, zs):
        return [along(FIRST[key], z) for key, z in zip(names[p], zs)]

    def jump(p, near):
        return [along(other(FIRST[key]), n) for key, n in zip(names[p], near)]

    def joined(left, right):
        return [jnp.concatenate([a, b]) for a, b in zip(left, right)]

    def z_blocks(near, far):
        return [jnp.concatenate([near[:, i], far[:, i]]) for i in range(2)]

    def mates(values):
        return [mate(v) for v in values]

    weights = {}

    def arrived(p, near, far, near_mate, far_mate):
        for i, key in enumerate(names[p]):
            weights[key] = ([near[i], near_mate[i], far[i], far_mate[i]], FIRST[key])

    zs0, pairs[1] = stage([attn_z, down_z], pairs[1])
    hop0, got1 = hop(0, zs0), along("z0", pairs[1])
    near0, t1 = stage(joined(zs0, hop0), jnp.stack([pairs[1], got1]))
    far0, mate0, u1 = jump(0, near0), mates(near0), along("z1", t1)
    far0, mate0, zs1, near0, pairs[2] = stage(far0, mate0, z_blocks(t1, u1), near0, pairs[2])
    far_mate0, hop1, got2 = mates(far0), hop(1, zs1), along("z0", pairs[2])
    far_mate0, near1, t2, near0, far0, mate0 = stage(
        far_mate0, joined(zs1, hop1), jnp.stack([pairs[2], got2]), near0, far0, mate0
    )
    arrived(0, near0, far0, mate0, far_mate0)
    cut = jnp.stack([p[:, PIECE, :width] for p in weights["attn", 0][0]]).reshape(2, 2, 2, 2, 2, width)
    cut = jnp.transpose(cut, (3, 4, 2, 0, 1, 5) if FIRST["attn", 0] == "y" else (3, 4, 0, 2, 1, 5))
    for axis, bit in enumerate(bits):
        cut = jnp.where(bit > 0, jnp.flip(cut, axis), cut)
    cut = cut.reshape(32, width)
    vectors = vector_tables(cut[:, : gains.shape[0]].reshape(-1), cut[:, gains.shape[0] :].reshape(-1))
    far1, mate1, u2 = jump(1, near1), mates(near1), along("z1", t2)
    kept[0] = attn_fwd(coords, tokens, vectors[0], table, weights["attn", 0])
    far1, mate1, zs2, near1, kept[0] = stage(far1, mate1, z_blocks(t2, u2), near1, kept[0])
    far_mate1, hop2 = mates(far1), hop(2, zs2)
    arrived(1, near1, far1, mate1, far_mate1)
    x, more = ffn_fwd(coords, kept[0], vectors[0], weights["up", 0], weights["down", 0], False)
    kept[0] |= more
    near2, x = stage(joined(zs2, hop2), x)
    far2, mate2 = jump(2, near2), mates(near2)
    kept[1] = attn_fwd(coords, x, vectors[1], table, weights["attn", 1])
    far2, mate2, kept[1] = stage(far2, mate2, kept[1])
    far_mate2 = mates(far2)
    arrived(2, near2, far2, mate2, far_mate2)
    output, more = ffn_fwd(coords, kept[1], vectors[1], weights["up", 1], weights["down", 1], True)
    kept[1] |= more

    lots = [Lot(halves) for halves, _ in LOTS]
    back[1] = ffn_bwd(coords, cotangent, kept[1], vectors[1], weights["up", 1], weights["down", 1], True)
    core = gradient_blocks(coords, 0, kept, back, 1)
    core, back[1]["gu"] = stage(core, back[1]["gu"])
    first = lots[0].first(mate(core), gradient_blocks(coords, 0, kept, back, 0))
    first, back[1] = stage(first, back[1])
    got = lots[0].send_first(first)
    gpm = attn_bwd(coords, back[1]["gmb"], kept[1], table, weights["attn", 1])
    got, back[1]["gpm"] = stage(got, gpm)
    second, back[1] = stage(lots[0].second(got), back[1])
    got = lots[0].send_second(second)
    grad, more = attn_after(coords, back[1], kept[1], vectors[1], weights["attn", 1], False)
    back[0] = ffn_bwd(coords, grad, kept[0], vectors[0], weights["up", 0], weights["down", 0], False)
    sums = [None, back[1]["sums"] + more]
    got, back[0] = stage(got, back[0])
    third, back[0] = stage(lots[0].third(got), back[0])
    got, core = stage(along("z1", third), gradient_blocks(coords, 1, kept, back, 1))
    fourth, core, back[1]["gpm"] = stage(lots[0].fourth(got), core, back[1]["gpm"])
    got, core = along("z0", fourth), mate(core)
    first = lots[1].first(core, gradient_blocks(coords, 1, kept, back, 0))
    first, back[0], done0 = stage(first, back[0], lots[0].last(got))
    got = lots[1].send_first(first)
    gpm = attn_bwd(coords, back[0]["gmb"], kept[0], table, weights["attn", 0])
    got, back[0]["gpm"] = stage(got, gpm)
    second, back[0] = stage(lots[1].second(got), back[0])
    got = lots[1].send_second(second)
    grad, more = attn_after(coords, back[0], kept[0], vectors[0], weights["attn", 0], True)
    sums[0] = back[0]["sums"] + more
    small = jnp.concatenate([v.reshape(32, -1) for v in layer_grads(sums)], 1).reshape(2, 2, 2, 2, 2, width)
    for axis, bit in enumerate(bits):
        small = jnp.where(bit > 0, jnp.flip(small, axis), small)
    small = jnp.transpose(small, (4, 3, 2, 0, 1, 5)).reshape(2, 2, 2, 4, 1, width)
    back[0]["rest"] = jnp.pad(small, ((0, 0),) * 4 + ((0, 15), (0, D - width))).astype(bf16)
    core = gradient_blocks(coords, 2, kept, back, 1)
    got, core, back[0]["gpm"] = stage(got, core, back[0]["gpm"])
    third, core = stage(lots[1].third(got), core)
    got, core = along("z1", third), mate(core)
    first = lots[2].first(core, gradient_blocks(coords, 2, kept, back, 0))
    got, first = stage(got, first)
    fourth, first = stage(lots[1].fourth(got), first)
    got, got2 = along("z0", fourth), lots[2].send_first(first)
    second, done1 = stage(lots[2].second(got2), lots[1].last(got))
    got2 = lots[2].send_second(second)
    up0 = jnp.concatenate([done1[80:128], done1[208:240]])
    up1, attn1, up0 = shares_of([done0[80:160], done1[:80], up0], bits)
    fourth = lots[2].fourth(along("z1", lots[2].third(got2)))
    done2 = lots[2].last(along("z0", fourth))
    (attn0,) = shares_of([done2[:80]], bits)
    mine = done2[80, :width]
    return (
        output,
        grad,
        jnp.stack([v[:, : 3 * D].reshape(-1) for v in (attn0, attn1)]),
        jnp.stack([v[:, 3 * D :].reshape(-1) for v in (attn0, attn1)]),
        jnp.stack([up0.reshape(-1), up1.reshape(-1)]),
        jnp.stack([done1[128:208].reshape(-1), done0[:80].reshape(-1)]),
        mine[: gains.shape[0]],
        mine[gains.shape[0] :],
    )


def solution(mesh):
    both, flat, rows = P(AXES), P(None, AXES), P(AXES, None)
    return jax.shard_map(
        body,
        mesh=mesh,
        in_specs=(rows, both, flat, flat, flat, flat, both, both, rows),
        out_specs=(rows, rows, flat, flat, flat, flat, both, both),
        check_vma=False,
    )
```

```python
import functools

import jax
import jax.numpy as jnp
import numpy as np
from jax import lax
from jax.experimental import pallas as pl
from jax.experimental.pallas import tpu as pltpu
from jax.sharding import PartitionSpec as P

D = 640
HEADS = 20
HEAD_DIM = 32
FF = 2560
LAYERS = 2
EPSILON = 1e-05
MASKED = -1e9
LANES = 128
GROUPS = D // LANES
PER_GROUP = LANES // HEAD_DIM
BLOCKS = FF // D
EARLY, LATE = (0, 3), (3, 2)
PIECE = 80
VECS = 16
AXES = ("wide", "narrow")
WHOLE, WHOLE_ROWS = (4, 2, PIECE, FF), (4, 2, 2, 2, PIECE, D)
SLACK = 8 * 1024 * 1024
f32, bf16 = jnp.float32, jnp.bfloat16

GAIN_A, GAIN_F, SHIFT_A, BIAS_QKV, BIAS_OUT, SHIFT_F, BIAS_UP, BIAS_DOWN = 0, 1, 2, 3, 6, 7, 8, 12


def rotary_tables(length):
    half = HEAD_DIM // 2
    inverse = 1.0 / 10000.0 ** (np.arange(half) * (2.0 / HEAD_DIM))
    angles = np.arange(length)[:, None] * inverse[None, :]
    cos, sine = np.cos(angles), np.sin(angles)
    none = np.zeros_like(sine)
    ahead = np.tile(np.concatenate([-sine, none], 1), (1, PER_GROUP))
    behind = np.tile(np.concatenate([none, sine], 1), (1, PER_GROUP))
    wide = np.stack([np.tile(cos, (1, 2 * PER_GROUP)), ahead, behind]).astype(np.float32)
    return jnp.asarray(wide), jnp.asarray(np.stack([cos.T, sine.T]).astype(np.float32))


def dot(left, right):
    return jnp.dot(left, right, preferred_element_type=f32)


def dot_nt(left, right):
    return lax.dot_general(left, right, (((1,), (1,)), ((), ())), preferred_element_type=f32)


def dot_tn(left, right):
    return lax.dot_general(left, right, (((0,), (0,)), ((), ())), preferred_element_type=f32)


def rotated(value, table):
    half = HEAD_DIM // 2
    return value * table[0] + pltpu.roll(value, LANES - half, 1) * table[1] + pltpu.roll(value, half, 1) * table[2]


def rotated_back(value, table):
    half = HEAD_DIM // 2
    first, second = value[:half], value[half:]
    return jnp.concatenate([first * table[0] + second * table[1], second * table[0] - first * table[1]], 0)


def unit_of(value):
    centered = value - jnp.mean(value, -1, keepdims=True)
    inverse = lax.rsqrt(jnp.mean(centered * centered, -1, keepdims=True) + EPSILON)
    return centered * inverse, inverse


def norm_back(grad, unit, inverse, gain):
    scaled = grad * gain
    return inverse * (scaled - jnp.mean(scaled, -1, keepdims=True) - unit * jnp.mean(scaled * unit, -1, keepdims=True))


def column_sum(value):
    return jnp.sum(value, 0, keepdims=True)


def gelu_parts(value):
    scaled = jnp.abs(value) * 0.7071067811865476
    t = 1.0 / (1.0 + 0.3275911 * scaled)
    bell = jnp.exp(-scaled * scaled)
    series = t * (0.127414796 + t * (-0.142248368 + t * (0.7107068705 + t * (-0.7265760135 + t * 0.5307027145))))
    tail = series * bell
    return jnp.where(value >= 0.0, 1.0 - tail, tail), bell * 0.3989422804014327


def row_loop(length, step, body):
    def run(i, carry):
        body(pl.ds(pl.multiple_of(i * step, step), step), i)
        return carry

    lax.fori_loop(0, length // step, run, 0)


def owner_of(coords, kn, kb, ka, k2, k1):
    n = coords[3] ^ kn
    z = coords[0] ^ (2 * k1 + k2 + n * (k2 - k1))
    return z, coords[1] ^ (kb + n * (ka - kb)), coords[2] ^ (ka + n * (kb - ka)), n


PLACES = [(ka, k2, k1) for ka in range(2) for k2 in range(2) for k1 in range(2)]


class Assembly:
    def __init__(self, coords, by_rows, pieces, offset, whole, sems):
        self.by_rows, self.whole, self.sems = by_rows, whole, sems
        self.any = pieces[0].at[0, :, pl.ds(offset, PIECE)]
        for kb in range(2):
            for kn in range(2):
                n = coords[3] ^ kn
                b = (coords[1] + n * (coords[2] - coords[1])) ^ kb
                for a in range(2):
                    target = self.target(a + n * (b - a), b + n * (a - b), n)
                    pltpu.make_async_copy(pieces[2 * kb + kn].at[a, :, pl.ds(offset, PIECE)], *target).start()

    def target(self, x, y, n):
        to = (y, x, n) if self.by_rows else (y, slice(None), pl.ds(pl.multiple_of((2 * x + n) * D, D), D))
        return self.whole.at[(slice(None), *to)], self.sems.at[4 * x + 2 * n + y]

    def wait(self, quarters=(0, 1, 2, 3)):
        for quarter in quarters:
            for y in range(2):
                pltpu.make_async_copy(self.any, *self.target(quarter // 2, y, quarter % 2)).wait()


def head_masks():
    lane = lax.broadcasted_iota(jnp.int32, (1, LANES), 1)
    return [(lane // HEAD_DIM == head).astype(f32).astype(bf16) for head in range(PER_GROUP)]


def masked_tail(length, live):
    row = lax.broadcasted_iota(jnp.int32, (length, LANES), 0)
    lane = lax.broadcasted_iota(jnp.int32, (length, LANES), 1)
    keys = jnp.where((lane == 0) & (row >= live), MASKED, 0.0).astype(bf16)
    row = lax.broadcasted_iota(jnp.int32, (LANES, length), 0)
    return keys, jnp.where(row == 0, 1.0, 0.0).astype(bf16)


def attn_fwd_kernel(plan, coords, x_ref, vec_ref, table_ref, *refs):
    count = len(plan)
    pieces, refs = refs[: 4 * count], refs[4 * count :]
    at_ref, qt_ref, kv_ref, ot_ref, lse_ref, m_ref, b_ref, bt_ref, *refs = refs
    wholes, refs = refs[:count], refs[count:]
    a_ref, q_ref, key_ref, query_ref, sems = refs
    length = x_ref.shape[0]
    jobs = [
        Assembly(coords, by_rows, pieces[4 * i : 4 * i + 4], offset, wholes[i], sems.at[i])
        for i, (offset, by_rows) in enumerate(plan)
    ]
    w_ref = wholes[0]

    def norm(rows, _):
        unit, _ = unit_of(x_ref[rows, :].astype(f32))
        a_ref[rows, :] = (unit * vec_ref[GAIN_A : GAIN_A + 1, :] + vec_ref[SHIFT_A : SHIFT_A + 1, :]).astype(bf16)

    row_loop(length, 128, norm)
    normed = a_ref[...]
    at_ref[...] = normed.T
    for part in range(3):
        jobs[0].wait([part])
        out = dot(normed, w_ref[:, :, :, part * D : (part + 1) * D].reshape(D, D)) + vec_ref[BIAS_QKV + part : BIAS_QKV + part + 1, :]
        if part == 0:
            out = out * HEAD_DIM**-0.5
        for group in range(GROUPS):
            lanes = slice(group * LANES, (group + 1) * LANES)
            piece = out[:, lanes]
            if part < 2:
                piece = rotated(piece, table_ref)
            if part == 0:
                qt_ref[lanes, :] = piece.astype(bf16).T
            else:
                kv_ref[:, (part - 1) * D + group * LANES : (part - 1) * D + (group + 1) * LANES] = piece.astype(bf16)
    masks = head_masks()
    tail, query_ref[LANES:, :] = masked_tail(length, coords[4])
    for head in range(PER_GROUP):
        key_ref[head, :, LANES:] = tail
    ones = jnp.ones((16, length), bf16)

    def group_step(group, carry):
        rows = pl.ds(pl.multiple_of(group * LANES, LANES), LANES)
        query_ref[:LANES, :] = qt_ref[rows, :]
        values = kv_ref[:, pl.ds(pl.multiple_of(D + group * LANES, LANES), LANES)].T
        for head in range(PER_GROUP):
            key_ref[head, :, :LANES] = kv_ref[:, rows] * masks[head]
        for head in range(PER_GROUP):
            scores = dot(key_ref[head], query_ref[...])
            top = jnp.max(scores, 0, keepdims=True)
            probs = jnp.exp(scores - top).astype(bf16)
            wide = jnp.concatenate([values[head * HEAD_DIM : (head + 1) * HEAD_DIM], ones], 0)
            out = dot(wide, probs)
            total = out[HEAD_DIM : HEAD_DIM + 1]
            to = pl.ds(pl.multiple_of(group * LANES + head * HEAD_DIM, HEAD_DIM), HEAD_DIM)
            ot_ref[to, :] = (out[:HEAD_DIM] / total).astype(bf16)
            lse_ref[pl.ds(group * PER_GROUP + head, 1), :] = top + jnp.log(total)
        return carry

    lax.fori_loop(0, GROUPS, group_step, 0)
    jobs[0].wait([3])
    q_ref[...] = ot_ref[...].T
    m_ref[...] = x_ref[...].astype(f32) + (dot(q_ref[...], w_ref[:, :, :, 3 * D :].reshape(D, D)) + vec_ref[BIAS_OUT : BIAS_OUT + 1, :])

    def after(rows, _):
        unit, _ = unit_of(m_ref[rows, :])
        b_ref[rows, :] = (unit * vec_ref[GAIN_F : GAIN_F + 1, :] + vec_ref[SHIFT_F : SHIFT_F + 1, :]).astype(bf16)

    row_loop(length, 128, after)
    bt_ref[...] = b_ref[...].T
    for job in jobs[1:]:
        job.wait()


def assemble_kernel(offset, by_rows, coords, *refs):
    Assembly(coords, by_rows, refs[:4], offset, refs[4], refs[5]).wait()


def ffn_fwd_kernel(offsets, last, coords, m_ref, b_ref, vec_ref, *refs):
    offset, offset_down = offsets
    if offset is None:
        up_ref, down_ref, y_ref, zt_ref, slope_ref, z_ref = refs
    elif offset_down is None:
        down_ref, *pieces, y_ref, zt_ref, slope_ref, up_ref, z_ref, sems = refs
    else:
        *pieces, y_ref, zt_ref, slope_ref, up_ref, down_ref, z_ref, sems = refs
    if offset is not None:
        job = Assembly(coords, False, pieces, offset, up_ref, sems.at[0])
    if offset_down is not None:
        job_down = Assembly(coords, True, pieces, offset_down, down_ref, sems.at[1])
    length = m_ref.shape[0]
    normed = b_ref[...]
    for block in range(BLOCKS):
        if offset is not None:
            job.wait([block])
        columns = slice(block * D, (block + 1) * D)
        part = up_ref[:, columns] if offset is None else up_ref[:, :, :, columns].reshape(D, D)
        pre = dot(normed, part) + vec_ref[BIAS_UP + block : BIAS_UP + block + 1, :]
        cdf, bell = gelu_parts(pre)
        z_ref[:, columns] = (pre * cdf).astype(bf16)
        slope_ref[:, columns] = (cdf + pre * bell).astype(bf16)
        zt_ref[columns, :] = z_ref[:, columns].T
    if offset_down is not None:
        job_down.wait()
    out = m_ref[...] + (dot(z_ref[...], down_ref[...].reshape(FF, D)) + vec_ref[BIAS_DOWN : BIAS_DOWN + 1, :])
    if last:
        row = lax.broadcasted_iota(jnp.int32, (length, 1), 0)
        out = jnp.where(row < coords[4], out, 0.0)
    y_ref[...] = out.astype(y_ref.dtype)


def ffn_bwd_kernel(top, coords, g_ref, slope_ref, m_ref, vec_ref, up_ref, down_ref, *refs):
    gb_ref, gu_ref, gm_ref, gmb_ref, sums_ref = refs
    length = m_ref.shape[0]
    sums_ref[...] = jnp.zeros_like(sums_ref)

    def add(row, value):
        sums_ref[row : row + 1, :] += column_sum(value)

    grad = g_ref[...].astype(f32)
    if top:
        row = lax.broadcasted_iota(jnp.int32, (length, 1), 0)
        grad = jnp.where(row < coords[4], grad, 0.0)
    low = grad.astype(bf16)
    gb_ref[...] = low
    add(BIAS_DOWN, low.astype(f32))
    for block in range(BLOCKS):
        columns = slice(block * D, (block + 1) * D)
        part = (dot_nt(low, down_ref[columns, :]) * slope_ref[:, columns].astype(f32)).astype(bf16)
        gu_ref[:, columns] = part
        add(BIAS_UP + block, part.astype(f32))
    gm_ref[...] = dot_nt(gu_ref[...], up_ref[...])

    def after(rows, i):
        normed_grad = gm_ref[rows, :]
        unit, inverse = unit_of(m_ref[rows, :])
        add(GAIN_F, normed_grad * unit)
        add(SHIFT_F, normed_grad)
        grad = g_ref[rows, :].astype(f32)
        if top:
            row = lax.broadcasted_iota(jnp.int32, (128, 1), 0) + i * 128
            grad = jnp.where(row < coords[4], grad, 0.0)
        middle = grad + norm_back(normed_grad, unit, inverse, vec_ref[GAIN_F : GAIN_F + 1, :])
        gm_ref[rows, :] = middle
        low = middle.astype(bf16)
        gmb_ref[rows, :] = low
        add(BIAS_OUT, low.astype(f32))

    row_loop(length, 128, after)


def attn_bwd_kernel(groups, coords, gmb_ref, qt_ref, kv_ref, ot_ref, lse_ref, table_ref, w_ref, *refs):
    start, count = groups
    gp_ref, *flip_ref, go_ref, key_ref, query_ref = refs
    length = gmb_ref.shape[0]
    low = gmb_ref[...]
    if flip_ref:
        flip_ref[0][...] = low.T
    go_ref[...] = dot_nt(w_ref[start * LANES : (start + count) * LANES, 3 * D :], low).astype(bf16)
    masks = head_masks()
    tail, query_ref[LANES:, :] = masked_tail(length, coords[4])
    for head in range(PER_GROUP):
        key_ref[head, :, LANES:] = tail

    def group_step(i, carry):
        group = i + start
        rows = pl.ds(pl.multiple_of(group * LANES, LANES), LANES)
        query, grad = qt_ref[rows, :], go_ref[pl.ds(pl.multiple_of(i * LANES, LANES), LANES), :]
        query_ref[:LANES, :] = query
        keys = kv_ref[:, rows]
        values = kv_ref[:, pl.ds(pl.multiple_of(D + group * LANES, LANES), LANES)]
        flipped = keys.T
        products = grad.astype(f32) * ot_ref[rows, :].astype(f32)
        for head in range(PER_GROUP):
            key_ref[head, :, :LANES] = keys * masks[head]
        for head in range(PER_GROUP):
            part = slice(head * HEAD_DIM, (head + 1) * HEAD_DIM)
            delta = column_sum(products[part])
            probs = jnp.exp(dot(key_ref[head], query_ref[...]) - lse_ref[pl.ds(group * PER_GROUP + head, 1), :])
            scores = (probs * (dot(values * masks[head], grad) - delta)).astype(bf16)
            dv = dot_nt(grad[part], probs.astype(bf16))
            dk = dot_nt(query[part], scores)
            dq = dot(flipped[part], scores)
            to = pl.ds(pl.multiple_of(i * LANES + head * HEAD_DIM, HEAD_DIM), HEAD_DIM)
            dq = rotated_back(dq.astype(bf16).astype(f32), table_ref) * HEAD_DIM**-0.5
            dk = rotated_back(dk.astype(bf16).astype(f32), table_ref)
            for part, value in enumerate((dq, dk, dv)):
                gp_ref[part, to, :] = value.astype(bf16)
        return carry

    lax.fori_loop(0, count, group_step, 0)


def attn_after_kernel(early_ref, late_ref, gm_ref, x_ref, vec_ref, w_ref, *refs):
    gx_ref, sums_ref, ga_ref = refs
    length = x_ref.shape[0]
    sums_ref[...] = jnp.zeros_like(sums_ref)

    def add(row, value):
        sums_ref[row : row + 1, :] += column_sum(value)

    ones = jnp.ones((16, length), bf16)
    total = 0.0
    for part in range(3):
        for ref, (start, count) in ((early_ref, EARLY), (late_ref, LATE)):
            columns = slice(start * LANES, (start + count) * LANES)
            sums_ref[BIAS_QKV + part : BIAS_QKV + part + 1, columns] = dot_nt(ones, ref[part])[:1]
            total = total + dot(w_ref[:, part * D + start * LANES : part * D + (start + count) * LANES], ref[part])
    ga_ref[...] = total.T

    def after(rows, _):
        normed_grad = ga_ref[rows, :]
        unit, inverse = unit_of(x_ref[rows, :].astype(f32))
        add(GAIN_A, normed_grad * unit)
        add(SHIFT_A, normed_grad)
        out = gm_ref[rows, :] + norm_back(normed_grad, unit, inverse, vec_ref[GAIN_A : GAIN_A + 1, :])
        gx_ref[rows, :] = out.astype(gx_ref.dtype)

    row_loop(length, 128, after)


def grads_kernel(items, inputs, phase, coords, *refs):
    ins, outs, (left_ref, whole_ref) = refs[:inputs], refs[inputs:-2], refs[-2:]

    def put(value, kb, ka, k2, k1, to):
        to = slice(to, to + value.shape[0])
        if phase:
            outs[0][kb, ka, k2, k1, to] = value
        elif kb:
            outs[0][ka, k2, k1, to] = value
        elif ka:
            outs[1][k2, k1, to] = value
        else:
            outs[2][k2, k1, to] = value

    for kind, lefts, right, to in items:
        if kind == "down":
            for kb in range(2):
                for place, (ka, k2, k1) in enumerate(PLACES):
                    z, y, x, n = owner_of(coords, phase, kb, ka, k2, k1)
                    start = pl.multiple_of((8 * z + 4 * y + 2 * x + n) * PIECE, PIECE)
                    left_ref[place * PIECE : (place + 1) * PIECE, :] = ins[lefts[0]][pl.ds(start, PIECE), :]
                whole = dot(left_ref[...], ins[right][...]).astype(bf16)
                for place, (ka, k2, k1) in enumerate(PLACES):
                    put(whole[place * PIECE : (place + 1) * PIECE], kb, ka, k2, k1, to)
        else:
            for kx in range(2):
                quarter = 2 * (coords[2] ^ kx) + (coords[3] ^ phase)
                n = coords[3] ^ phase
                for ky in range(2):
                    for kz in range(4):
                        k2, k1 = kz // 2, kz % 2
                        z = coords[0] ^ (2 * k1 + k2 + n * (k2 - k1))
                        start = pl.multiple_of((2 * z + (coords[1] ^ ky)) * PIECE, PIECE)
                        to_row = (4 * ky + kz) * PIECE
                        if kind == "up":
                            part = ins[lefts[0]][pl.ds(start, PIECE), :]
                        else:
                            part = jnp.where(quarter == 3, ins[lefts[1]][pl.ds(start, PIECE), :], ins[lefts[0]][pl.ds(start, PIECE), :])
                        left_ref[to_row : to_row + PIECE, :] = part
                if kind == "attn":

                    @pl.when(quarter == 3)
                    def _(right=right):
                        whole_ref[...] = dot_nt(left_ref[...], ins[right][...]).astype(bf16)

                    @pl.when(quarter < 3)
                    def _(right=right, quarter=quarter):
                        part = jnp.minimum(quarter, 2)
                        for i, (start, count) in ((2, EARLY), (1, LATE)):
                            columns = slice(start * LANES, (start + count) * LANES)
                            whole_ref[:, columns] = dot_nt(left_ref[...], ins[right - i][part]).astype(bf16)

                else:
                    columns = pl.ds(pl.multiple_of(quarter * D, D), D)
                    whole_ref[...] = dot(left_ref[...], ins[right][:, columns]).astype(bf16)

                def write(swapped, kx=kx, to=to):
                    for ky in range(2):
                        for kz in range(4):
                            start = (4 * ky + kz) * PIECE
                            ka, kb = (ky, kx) if swapped else (kx, ky)
                            put(whole_ref[start : start + PIECE, :], kb, ka, kz // 2, kz % 2, to)

                pl.when(n == 0)(functools.partial(write, False))
                pl.when(n == 1)(functools.partial(write, True))


def call(kernel, ins, outs, scratch, name, flops, exps=0):
    moved = sum(a.size * a.dtype.itemsize for a, _ in ins) + sum(int(np.prod(s)) * jnp.dtype(t).itemsize for s, t in outs)
    limit = SLACK + sum(int(np.prod(t.shape)) * t.dtype.itemsize for t in scratch if t.memory_space == V)
    return pl.pallas_call(
        kernel,
        out_shape=[jax.ShapeDtypeStruct(s, t) for s, t in outs],
        in_specs=[pl.BlockSpec(memory_space=space) for _, space in ins],
        out_specs=[pl.BlockSpec(memory_space=pltpu.VMEM)] * len(outs),
        scratch_shapes=scratch,
        compiler_params=pltpu.CompilerParams(vmem_limit_bytes=limit),
        cost_estimate=pl.CostEstimate(flops=int(flops), bytes_accessed=int(moved), transcendentals=int(exps)),
        name=name,
    )(*[a for a, _ in ins])


V, S, H = pltpu.VMEM, pltpu.SMEM, pl.ANY
SEMS = pltpu.SemaphoreType.DMA


def attn_fwd(coords, x, vec, table, weights):
    n = x.shape[0]
    ins = [(coords, S), (x, V), (vec, V), (table[0], V)] + [(p, H) for w in weights for p in w[0]]
    outs = [((D, n), bf16), ((D, n), bf16), ((n, 2 * D), bf16), ((D, n), bf16), ((24, n), f32)]
    outs += [((n, D), f32), ((n, D), bf16), ((D, n), bf16)]
    outs += [(WHOLE_ROWS if w[2] else WHOLE, bf16) for w in weights]
    scratch = [V((n, D), bf16), V((n, D), bf16), V((PER_GROUP, n, 2 * LANES), bf16), V((2 * LANES, n), bf16)]
    scratch.append(SEMS((len(weights), 8)))
    kernel = functools.partial(attn_fwd_kernel, [w[1:] for w in weights])
    out = call(kernel, ins, outs, scratch, "attn_fwd", 2 * n * D * FF + 4 * n * n * D, HEADS * n * n)
    return dict(zip(("at", "qt", "kv", "ot", "lse", "m", "b", "bt"), out[:8], strict=True)) | {"x": x}, [w.reshape((FF, D) if w.ndim == 6 else (D, FF)) for w in out[8:]]


def assemble(coords, weight):
    pieces, offset, by_rows = weight
    outs = [(WHOLE_ROWS if by_rows else WHOLE, bf16)]
    ins = [(coords, S)] + [(p, H) for p in pieces]
    out = call(functools.partial(assemble_kernel, offset, by_rows), ins, outs, [SEMS((8,))], "assemble", 0)[0]
    return out.reshape((FF, D) if by_rows else (D, FF))


def ffn_fwd(coords, kept, vec, up, down, last):
    n = kept["m"].shape[0]
    parts = [isinstance(w, tuple) for w in (up, down)]
    ins = [(coords, S), (kept["m"], V), (kept["b"], V), (vec, V)]
    ins += [(w, V) for w, part in zip((up, down), parts) if not part]
    ins += [(p, H) for p in up[0]] if parts[0] else []
    outs = [((n, D), bf16 if last else f32), ((FF, n), bf16), ((n, FF), bf16)]
    outs += [(shape, bf16) for shape, part in zip((WHOLE, WHOLE_ROWS), parts) if part]
    scratch = [V((n, FF), bf16)] + ([SEMS((2, 8))] if parts[0] else [])
    offsets = [w[1] if part else None for w, part in zip((up, down), parts)]
    kernel = functools.partial(ffn_fwd_kernel, offsets, last)
    y, zt, slope, *more = call(kernel, ins, outs, scratch, "ffn_fwd", 4 * n * D * FF, 2 * n * FF)
    up = more[0].reshape(D, FF) if parts[0] else up
    down = more[1].reshape(FF, D) if parts[1] else down
    return y, {"zt": zt, "slope": slope}, up, down


def ffn_bwd(coords, g, kept, vec, up, down, top):
    n = g.shape[0]
    ins = [(coords, S)] + [(a, V) for a in (g, kept["slope"], kept["m"], vec, up, down)]
    outs = [((n, D), bf16), ((n, FF), bf16), ((n, D), f32), ((n, D), bf16), ((VECS, D), f32)]
    out = call(functools.partial(ffn_bwd_kernel, top), ins, outs, [], "ffn_bwd", 4 * n * D * FF, 0)
    return dict(zip(("gb", "gu", "gm", "gmb", "sums"), out, strict=True))


def attn_bwd(coords, gmb, kept, table, weight, groups):
    n = gmb.shape[0]
    ins = [(coords, S)] + [(a, V) for a in (gmb, kept["qt"], kept["kv"], kept["ot"], kept["lse"], table[1], weight)]
    rows = groups[1] * LANES
    scratch = [V((rows, n), bf16), V((PER_GROUP, n, 2 * LANES), bf16), V((2 * LANES, n), bf16)]
    outs = [((3, rows, n), bf16)] + ([((D, n), bf16)] if groups == LATE else [])
    flops = 2 * n * D * rows + 10 * n * n * rows
    kernel = functools.partial(attn_bwd_kernel, groups)
    return call(kernel, ins, outs, scratch, "attn_bwd", flops, HEADS * n * n)


def attn_after(back, kept, vec, weight, last):
    n = back["gm"].shape[0]
    ins = [(a, V) for a in (back["early"], back["late"], back["gm"], kept["x"], vec, weight)]
    outs = [((n, D), bf16 if last else f32), ((VECS, D), f32)]
    return call(attn_after_kernel, ins, outs, [V((n, D), f32)], "attn_after", 6 * n * D * D, 0)


def grads(coords, items, phase):
    arrays, plan, flops, rows = [], [], 0, 0
    for kind, lefts, right, height in items:
        index = list(range(len(arrays), len(arrays) + len(lefts)))
        arrays += [*lefts, right]
        plan.append((kind, index, len(arrays) - 1, rows))
        rows += height
        flops += 2 * arrays[0].shape[1] * D * D * 2
    leads = [(2, 2, 2, 2)] if phase else [(2, 2, 2), (2, 2), (2, 2)]
    outs = [((*lead, rows, D), bf16) for lead in leads]
    kernel = functools.partial(grads_kernel, plan, len(arrays), phase)
    ins = [(coords, S)] + [(a, V) for a in arrays]
    return call(kernel, ins, outs, [V((D, arrays[0].shape[1]), bf16), V((D, D), bf16)], "grads", flops, 0)


def mate(value):
    return lax.ppermute(value, "narrow", [(0, 1), (1, 0)])


def step(link, value):
    masks = ((8, 4, 1, 2)[link], (4, 8, 2, 1)[link])
    pairs = [(2 * w + n, 2 * (w ^ masks[n]) + n) for w in range(16) for n in range(2)]
    return lax.ppermute(value, AXES, pairs)


def relative(values, bits):
    for place_of, bit in enumerate(reversed(bits)):
        flip = 1 << place_of
        values = [jnp.where(bit > 0, values[i ^ flip], values[i]) for i in range(len(values))]
    return values


def add(*terms):
    return functools.reduce(lambda p, q: p + q, [t.astype(f32) for t in terms])


def regroup(parts, bits):
    mine = relative(parts, bits)
    return relative([mine[0]] + [lax.ppermute(mine[k], AXES, [(i, i ^ k) for i in range(32)]) for k in (1, 2, 3)], bits)


def vector_tables(gains, biases):
    gains = gains.astype(f32).reshape(LAYERS, 2, D)
    biases = biases.astype(f32).reshape(LAYERS, 11, D)
    return jnp.concatenate([gains, biases, jnp.zeros((LAYERS, VECS - 13, D), f32)], 1)


NAMES = ("down", "up", "attn")
LOTS = tuple(((name, l),) for l in (1, 0) for name in NAMES)


def whole_weight(matrix, by_rows):
    if by_rows:
        cut = jnp.transpose(matrix.reshape(4, 2, 2, 2, PIECE, D), (3, 1, 2, 0, 4, 5))
    else:
        cut = jnp.transpose(matrix.reshape(4, 2, PIECE, 2, 2, D), (4, 1, 3, 0, 2, 5))
    cut = [cut[0], jnp.swapaxes(cut[1], 0, 1)]
    return [cut[kn][kb] for kb in range(2) for kn in range(2)], 0, by_rows


def whole_grad(core, rest, rows, by_rows):
    near = jnp.stack([jnp.stack([rest[2], rest[1]]), rest[0]])
    cut = jnp.stack([jnp.transpose(near, (1, 0, 3, 2, 4, 5)), core])[..., rows, :]
    if by_rows:
        return jnp.transpose(cut, (3, 4, 2, 1, 0, 5, 6)).reshape(FF, D)
    return jnp.transpose(cut, (3, 4, 2, 5, 1, 0, 6)).reshape(D, FF)


def fetch_plain(w_qkv, w_out, w_up, w_down, gains, biases):
    def whole(value, rows):
        return lax.all_gather(value, AXES, axis=0, tiled=True).reshape(rows, -1)

    weights = {}
    for l in range(LAYERS):
        attn = jnp.concatenate([whole(w_qkv[l], D), whole(w_out[l], D)], 1)
        weights["attn", l] = whole_weight(attn, False)
        weights["up", l] = whole_weight(whole(w_up[l], D), False)
        weights["down", l] = whole_weight(whole(w_down[l], FF), True)
    return weights, vector_tables(whole(gains, 1)[0], whole(biases, 1)[0])


class Lot:
    def first(self, core, rest):
        self.core, self.rest = core, rest
        return add(rest[0], core[1]).astype(bf16)

    def second(self, got):
        self.got = got
        return add(self.rest[1], self.core[0, 1], got[1]).astype(bf16)

    def third(self, got):
        total = add(self.rest[2], self.core[0, 0], self.got[0], got)
        self.total = total[0]
        return total[1].astype(bf16)

    def fourth(self, got):
        total = add(self.total, got)
        self.total = total[0]
        return total[1].astype(bf16)

    def last(self, got):
        return add(self.total, got)


def stage(*groups):
    flat, tree = jax.tree.flatten(groups)
    return jax.tree.unflatten(tree, lax.optimization_barrier(flat))


def device_bits():
    wide = lax.axis_index("wide")
    return [(wide >> 3) & 1, (wide >> 2) & 1, (wide >> 1) & 1, wide & 1, lax.axis_index("narrow")]


def coordinates(values):
    return jnp.stack([jnp.asarray(v, jnp.int32) for v in values])


def layer_grads(sums):
    both = jnp.stack(sums)
    return both[:, :2].reshape(-1), both[:, 2:13].reshape(-1)


def gradient_blocks(coords, lot, kept, back, phase):
    items = []
    for name, l in LOTS[lot]:
        if name == "attn":
            items.append((name, [kept[l]["at"], kept[l]["ot"], back[l]["early"], back[l]["late"]], back[l]["flip"], PIECE))
        elif name == "up":
            items.append((name, [kept[l]["bt"]], back[l]["gu"], PIECE))
        else:
            items.append((name, [kept[l]["zt"]], back[l]["gb"], PIECE))
    outs = grads(coords, items, phase)
    return outs[0] if phase else outs


def shares_of(parts, bits):
    rows = D // 32
    cut = jnp.stack(parts)
    whole = jnp.concatenate(regroup([cut[:, s * rows : (s + 1) * rows] for s in range(4)], bits[3:]), 2)
    return [whole[i] for i in range(len(parts))]


def body(tokens, lengths, w_qkv, w_out, w_up, w_down, gains, biases, cotangent):
    args = (tokens, lengths, w_qkv, w_out, w_up, w_down, gains, biases, cotangent)
    if lax.axis_size("wide") == 16 and lax.axis_size("narrow") == 2:
        return staged(*args)
    return plain(*args)


def plain(tokens, lengths, w_qkv, w_out, w_up, w_down, gains, biases, cotangent):
    length = tokens.shape[0] // lengths.shape[0]
    coords = coordinates([0, 0, 0, 0, lengths[0]])
    table = rotary_tables(length)
    weights, vectors = fetch_plain(w_qkv, w_out, w_up, w_down, gains, biases)
    kept, back, wholes, x = [], [{}, {}], [], tokens
    for l in range(LAYERS):
        held, whole = attn_fwd(coords, x, vectors[l], table, [weights[name, l] for name in ("attn", "up", "down")])
        x, more, *_ = ffn_fwd(coords, held, vectors[l], whole[1], whole[2], l == LAYERS - 1)
        kept.append(held | more)
        wholes.append(whole)
    output, grad, sums = x, cotangent, [None] * LAYERS
    for l in reversed(range(LAYERS)):
        last = l == 0
        back[l] = ffn_bwd(coords, grad, kept[l], vectors[l], wholes[l][1], wholes[l][2], not last)
        (back[l]["early"],) = attn_bwd(coords, back[l]["gmb"], kept[l], table, wholes[l][0], EARLY)
        back[l]["late"], back[l]["flip"] = attn_bwd(coords, back[l]["gmb"], kept[l], table, wholes[l][0], LATE)
        grad, more = attn_after(back[l], kept[l], vectors[l], wholes[l][0], last)
        sums[l] = back[l]["sums"] + more
    matrices = {}
    for lot, keys in enumerate(LOTS):
        core, rest = [gradient_blocks(coords, lot, kept, back, phase) for phase in (1, 0)]
        for i, key in enumerate(keys):
            rows = slice(i * PIECE, (i + 1) * PIECE)
            matrices[key] = whole_grad(core, rest, rows, key[0] == "down").astype(f32)
    outs = []
    for name, begin, end in (("attn", 0, 3 * D), ("attn", 3 * D, FF), ("up", 0, FF), ("down", 0, D)):
        cut = jnp.stack([matrices[name, l][:, begin:end].reshape(-1) for l in range(LAYERS)])
        outs.append(lax.psum_scatter(cut, AXES, scatter_dimension=1, tiled=True))
    outs += [lax.psum_scatter(v, AXES, scatter_dimension=0, tiled=True) for v in layer_grads(sums)]
    return (output, grad, *outs)


def turned(value, bits):
    value = value.reshape(2, 2, 2, 2, 2, -1)
    for axis, bit in enumerate(bits):
        value = jnp.where(bit > 0, jnp.flip(value, axis), value)
    cores = [jnp.transpose(value, order) for order in ((4, 2, 3, 1, 0, 5), (4, 3, 2, 0, 1, 5))]
    own = jnp.where(bits[4] > 0, cores[1][0], cores[0][0])
    other = jnp.where(bits[4] > 0, cores[0][1], cores[1][1])
    return jnp.stack([own, other])


def ordered(bit, own, got):
    return jnp.stack([jnp.where(bit > 0, got, own), jnp.where(bit > 0, own, got)])


def staged(tokens, lengths, w_qkv, w_out, w_up, w_down, gains, biases, cotangent):
    length = tokens.shape[0] // lengths.shape[0]
    bits = device_bits()
    coords = coordinates([lax.axis_index("wide") >> 2, *bits[2:], lengths[0]])
    table = rotary_tables(length)
    rows = D // 32
    weights, whole = {}, {}

    z1, z0, y, x, n = bits
    third, fourth = jnp.where(n > 0, y, x), jnp.where(n > 0, x, y)

    def link0(value):
        return ordered(jnp.where(n > 0, z0, z1), value, step(0, value))

    def link1(value):
        return value, step(1, value)

    def by_z(pair):
        own, got = pair
        blocks = []
        for high in range(2):
            for low in range(2):
                core0 = jnp.where(z0 == low, own[high], got[high])
                blocks.append(jnp.where(n > 0, jnp.where(z1 == high, own[low], got[low]), core0))
        return jnp.stack(blocks)

    def link2(value):
        return ordered(third, value, step(2, value))

    def arrived(keys, *pieces):
        offset = 0
        for key, height in keys:
            weights[key] = (list(pieces), offset, key[0] == "down")
            offset += height

    small = jnp.concatenate([gains, biases])
    width = small.shape[0]
    c0 = jnp.concatenate([w_down[0].reshape(PIECE, D), jnp.zeros((16, D), bf16).at[0, :width].set(small)])
    c0, w_qkv, w_out, w_up = stage(c0, w_qkv, w_out, w_up)
    t0 = link0(c0)
    flat = []
    for l in range(LAYERS):
        flat.append(jnp.concatenate([w_qkv[l].reshape(rows, 3 * D), w_out[l].reshape(rows, D)], 1))
        flat.append(w_up[l].reshape(rows, FF))
    flat = jnp.stack(flat)
    parts = [flat[:, :, s * D : (s + 1) * D] for s in range(4)]
    t0, parts = stage(t0, parts)
    u0 = link1(t0)
    c1, up0, attn1, up1 = jnp.concatenate(regroup(parts, bits[3:]), 1)
    c2, c3 = jnp.concatenate([up0, attn1]), jnp.concatenate([w_down[1].reshape(PIECE, D), up1])
    zz0, c1, c2, c3 = stage(by_z(u0), c1, c2, c3)
    near0, t1 = stage(link2(zz0), link0(c1))
    far0, mate0, u1, t2 = step(3, near0), mate(near0), link1(t1), link0(c2)
    far0, mate0, zz1, t2 = stage(far0, mate0, by_z(u1), t2)
    near1, far_mate0, u2, t3 = link2(zz1), mate(far0), link1(t2), link0(c3)
    near1, far_mate0, zz2, t3 = stage(near1, far_mate0, by_z(u2), t3)
    arrived(((("down", 0), PIECE),), near0, mate0, far0, far_mate0)
    far1, mate1, near2, u3 = step(3, near1), mate(near1), link2(zz2), link1(t3)
    whole["down", 0] = assemble(coords, weights["down", 0])
    own, other = [], []
    for first, second, to in ((near0, far0, own), (mate0, far_mate0, other)):
        turn = n if to is own else 1 - n
        both = ordered(jnp.where(turn > 0, x, y), first[:, :, PIECE, :width], second[:, :, PIECE, :width])
        to.append(jnp.where(turn > 0, jnp.transpose(both, (2, 1, 0, 3)), jnp.transpose(both, (2, 0, 1, 3))))
    both = ordered(n, own[0], other[0])
    both = jnp.transpose(both, (1, 2, 3, 0, 4)).reshape(32, width)
    vectors = vector_tables(both[:, : gains.shape[0]].reshape(-1), both[:, gains.shape[0] :].reshape(-1))
    far1, mate1, near2, zz3, vectors, whole = stage(far1, mate1, near2, by_z(u3), vectors, whole)
    far_mate1, near2, zz3 = stage(mate(far1), near2, zz3)
    arrived(((("attn", 0), PIECE),), near1, mate1, far1, far_mate1)
    kept, back = [None, None], [None, None]
    far2, mate2 = step(3, near2), mate(near2)
    kept[0], got = attn_fwd(coords, tokens, vectors[0], table, [weights["attn", 0]])
    whole["attn", 0] = got[0]
    far2, mate2, kept[0] = stage(far2, mate2, kept[0])
    far_mate2, kept[0], zz3 = stage(mate(far2), kept[0], zz3)
    arrived(((("up", 0), PIECE), (("attn", 1), PIECE)), near2, mate2, far2, far_mate2)
    got3 = step(2, zz3)
    h, more, whole["up", 0], _ = ffn_fwd(coords, kept[0], vectors[0], weights["up", 0], whole["down", 0], False)
    kept[0] |= more
    got3, h = stage(got3, h)
    near3, h = stage(ordered(third, zz3, got3), h)
    far3, mate3 = step(3, near3), mate(near3)
    kept[1], got = attn_fwd(coords, h, vectors[1], table, [weights["attn", 1]])
    whole["attn", 1] = got[0]
    far3, mate3, kept[1] = stage(far3, mate3, kept[1])
    arrived(((("down", 1), PIECE), (("up", 1), PIECE)), near3, mate3, far3, mate(far3))
    output, more, whole["up", 1], whole["down", 1] = ffn_fwd(
        coords, kept[1], vectors[1], weights["up", 1], weights["down", 1], True
    )
    kept[1] |= more

    d1, u1, a1, d0, u0, a0 = [Lot() for _ in LOTS]

    def blocks(lot, phase):
        return gradient_blocks(coords, lot, kept, back, phase)

    live = jnp.arange(length, dtype=jnp.int32)[:, None] < lengths[0]
    back[1] = {"gb": jnp.where(live, cotangent, jnp.zeros((), bf16))}
    core, back[1] = stage(blocks(0, 1), back[1])
    first, cotangent = stage(d1.first(mate(core), blocks(0, 0)), cotangent)

    got_d1 = step(3, first)
    back[1] |= ffn_bwd(coords, cotangent, kept[1], vectors[1], whole["up", 1], whole["down", 1], True)
    got_d1, core, back[1] = stage(got_d1, blocks(1, 1), back[1])
    second, core, back[1] = stage(d1.second(got_d1), core, back[1])

    got_d1, core, rest = stage(step(2, second), mate(core), blocks(1, 0))
    first, third, back[1] = stage(u1.first(core, rest), d1.third(got_d1), back[1])

    got_u1, got_d1 = step(3, first), step(1, third)
    (back[1]["early"],) = attn_bwd(coords, back[1]["gmb"], kept[1], table, whole["attn", 1], EARLY)
    got_u1, got_d1, back[1] = stage(got_u1, got_d1, back[1])
    second, fourth, back[1] = stage(u1.second(got_u1), d1.fourth(got_d1), back[1])

    got_u1, got_d1 = step(2, second), step(0, fourth)
    back[1]["late"], back[1]["flip"] = attn_bwd(coords, back[1]["gmb"], kept[1], table, whole["attn", 1], LATE)
    got_u1, got_d1, core, back[1] = stage(got_u1, got_d1, blocks(2, 1), back[1])
    third, core, back[1] = stage(u1.third(got_u1), core, back[1])

    got_u1, core, rest = stage(step(1, third), mate(core), blocks(2, 0))
    first, fourth, back[1] = stage(a1.first(core, rest), u1.fourth(got_u1), back[1])

    got_a1, got_u1 = step(3, first), step(0, fourth)
    grad, more = attn_after(back[1], kept[1], vectors[1], whole["attn", 1], False)
    sums = [None, back[1]["sums"] + more]
    back[0] = {"gb": grad.astype(bf16)}
    got_a1, got_u1, core, grad, back[0] = stage(got_a1, got_u1, blocks(3, 1), grad, back[0])
    second, core, grad, back[0] = stage(a1.second(got_a1), core, grad, back[0])

    got_a1, core, rest = stage(step(2, second), mate(core), blocks(3, 0))
    first, third, grad, back[0] = stage(d0.first(core, rest), a1.third(got_a1), grad, back[0])

    got_d0, got_a1 = step(3, first), step(1, third)
    back[0] |= ffn_bwd(coords, grad, kept[0], vectors[0], whole["up", 0], whole["down", 0], False)
    got_d0, got_a1, core, back[0] = stage(got_d0, got_a1, blocks(4, 1), back[0])
    second, fourth, core, back[0] = stage(d0.second(got_d0), a1.fourth(got_a1), core, back[0])

    got_d0, got_a1, core, rest = stage(step(2, second), step(0, fourth), mate(core), blocks(4, 0))
    first, third, back[0] = stage(u0.first(core, rest), d0.third(got_d0), back[0])

    got_u0, got_d0 = step(3, first), step(1, third)
    (back[0]["early"],) = attn_bwd(coords, back[0]["gmb"], kept[0], table, whole["attn", 0], EARLY)
    got_u0, got_d0, back[0] = stage(got_u0, got_d0, back[0])
    second, fourth, back[0] = stage(u0.second(got_u0), d0.fourth(got_d0), back[0])

    got_u0, got_d0 = step(2, second), step(0, fourth)
    back[0]["late"], back[0]["flip"] = attn_bwd(coords, back[0]["gmb"], kept[0], table, whole["attn", 0], LATE)
    got_u0, got_d0, core, back[0] = stage(got_u0, got_d0, blocks(5, 1), back[0])
    third, core, back[0] = stage(u0.third(got_u0), core, back[0])

    got_u0, core, rest = stage(step(1, third), mate(core), blocks(5, 0))
    first, fourth, back[0] = stage(a0.first(core, rest), u0.fourth(got_u0), back[0])

    got_a0, got_u0 = step(3, first), step(0, fourth)
    grad, more = attn_after(back[0], kept[0], vectors[0], whole["attn", 0], True)
    sums[0] = back[0]["sums"] + more
    got_a0, got_u0, grad, sums = stage(got_a0, got_u0, grad, sums)
    small = turned(jnp.concatenate([v.reshape(32, -1) for v in layer_grads(sums)], 1), bits)[..., None, :]
    small = jnp.pad(small, ((0, 0),) * 5 + ((0, 15), (0, D - width))).astype(bf16)
    extra = Lot()
    first_x = extra.first(mate(small[1]), [small[0, 1], small[0, 0, 1], small[0, 0, 0]])
    second, first_x = stage(a0.second(got_a0), first_x)

    got_a0, got_x = step(2, second), step(3, first_x)
    up1, attn1, up0 = shares_of([u1.last(got_u1), a1.last(got_a1), u0.last(got_u0)], bits)
    got_x = step(2, extra.second(got_x))
    got_a0, got_x, up1, attn1, up0 = stage(got_a0, got_x, up1, attn1, up0)
    third = jnp.concatenate([a0.third(got_a0), extra.third(got_x)], -2)
    a0.total = jnp.concatenate([a0.total, extra.total], -2)
    got_a0 = step(1, third)
    fourth = a0.fourth(got_a0)
    done_a0 = a0.last(step(0, fourth))
    (attn0,) = shares_of([done_a0[:PIECE]], bits)
    mine = done_a0[PIECE, :width]
    return (
        output,
        grad,
        jnp.stack([v[:, : 3 * D].reshape(-1) for v in (attn0, attn1)]),
        jnp.stack([v[:, 3 * D :].reshape(-1) for v in (attn0, attn1)]),
        jnp.stack([up0.reshape(-1), up1.reshape(-1)]),
        jnp.stack([d0.last(got_d0).reshape(-1), d1.last(got_d1).reshape(-1)]),
        mine[: gains.shape[0]],
        mine[gains.shape[0] :],
    )


def solution(mesh):
    both, flat, rows = P(AXES), P(None, AXES), P(AXES, None)
    return jax.shard_map(
        body,
        mesh=mesh,
        in_specs=(rows, both, flat, flat, flat, flat, both, both, rows),
        out_specs=(rows, rows, flat, flat, flat, flat, both, both),
        check_vma=False,
    )
```

```python
import functools

import jax
import jax.numpy as jnp
import numpy as np
from jax import lax
from jax.experimental import pallas as pl
from jax.experimental.pallas import tpu as pltpu
from jax.sharding import PartitionSpec as P

D = 640
HEADS = 20
HEAD_DIM = 32
FF = 2560
LAYERS = 2
EPSILON = 1e-05
MASKED = -1e9
LANES = 128
GROUPS = D // LANES
PER_GROUP = LANES // HEAD_DIM
BLOCKS = FF // D
EARLY, LATE = (0, 3), (3, 2)
PIECE = 80
VECS = 16
AXES = ("wide", "narrow")
WHOLE, WHOLE_ROWS = (4, 2, PIECE, FF), (4, 2, 2, 2, PIECE, D)
SLACK = 8 * 1024 * 1024
f32, bf16 = jnp.float32, jnp.bfloat16

GAIN_A, GAIN_F, SHIFT_A, BIAS_QKV, BIAS_OUT, SHIFT_F, BIAS_UP, BIAS_DOWN = 0, 1, 2, 3, 6, 7, 8, 12


def rotary_tables(length):
    half = HEAD_DIM // 2
    inverse = 1.0 / 10000.0 ** (np.arange(half) * (2.0 / HEAD_DIM))
    angles = np.arange(length)[:, None] * inverse[None, :]
    cos, sine = np.cos(angles), np.sin(angles)
    none = np.zeros_like(sine)
    ahead = np.tile(np.concatenate([-sine, none], 1), (1, PER_GROUP))
    behind = np.tile(np.concatenate([none, sine], 1), (1, PER_GROUP))
    wide = np.stack([np.tile(cos, (1, 2 * PER_GROUP)), ahead, behind]).astype(np.float32)
    return jnp.asarray(wide), jnp.asarray(np.stack([cos.T, sine.T]).astype(np.float32))


def dot(left, right):
    return jnp.dot(left, right, preferred_element_type=f32)


def dot_nt(left, right):
    return lax.dot_general(left, right, (((1,), (1,)), ((), ())), preferred_element_type=f32)


def dot_tn(left, right):
    return lax.dot_general(left, right, (((0,), (0,)), ((), ())), preferred_element_type=f32)


def rotated(value, table):
    half = HEAD_DIM // 2
    return value * table[0] + pltpu.roll(value, LANES - half, 1) * table[1] + pltpu.roll(value, half, 1) * table[2]


def rotated_back(value, table):
    half = HEAD_DIM // 2
    first, second = value[:half], value[half:]
    return jnp.concatenate([first * table[0] + second * table[1], second * table[0] - first * table[1]], 0)


def unit_of(value):
    centered = value - jnp.mean(value, -1, keepdims=True)
    inverse = lax.rsqrt(jnp.mean(centered * centered, -1, keepdims=True) + EPSILON)
    return centered * inverse, inverse


def norm_back(grad, unit, inverse, gain):
    scaled = grad * gain
    return inverse * (scaled - jnp.mean(scaled, -1, keepdims=True) - unit * jnp.mean(scaled * unit, -1, keepdims=True))


def column_sum(value):
    return jnp.sum(value, 0, keepdims=True)


def gelu_parts(value):
    scaled = jnp.abs(value) * 0.7071067811865476
    t = 1.0 / (1.0 + 0.3275911 * scaled)
    bell = jnp.exp(-scaled * scaled)
    series = t * (0.127414796 + t * (-0.142248368 + t * (0.7107068705 + t * (-0.7265760135 + t * 0.5307027145))))
    tail = series * bell
    return jnp.where(value >= 0.0, 1.0 - tail, tail), bell * 0.3989422804014327


def row_loop(length, step, body):
    def run(i, carry):
        body(pl.ds(pl.multiple_of(i * step, step), step), i)
        return carry

    lax.fori_loop(0, length // step, run, 0)


def owner_of(coords, kn, kb, ka, k2, k1):
    n = coords[3] ^ kn
    z = coords[0] ^ (2 * k1 + k2 + n * (k2 - k1))
    return z, coords[1] ^ (kb + n * (ka - kb)), coords[2] ^ (ka + n * (kb - ka)), n


PLACES = [(ka, k2, k1) for ka in range(2) for k2 in range(2) for k1 in range(2)]


class Assembly:
    def __init__(self, coords, by_rows, pieces, offset, whole, sems):
        self.by_rows, self.whole, self.sems = by_rows, whole, sems
        self.any = pieces[0].at[0, :, pl.ds(offset, PIECE)]
        for kb in range(2):
            for kn in range(2):
                n = coords[3] ^ kn
                b = (coords[1] + n * (coords[2] - coords[1])) ^ kb
                for a in range(2):
                    target = self.target(a + n * (b - a), b + n * (a - b), n)
                    pltpu.make_async_copy(pieces[2 * kb + kn].at[a, :, pl.ds(offset, PIECE)], *target).start()

    def target(self, x, y, n):
        to = (y, x, n) if self.by_rows else (y, slice(None), pl.ds(pl.multiple_of((2 * x + n) * D, D), D))
        return self.whole.at[(slice(None), *to)], self.sems.at[4 * x + 2 * n + y]

    def wait(self, quarters=(0, 1, 2, 3)):
        for quarter in quarters:
            for y in range(2):
                pltpu.make_async_copy(self.any, *self.target(quarter // 2, y, quarter % 2)).wait()


def head_masks():
    lane = lax.broadcasted_iota(jnp.int32, (1, LANES), 1)
    return [(lane // HEAD_DIM == head).astype(f32).astype(bf16) for head in range(PER_GROUP)]


def masked_tail(length, live):
    row = lax.broadcasted_iota(jnp.int32, (length, LANES), 0)
    lane = lax.broadcasted_iota(jnp.int32, (length, LANES), 1)
    keys = jnp.where((lane == 0) & (row >= live), MASKED, 0.0).astype(bf16)
    row = lax.broadcasted_iota(jnp.int32, (LANES, length), 0)
    return keys, jnp.where(row == 0, 1.0, 0.0).astype(bf16)


def attn_fwd_kernel(plan, coords, x_ref, vec_ref, table_ref, *refs):
    count = len(plan)
    pieces, refs = refs[: 4 * count], refs[4 * count :]
    at_ref, qt_ref, kv_ref, ot_ref, lse_ref, m_ref, b_ref, bt_ref, *refs = refs
    wholes, refs = refs[:count], refs[count:]
    a_ref, q_ref, key_ref, query_ref, sems = refs
    length = x_ref.shape[0]
    jobs = [
        Assembly(coords, by_rows, pieces[4 * i : 4 * i + 4], offset, wholes[i], sems.at[i])
        for i, (offset, by_rows) in enumerate(plan)
    ]
    w_ref = wholes[0]

    def norm(rows, _):
        unit, _ = unit_of(x_ref[rows, :].astype(f32))
        a_ref[rows, :] = (unit * vec_ref[GAIN_A : GAIN_A + 1, :] + vec_ref[SHIFT_A : SHIFT_A + 1, :]).astype(bf16)

    row_loop(length, 128, norm)
    normed = a_ref[...]
    at_ref[...] = normed.T
    for part in range(3):
        jobs[0].wait([part])
        out = dot(normed, w_ref[:, :, :, part * D : (part + 1) * D].reshape(D, D)) + vec_ref[BIAS_QKV + part : BIAS_QKV + part + 1, :]
        if part == 0:
            out = out * HEAD_DIM**-0.5
        for group in range(GROUPS):
            lanes = slice(group * LANES, (group + 1) * LANES)
            piece = out[:, lanes]
            if part < 2:
                piece = rotated(piece, table_ref)
            if part == 0:
                qt_ref[lanes, :] = piece.astype(bf16).T
            else:
                kv_ref[:, (part - 1) * D + group * LANES : (part - 1) * D + (group + 1) * LANES] = piece.astype(bf16)
    masks = head_masks()
    tail, query_ref[LANES:, :] = masked_tail(length, coords[4])
    for head in range(PER_GROUP):
        key_ref[head, :, LANES:] = tail
    ones = jnp.ones((16, length), bf16)

    def group_step(group, carry):
        rows = pl.ds(pl.multiple_of(group * LANES, LANES), LANES)
        query_ref[:LANES, :] = qt_ref[rows, :]
        values = kv_ref[:, pl.ds(pl.multiple_of(D + group * LANES, LANES), LANES)].T
        for head in range(PER_GROUP):
            key_ref[head, :, :LANES] = kv_ref[:, rows] * masks[head]
        every = dot(key_ref[...].reshape(PER_GROUP * length, 2 * LANES), query_ref[...])
        for head in range(PER_GROUP):
            scores = every[head * length : (head + 1) * length]
            top = jnp.max(scores, 0, keepdims=True)
            probs = jnp.exp(scores - top).astype(bf16)
            wide = jnp.concatenate([values[head * HEAD_DIM : (head + 1) * HEAD_DIM], ones], 0)
            out = dot(wide, probs)
            total = out[HEAD_DIM : HEAD_DIM + 1]
            to = pl.ds(pl.multiple_of(group * LANES + head * HEAD_DIM, HEAD_DIM), HEAD_DIM)
            ot_ref[to, :] = (out[:HEAD_DIM] / total).astype(bf16)
            lse_ref[pl.ds(group * PER_GROUP + head, 1), :] = top + jnp.log(total)
        return carry

    for group in range(GROUPS):
        group_step(group, 0)
    jobs[0].wait([3])
    q_ref[...] = ot_ref[...].T
    m_ref[...] = x_ref[...].astype(f32) + (dot(q_ref[...], w_ref[:, :, :, 3 * D :].reshape(D, D)) + vec_ref[BIAS_OUT : BIAS_OUT + 1, :])

    def after(rows, _):
        unit, _ = unit_of(m_ref[rows, :])
        b_ref[rows, :] = (unit * vec_ref[GAIN_F : GAIN_F + 1, :] + vec_ref[SHIFT_F : SHIFT_F + 1, :]).astype(bf16)

    row_loop(length, 128, after)
    bt_ref[...] = b_ref[...].T
    for job in jobs[1:]:
        job.wait()


def assemble_kernel(offset, by_rows, coords, *refs):
    Assembly(coords, by_rows, refs[:4], offset, refs[4], refs[5]).wait()


def ffn_fwd_kernel(offsets, last, coords, m_ref, b_ref, vec_ref, *refs):
    offset, offset_down = offsets
    if offset is None:
        up_ref, down_ref, y_ref, zt_ref, slope_ref, z_ref = refs
    elif offset_down is None:
        down_ref, *pieces, y_ref, zt_ref, slope_ref, up_ref, z_ref, sems = refs
    else:
        *pieces, y_ref, zt_ref, slope_ref, up_ref, down_ref, z_ref, sems = refs
    if offset is not None:
        job = Assembly(coords, False, pieces, offset, up_ref, sems.at[0])
    if offset_down is not None:
        job_down = Assembly(coords, True, pieces, offset_down, down_ref, sems.at[1])
    length = m_ref.shape[0]
    normed = b_ref[...]
    for block in range(BLOCKS):
        if offset is not None:
            job.wait([block])
        columns = slice(block * D, (block + 1) * D)
        part = up_ref[:, columns] if offset is None else up_ref[:, :, :, columns].reshape(D, D)
        pre = dot(normed, part) + vec_ref[BIAS_UP + block : BIAS_UP + block + 1, :]
        cdf, bell = gelu_parts(pre)
        z_ref[:, columns] = (pre * cdf).astype(bf16)
        slope_ref[:, columns] = (cdf + pre * bell).astype(bf16)
        zt_ref[columns, :] = z_ref[:, columns].T
    if offset_down is not None:
        job_down.wait()
    out = m_ref[...] + (dot(z_ref[...], down_ref[...].reshape(FF, D)) + vec_ref[BIAS_DOWN : BIAS_DOWN + 1, :])
    if last:
        row = lax.broadcasted_iota(jnp.int32, (length, 1), 0)
        out = jnp.where(row < coords[4], out, 0.0)
    y_ref[...] = out.astype(y_ref.dtype)


def ffn_bwd_kernel(top, coords, g_ref, slope_ref, m_ref, vec_ref, up_ref, down_ref, *refs):
    gb_ref, gu_ref, gm_ref, gmb_ref, sums_ref = refs
    length = m_ref.shape[0]
    sums_ref[...] = jnp.zeros_like(sums_ref)

    def add(row, value):
        sums_ref[row : row + 1, :] += column_sum(value)

    grad = g_ref[...].astype(f32)
    if top:
        row = lax.broadcasted_iota(jnp.int32, (length, 1), 0)
        grad = jnp.where(row < coords[4], grad, 0.0)
    low = grad.astype(bf16)
    gb_ref[...] = low
    add(BIAS_DOWN, low.astype(f32))
    for block in range(BLOCKS):
        columns = slice(block * D, (block + 1) * D)
        part = (dot_nt(low, down_ref[columns, :]) * slope_ref[:, columns].astype(f32)).astype(bf16)
        gu_ref[:, columns] = part
        add(BIAS_UP + block, part.astype(f32))
    gm_ref[...] = dot_nt(gu_ref[...], up_ref[...])

    def after(rows, i):
        normed_grad = gm_ref[rows, :]
        unit, inverse = unit_of(m_ref[rows, :])
        add(GAIN_F, normed_grad * unit)
        add(SHIFT_F, normed_grad)
        grad = g_ref[rows, :].astype(f32)
        if top:
            row = lax.broadcasted_iota(jnp.int32, (128, 1), 0) + i * 128
            grad = jnp.where(row < coords[4], grad, 0.0)
        middle = grad + norm_back(normed_grad, unit, inverse, vec_ref[GAIN_F : GAIN_F + 1, :])
        gm_ref[rows, :] = middle
        low = middle.astype(bf16)
        gmb_ref[rows, :] = low
        add(BIAS_OUT, low.astype(f32))

    row_loop(length, 128, after)


def attn_bwd_kernel(groups, coords, gmb_ref, qt_ref, kv_ref, ot_ref, lse_ref, table_ref, w_ref, *refs):
    start, count = groups
    gp_ref, *flip_ref, go_ref, key_ref, query_ref = refs
    length = gmb_ref.shape[0]
    low = gmb_ref[...]
    if flip_ref:
        flip_ref[0][...] = low.T
    go_ref[...] = dot_nt(w_ref[start * LANES : (start + count) * LANES, 3 * D :], low).astype(bf16)
    masks = head_masks()
    tail, query_ref[LANES:, :] = masked_tail(length, coords[4])
    for head in range(PER_GROUP):
        key_ref[head, :, LANES:] = tail

    def group_step(i, carry):
        group = i + start
        rows = pl.ds(pl.multiple_of(group * LANES, LANES), LANES)
        query, grad = qt_ref[rows, :], go_ref[pl.ds(pl.multiple_of(i * LANES, LANES), LANES), :]
        query_ref[:LANES, :] = query
        keys = kv_ref[:, rows]
        values = kv_ref[:, pl.ds(pl.multiple_of(D + group * LANES, LANES), LANES)]
        flipped = keys.T
        products = grad.astype(f32) * ot_ref[rows, :].astype(f32)
        for head in range(PER_GROUP):
            key_ref[head, :, :LANES] = keys * masks[head]
        for head in range(PER_GROUP):
            part = slice(head * HEAD_DIM, (head + 1) * HEAD_DIM)
            delta = column_sum(products[part])
            probs = jnp.exp(dot(key_ref[head], query_ref[...]) - lse_ref[pl.ds(group * PER_GROUP + head, 1), :])
            scores = (probs * (dot(values * masks[head], grad) - delta)).astype(bf16)
            dv = dot_nt(grad[part], probs.astype(bf16))
            dk = dot_nt(query[part], scores)
            dq = dot(flipped[part], scores)
            to = pl.ds(pl.multiple_of(i * LANES + head * HEAD_DIM, HEAD_DIM), HEAD_DIM)
            dq = rotated_back(dq.astype(bf16).astype(f32), table_ref) * HEAD_DIM**-0.5
            dk = rotated_back(dk.astype(bf16).astype(f32), table_ref)
            for part, value in enumerate((dq, dk, dv)):
                gp_ref[part, to, :] = value.astype(bf16)
        return carry

    lax.fori_loop(0, count, group_step, 0)


def attn_after_kernel(early_ref, late_ref, gm_ref, x_ref, vec_ref, w_ref, *refs):
    gx_ref, sums_ref, ga_ref = refs
    length = x_ref.shape[0]
    sums_ref[...] = jnp.zeros_like(sums_ref)

    def add(row, value):
        sums_ref[row : row + 1, :] += column_sum(value)

    ones = jnp.ones((16, length), bf16)
    total = 0.0
    for part in range(3):
        for ref, (start, count) in ((early_ref, EARLY), (late_ref, LATE)):
            columns = slice(start * LANES, (start + count) * LANES)
            sums_ref[BIAS_QKV + part : BIAS_QKV + part + 1, columns] = dot_nt(ones, ref[part])[:1]
            total = total + dot(w_ref[:, part * D + start * LANES : part * D + (start + count) * LANES], ref[part])
    ga_ref[...] = total.T

    def after(rows, _):
        normed_grad = ga_ref[rows, :]
        unit, inverse = unit_of(x_ref[rows, :].astype(f32))
        add(GAIN_A, normed_grad * unit)
        add(SHIFT_A, normed_grad)
        out = gm_ref[rows, :] + norm_back(normed_grad, unit, inverse, vec_ref[GAIN_A : GAIN_A + 1, :])
        gx_ref[rows, :] = out.astype(gx_ref.dtype)

    row_loop(length, 128, after)


def grads_kernel(items, inputs, phase, coords, *refs):
    ins, outs, (left_ref, whole_ref) = refs[:inputs], refs[inputs:-2], refs[-2:]

    def put(value, kb, ka, k2, k1, to):
        to = slice(to, to + value.shape[0])
        if phase:
            outs[0][kb, ka, k2, k1, to] = value
        elif kb:
            outs[0][ka, k2, k1, to] = value
        elif ka:
            outs[1][k2, k1, to] = value
        else:
            outs[2][k2, k1, to] = value

    for kind, lefts, right, to in items:
        if kind == "down":
            for kb in range(2):
                for place, (ka, k2, k1) in enumerate(PLACES):
                    z, y, x, n = owner_of(coords, phase, kb, ka, k2, k1)
                    start = pl.multiple_of((8 * z + 4 * y + 2 * x + n) * PIECE, PIECE)
                    left_ref[place * PIECE : (place + 1) * PIECE, :] = ins[lefts[0]][pl.ds(start, PIECE), :]
                whole = dot(left_ref[...], ins[right][...]).astype(bf16)
                for place, (ka, k2, k1) in enumerate(PLACES):
                    put(whole[place * PIECE : (place + 1) * PIECE], kb, ka, k2, k1, to)
        else:
            for kx in range(2):
                quarter = 2 * (coords[2] ^ kx) + (coords[3] ^ phase)
                n = coords[3] ^ phase
                for ky in range(2):
                    for kz in range(4):
                        k2, k1 = kz // 2, kz % 2
                        z = coords[0] ^ (2 * k1 + k2 + n * (k2 - k1))
                        start = pl.multiple_of((2 * z + (coords[1] ^ ky)) * PIECE, PIECE)
                        to_row = (4 * ky + kz) * PIECE
                        if kind == "up":
                            part = ins[lefts[0]][pl.ds(start, PIECE), :]
                        else:
                            part = jnp.where(quarter == 3, ins[lefts[1]][pl.ds(start, PIECE), :], ins[lefts[0]][pl.ds(start, PIECE), :])
                        left_ref[to_row : to_row + PIECE, :] = part
                if kind == "attn":

                    @pl.when(quarter == 3)
                    def _(right=right):
                        whole_ref[...] = dot_nt(left_ref[...], ins[right][...]).astype(bf16)

                    @pl.when(quarter < 3)
                    def _(right=right, quarter=quarter):
                        part = jnp.minimum(quarter, 2)
                        for i, (start, count) in ((2, EARLY), (1, LATE)):
                            columns = slice(start * LANES, (start + count) * LANES)
                            whole_ref[:, columns] = dot_nt(left_ref[...], ins[right - i][part]).astype(bf16)

                else:
                    columns = pl.ds(pl.multiple_of(quarter * D, D), D)
                    whole_ref[...] = dot(left_ref[...], ins[right][:, columns]).astype(bf16)

                def write(swapped, kx=kx, to=to):
                    for ky in range(2):
                        for kz in range(4):
                            start = (4 * ky + kz) * PIECE
                            ka, kb = (ky, kx) if swapped else (kx, ky)
                            put(whole_ref[start : start + PIECE, :], kb, ka, kz // 2, kz % 2, to)

                pl.when(n == 0)(functools.partial(write, False))
                pl.when(n == 1)(functools.partial(write, True))


def call(kernel, ins, outs, scratch, name, flops, exps=0):
    moved = sum(a.size * a.dtype.itemsize for a, _ in ins) + sum(int(np.prod(s)) * jnp.dtype(t).itemsize for s, t in outs)
    limit = SLACK + sum(int(np.prod(t.shape)) * t.dtype.itemsize for t in scratch if t.memory_space == V)
    return pl.pallas_call(
        kernel,
        out_shape=[jax.ShapeDtypeStruct(s, t) for s, t in outs],
        in_specs=[pl.BlockSpec(memory_space=space) for _, space in ins],
        out_specs=[pl.BlockSpec(memory_space=pltpu.VMEM)] * len(outs),
        scratch_shapes=scratch,
        compiler_params=pltpu.CompilerParams(vmem_limit_bytes=limit),
        cost_estimate=pl.CostEstimate(flops=int(flops), bytes_accessed=int(moved), transcendentals=int(exps)),
        name=name,
    )(*[a for a, _ in ins])


V, S, H = pltpu.VMEM, pltpu.SMEM, pl.ANY
SEMS = pltpu.SemaphoreType.DMA


def attn_fwd(coords, x, vec, table, weights):
    n = x.shape[0]
    ins = [(coords, S), (x, V), (vec, V), (table[0], V)] + [(p, H) for w in weights for p in w[0]]
    outs = [((D, n), bf16), ((D, n), bf16), ((n, 2 * D), bf16), ((D, n), bf16), ((24, n), f32)]
    outs += [((n, D), f32), ((n, D), bf16), ((D, n), bf16)]
    outs += [(WHOLE_ROWS if w[2] else WHOLE, bf16) for w in weights]
    scratch = [V((n, D), bf16), V((n, D), bf16), V((PER_GROUP, n, 2 * LANES), bf16), V((2 * LANES, n), bf16)]
    scratch.append(SEMS((len(weights), 8)))
    kernel = functools.partial(attn_fwd_kernel, [w[1:] for w in weights])
    out = call(kernel, ins, outs, scratch, "attn_fwd", 2 * n * D * FF + 4 * n * n * D, HEADS * n * n)
    return dict(zip(("at", "qt", "kv", "ot", "lse", "m", "b", "bt"), out[:8], strict=True)) | {"x": x}, [w.reshape((FF, D) if w.ndim == 6 else (D, FF)) for w in out[8:]]


def assemble(coords, weight):
    pieces, offset, by_rows = weight
    outs = [(WHOLE_ROWS if by_rows else WHOLE, bf16)]
    ins = [(coords, S)] + [(p, H) for p in pieces]
    out = call(functools.partial(assemble_kernel, offset, by_rows), ins, outs, [SEMS((8,))], "assemble", 0)[0]
    return out.reshape((FF, D) if by_rows else (D, FF))


def ffn_fwd(coords, kept, vec, up, down, last):
    n = kept["m"].shape[0]
    parts = [isinstance(w, tuple) for w in (up, down)]
    ins = [(coords, S), (kept["m"], V), (kept["b"], V), (vec, V)]
    ins += [(w, V) for w, part in zip((up, down), parts) if not part]
    ins += [(p, H) for p in up[0]] if parts[0] else []
    outs = [((n, D), bf16 if last else f32), ((FF, n), bf16), ((n, FF), bf16)]
    outs += [(shape, bf16) for shape, part in zip((WHOLE, WHOLE_ROWS), parts) if part]
    scratch = [V((n, FF), bf16)] + ([SEMS((2, 8))] if parts[0] else [])
    offsets = [w[1] if part else None for w, part in zip((up, down), parts)]
    kernel = functools.partial(ffn_fwd_kernel, offsets, last)
    y, zt, slope, *more = call(kernel, ins, outs, scratch, "ffn_fwd", 4 * n * D * FF, 2 * n * FF)
    up = more[0].reshape(D, FF) if parts[0] else up
    down = more[1].reshape(FF, D) if parts[1] else down
    return y, {"zt": zt, "slope": slope}, up, down


def ffn_bwd(coords, g, kept, vec, up, down, top):
    n = g.shape[0]
    ins = [(coords, S)] + [(a, V) for a in (g, kept["slope"], kept["m"], vec, up, down)]
    outs = [((n, D), bf16), ((n, FF), bf16), ((n, D), f32), ((n, D), bf16), ((VECS, D), f32)]
    out = call(functools.partial(ffn_bwd_kernel, top), ins, outs, [], "ffn_bwd", 4 * n * D * FF, 0)
    return dict(zip(("gb", "gu", "gm", "gmb", "sums"), out, strict=True))


def attn_bwd(coords, gmb, kept, table, weight, groups):
    n = gmb.shape[0]
    ins = [(coords, S)] + [(a, V) for a in (gmb, kept["qt"], kept["kv"], kept["ot"], kept["lse"], table[1], weight)]
    rows = groups[1] * LANES
    scratch = [V((rows, n), bf16), V((PER_GROUP, n, 2 * LANES), bf16), V((2 * LANES, n), bf16)]
    outs = [((3, rows, n), bf16)] + ([((D, n), bf16)] if groups == LATE else [])
    flops = 2 * n * D * rows + 10 * n * n * rows
    kernel = functools.partial(attn_bwd_kernel, groups)
    return call(kernel, ins, outs, scratch, "attn_bwd", flops, HEADS * n * n)


def attn_after(back, kept, vec, weight, last):
    n = back["gm"].shape[0]
    ins = [(a, V) for a in (back["early"], back["late"], back["gm"], kept["x"], vec, weight)]
    outs = [((n, D), bf16 if last else f32), ((VECS, D), f32)]
    return call(attn_after_kernel, ins, outs, [V((n, D), f32)], "attn_after", 6 * n * D * D, 0)


def grads(coords, items, phase):
    arrays, plan, flops, rows = [], [], 0, 0
    for kind, lefts, right, height in items:
        index = list(range(len(arrays), len(arrays) + len(lefts)))
        arrays += [*lefts, right]
        plan.append((kind, index, len(arrays) - 1, rows))
        rows += height
        flops += 2 * arrays[0].shape[1] * D * D * 2
    leads = [(2, 2, 2, 2)] if phase else [(2, 2, 2), (2, 2), (2, 2)]
    outs = [((*lead, rows, D), bf16) for lead in leads]
    kernel = functools.partial(grads_kernel, plan, len(arrays), phase)
    ins = [(coords, S)] + [(a, V) for a in arrays]
    return call(kernel, ins, outs, [V((D, arrays[0].shape[1]), bf16), V((D, D), bf16)], "grads", flops, 0)


def mate(value):
    return lax.ppermute(value, "narrow", [(0, 1), (1, 0)])


def step(link, value):
    masks = ((8, 4, 1, 2)[link], (4, 8, 2, 1)[link])
    pairs = [(2 * w + n, 2 * (w ^ masks[n]) + n) for w in range(16) for n in range(2)]
    return lax.ppermute(value, AXES, pairs)


def relative(values, bits):
    for place_of, bit in enumerate(reversed(bits)):
        flip = 1 << place_of
        values = [jnp.where(bit > 0, values[i ^ flip], values[i]) for i in range(len(values))]
    return values


def add(*terms):
    return functools.reduce(lambda p, q: p + q, [t.astype(f32) for t in terms])


def regroup(parts, bits):
    mine = relative(parts, bits)
    return relative([mine[0]] + [lax.ppermute(mine[k], AXES, [(i, i ^ k) for i in range(32)]) for k in (1, 2, 3)], bits)


def vector_tables(gains, biases):
    gains = gains.astype(f32).reshape(LAYERS, 2, D)
    biases = biases.astype(f32).reshape(LAYERS, 11, D)
    return jnp.concatenate([gains, biases, jnp.zeros((LAYERS, VECS - 13, D), f32)], 1)


NAMES = ("down", "up", "attn")
LOTS = ((("down", 1),), (("up", 1),), (("attn", 1),), (("down", 0), ("up", 0)), (("attn", 0),))


def whole_weight(matrix, by_rows):
    if by_rows:
        cut = jnp.transpose(matrix.reshape(4, 2, 2, 2, PIECE, D), (3, 1, 2, 0, 4, 5))
    else:
        cut = jnp.transpose(matrix.reshape(4, 2, PIECE, 2, 2, D), (4, 1, 3, 0, 2, 5))
    cut = [cut[0], jnp.swapaxes(cut[1], 0, 1)]
    return [cut[kn][kb] for kb in range(2) for kn in range(2)], 0, by_rows


def whole_grad(core, rest, rows, by_rows):
    near = jnp.stack([jnp.stack([rest[2], rest[1]]), rest[0]])
    cut = jnp.stack([jnp.transpose(near, (1, 0, 3, 2, 4, 5)), core])[..., rows, :]
    if by_rows:
        return jnp.transpose(cut, (3, 4, 2, 1, 0, 5, 6)).reshape(FF, D)
    return jnp.transpose(cut, (3, 4, 2, 5, 1, 0, 6)).reshape(D, FF)


def fetch_plain(w_qkv, w_out, w_up, w_down, gains, biases):
    def whole(value, rows):
        return lax.all_gather(value, AXES, axis=0, tiled=True).reshape(rows, -1)

    weights = {}
    for l in range(LAYERS):
        attn = jnp.concatenate([whole(w_qkv[l], D), whole(w_out[l], D)], 1)
        weights["attn", l] = whole_weight(attn, False)
        weights["up", l] = whole_weight(whole(w_up[l], D), False)
        weights["down", l] = whole_weight(whole(w_down[l], FF), True)
    return weights, vector_tables(whole(gains, 1)[0], whole(biases, 1)[0])


class Lot:
    def first(self, core, rest):
        self.core, self.rest = core, rest
        return add(rest[0], core[1]).astype(bf16)

    def second(self, got):
        self.got = got
        return add(self.rest[1], self.core[0, 1], got[1]).astype(bf16)

    def third(self, got):
        total = add(self.rest[2], self.core[0, 0], self.got[0], got)
        self.total = total[0]
        return total[1].astype(bf16)

    def fourth(self, got):
        total = add(self.total, got)
        self.total = total[0]
        return total[1].astype(bf16)

    def last(self, got):
        return add(self.total, got)


def stage(*groups):
    flat, tree = jax.tree.flatten(groups)
    return jax.tree.unflatten(tree, lax.optimization_barrier(flat))


def device_bits():
    wide = lax.axis_index("wide")
    return [(wide >> 3) & 1, (wide >> 2) & 1, (wide >> 1) & 1, wide & 1, lax.axis_index("narrow")]


def coordinates(values):
    return jnp.stack([jnp.asarray(v, jnp.int32) for v in values])


def layer_grads(sums):
    both = jnp.stack(sums)
    return both[:, :2].reshape(-1), both[:, 2:13].reshape(-1)


def gradient_blocks(coords, lot, kept, back, phase):
    items = []
    for name, l in LOTS[lot]:
        if name == "attn":
            items.append((name, [kept[l]["at"], kept[l]["ot"], back[l]["early"], back[l]["late"]], back[l]["flip"], PIECE))
        elif name == "up":
            items.append((name, [kept[l]["bt"]], back[l]["gu"], PIECE))
        else:
            items.append((name, [kept[l]["zt"]], back[l]["gb"], PIECE))
    outs = grads(coords, items, phase)
    return outs[0] if phase else outs


def shares_of(parts, bits):
    rows = D // 32
    cut = jnp.stack(parts)
    whole = jnp.concatenate(regroup([cut[:, s * rows : (s + 1) * rows] for s in range(4)], bits[3:]), 2)
    return [whole[i] for i in range(len(parts))]


def body(tokens, lengths, w_qkv, w_out, w_up, w_down, gains, biases, cotangent):
    args = (tokens, lengths, w_qkv, w_out, w_up, w_down, gains, biases, cotangent)
    if lax.axis_size("wide") == 16 and lax.axis_size("narrow") == 2:
        return staged(*args)
    return plain(*args)


def plain(tokens, lengths, w_qkv, w_out, w_up, w_down, gains, biases, cotangent):
    length = tokens.shape[0] // lengths.shape[0]
    coords = coordinates([0, 0, 0, 0, lengths[0]])
    table = rotary_tables(length)
    weights, vectors = fetch_plain(w_qkv, w_out, w_up, w_down, gains, biases)
    kept, back, wholes, x = [], [{}, {}], [], tokens
    for l in range(LAYERS):
        held, whole = attn_fwd(coords, x, vectors[l], table, [weights[name, l] for name in ("attn", "up", "down")])
        x, more, *_ = ffn_fwd(coords, held, vectors[l], whole[1], whole[2], l == LAYERS - 1)
        kept.append(held | more)
        wholes.append(whole)
    output, grad, sums = x, cotangent, [None] * LAYERS
    for l in reversed(range(LAYERS)):
        last = l == 0
        back[l] = ffn_bwd(coords, grad, kept[l], vectors[l], wholes[l][1], wholes[l][2], not last)
        (back[l]["early"],) = attn_bwd(coords, back[l]["gmb"], kept[l], table, wholes[l][0], EARLY)
        back[l]["late"], back[l]["flip"] = attn_bwd(coords, back[l]["gmb"], kept[l], table, wholes[l][0], LATE)
        grad, more = attn_after(back[l], kept[l], vectors[l], wholes[l][0], last)
        sums[l] = back[l]["sums"] + more
    matrices = {}
    for lot, keys in enumerate(LOTS):
        core, rest = [gradient_blocks(coords, lot, kept, back, phase) for phase in (1, 0)]
        for i, key in enumerate(keys):
            rows = slice(i * PIECE, (i + 1) * PIECE)
            matrices[key] = whole_grad(core, rest, rows, key[0] == "down").astype(f32)
    outs = []
    for name, begin, end in (("attn", 0, 3 * D), ("attn", 3 * D, FF), ("up", 0, FF), ("down", 0, D)):
        cut = jnp.stack([matrices[name, l][:, begin:end].reshape(-1) for l in range(LAYERS)])
        outs.append(lax.psum_scatter(cut, AXES, scatter_dimension=1, tiled=True))
    outs += [lax.psum_scatter(v, AXES, scatter_dimension=0, tiled=True) for v in layer_grads(sums)]
    return (output, grad, *outs)


def turned(value, bits):
    value = value.reshape(2, 2, 2, 2, 2, -1)
    for axis, bit in enumerate(bits):
        value = jnp.where(bit > 0, jnp.flip(value, axis), value)
    cores = [jnp.transpose(value, order) for order in ((4, 2, 3, 1, 0, 5), (4, 3, 2, 0, 1, 5))]
    own = jnp.where(bits[4] > 0, cores[1][0], cores[0][0])
    other = jnp.where(bits[4] > 0, cores[0][1], cores[1][1])
    return jnp.stack([own, other])


def ordered(bit, own, got):
    return jnp.stack([jnp.where(bit > 0, got, own), jnp.where(bit > 0, own, got)])


def staged(tokens, lengths, w_qkv, w_out, w_up, w_down, gains, biases, cotangent):
    length = tokens.shape[0] // lengths.shape[0]
    bits = device_bits()
    coords = coordinates([lax.axis_index("wide") >> 2, *bits[2:], lengths[0]])
    table = rotary_tables(length)
    rows = D // 32
    weights, whole = {}, {}

    z1, z0, y, x, n = bits
    third, fourth = jnp.where(n > 0, y, x), jnp.where(n > 0, x, y)

    def link0(value):
        return ordered(jnp.where(n > 0, z0, z1), value, step(0, value))

    def link1(value):
        return value, step(1, value)

    def by_z(pair):
        own, got = pair
        blocks = []
        for high in range(2):
            for low in range(2):
                core0 = jnp.where(z0 == low, own[high], got[high])
                blocks.append(jnp.where(n > 0, jnp.where(z1 == high, own[low], got[low]), core0))
        return jnp.stack(blocks)

    def link2(value):
        return ordered(third, value, step(2, value))

    def arrived(keys, *pieces):
        offset = 0
        for key, height in keys:
            weights[key] = (list(pieces), offset, key[0] == "down")
            offset += height

    small = jnp.concatenate([gains, biases])
    width = small.shape[0]
    c0 = jnp.concatenate([w_down[0].reshape(PIECE, D), jnp.zeros((16, D), bf16).at[0, :width].set(small)])
    c0, w_qkv, w_out, w_up = stage(c0, w_qkv, w_out, w_up)
    t0 = link0(c0)
    flat = []
    for l in range(LAYERS):
        flat.append(jnp.concatenate([w_qkv[l].reshape(rows, 3 * D), w_out[l].reshape(rows, D)], 1))
        flat.append(w_up[l].reshape(rows, FF))
    flat = jnp.stack(flat)
    parts = [flat[:, :, s * D : (s + 1) * D] for s in range(4)]
    t0, parts = stage(t0, parts)
    u0 = link1(t0)
    c1, up0, attn1, up1 = jnp.concatenate(regroup(parts, bits[3:]), 1)
    c2, c3 = jnp.concatenate([up0, attn1]), jnp.concatenate([w_down[1].reshape(PIECE, D), up1])
    zz0, c1, c2, c3 = stage(by_z(u0), c1, c2, c3)
    near0, t12 = stage(link2(zz0), link0(jnp.concatenate([c1, c2])))
    t1, t2 = t12[:, :PIECE], t12[:, PIECE:]
    far0, mate0, u1 = step(3, near0), mate(near0), link1(t1)
    far0, mate0, zz1, t2 = stage(far0, mate0, by_z(u1), t2)
    near1, far_mate0, u2, t3 = link2(zz1), mate(far0), link1(t2), link0(c3)
    near1, far_mate0, zz2, t3 = stage(near1, far_mate0, by_z(u2), t3)
    arrived(((("down", 0), PIECE),), near0, mate0, far0, far_mate0)
    far1, mate1, near2, u3 = step(3, near1), mate(near1), link2(zz2), link1(t3)
    whole["down", 0] = assemble(coords, weights["down", 0])
    own, other = [], []
    for first, second, to in ((near0, far0, own), (mate0, far_mate0, other)):
        turn = n if to is own else 1 - n
        both = ordered(jnp.where(turn > 0, x, y), first[:, :, PIECE, :width], second[:, :, PIECE, :width])
        to.append(jnp.where(turn > 0, jnp.transpose(both, (2, 1, 0, 3)), jnp.transpose(both, (2, 0, 1, 3))))
    both = ordered(n, own[0], other[0])
    both = jnp.transpose(both, (1, 2, 3, 0, 4)).reshape(32, width)
    vectors = vector_tables(both[:, : gains.shape[0]].reshape(-1), both[:, gains.shape[0] :].reshape(-1))
    far1, mate1, near2, zz3, vectors, whole = stage(far1, mate1, near2, by_z(u3), vectors, whole)
    far_mate1, near2, zz3 = stage(mate(far1), near2, zz3)
    arrived(((("attn", 0), PIECE),), near1, mate1, far1, far_mate1)
    kept, back = [None, None], [None, None]
    far2, mate2 = step(3, near2), mate(near2)
    kept[0], got = attn_fwd(coords, tokens, vectors[0], table, [weights["attn", 0]])
    whole["attn", 0] = got[0]
    far2, mate2, kept[0] = stage(far2, mate2, kept[0])
    far_mate2, kept[0], zz3 = stage(mate(far2), kept[0], zz3)
    arrived(((("up", 0), PIECE), (("attn", 1), PIECE)), near2, mate2, far2, far_mate2)
    got3 = step(2, zz3)
    h, more, whole["up", 0], _ = ffn_fwd(coords, kept[0], vectors[0], weights["up", 0], whole["down", 0], False)
    kept[0] |= more
    got3, h = stage(got3, h)
    near3, h = stage(ordered(third, zz3, got3), h)
    far3, mate3 = step(3, near3), mate(near3)
    kept[1], got = attn_fwd(coords, h, vectors[1], table, [weights["attn", 1]])
    whole["attn", 1] = got[0]
    far3, mate3, kept[1] = stage(far3, mate3, kept[1])
    arrived(((("down", 1), PIECE), (("up", 1), PIECE)), near3, mate3, far3, mate(far3))
    output, more, whole["up", 1], whole["down", 1] = ffn_fwd(
        coords, kept[1], vectors[1], weights["up", 1], weights["down", 1], True
    )
    kept[1] |= more

    d1, u1, a1, du0, a0, extra = [Lot() for _ in range(6)]

    def blocks(lot, phase):
        return gradient_blocks(coords, lot, kept, back, phase)

    live = jnp.arange(length, dtype=jnp.int32)[:, None] < lengths[0]
    back[1] = {"gb": jnp.where(live, cotangent, jnp.zeros((), bf16))}
    core, back[1] = stage(blocks(0, 1), back[1])
    first, cotangent = stage(d1.first(mate(core), blocks(0, 0)), cotangent)

    got_d1 = step(3, first)
    back[1] |= ffn_bwd(coords, cotangent, kept[1], vectors[1], whole["up", 1], whole["down", 1], True)
    got_d1, core, back[1] = stage(got_d1, blocks(1, 1), back[1])
    second, core, back[1] = stage(d1.second(got_d1), core, back[1])

    got_d1, core, rest = stage(step(2, second), mate(core), blocks(1, 0))
    first, third, back[1] = stage(u1.first(core, rest), d1.third(got_d1), back[1])

    got_u1, got_d1 = step(3, first), step(1, third)
    (back[1]["early"],) = attn_bwd(coords, back[1]["gmb"], kept[1], table, whole["attn", 1], EARLY)
    got_u1, got_d1, back[1] = stage(got_u1, got_d1, back[1])
    second, fourth, back[1] = stage(u1.second(got_u1), d1.fourth(got_d1), back[1])

    got_u1, got_d1 = step(2, second), step(0, fourth)
    back[1]["late"], back[1]["flip"] = attn_bwd(coords, back[1]["gmb"], kept[1], table, whole["attn", 1], LATE)
    got_u1, got_d1, core, back[1] = stage(got_u1, got_d1, blocks(2, 1), back[1])
    third, core, back[1] = stage(u1.third(got_u1), core, back[1])

    got_u1, core, rest = stage(step(1, third), mate(core), blocks(2, 0))
    first, fourth, back[1] = stage(a1.first(core, rest), u1.fourth(got_u1), back[1])

    got_a1, got_u1 = step(3, first), step(0, fourth)
    grad, more = attn_after(back[1], kept[1], vectors[1], whole["attn", 1], False)
    sums = [None, back[1]["sums"] + more]
    back[0] = ffn_bwd(coords, grad, kept[0], vectors[0], whole["up", 0], whole["down", 0], False)
    got_a1, got_u1, core, back[0] = stage(got_a1, got_u1, blocks(3, 1), back[0])
    second, core, back[0] = stage(a1.second(got_a1), core, back[0])

    got_a1, core, rest = stage(step(2, second), mate(core), blocks(3, 0))
    first, third, back[0] = stage(du0.first(core, rest), a1.third(got_a1), back[0])

    got_du0, got_a1 = step(3, first), step(1, third)
    (back[0]["early"],) = attn_bwd(coords, back[0]["gmb"], kept[0], table, whole["attn", 0], EARLY)
    back[0]["late"], back[0]["flip"] = attn_bwd(coords, back[0]["gmb"], kept[0], table, whole["attn", 0], LATE)
    got_du0, got_a1, back[0] = stage(got_du0, got_a1, back[0])
    second, fourth, back[0] = stage(du0.second(got_du0), a1.fourth(got_a1), back[0])

    got_du0, got_a1 = step(2, second), step(0, fourth)
    core = blocks(4, 1)
    grad, more = attn_after(back[0], kept[0], vectors[0], whole["attn", 0], True)
    sums[0] = back[0]["sums"] + more
    got_du0, got_a1, core, grad, sums, back[0] = stage(got_du0, got_a1, core, grad, sums, back[0])
    third, core, back[0] = stage(du0.third(got_du0), core, back[0])

    got_du0 = step(1, third)
    core, rest = stage(mate(core), blocks(4, 0))
    first, sums = stage(a0.first(core, rest), sums)

    got_a0 = step(3, first)
    small = turned(jnp.concatenate([v.reshape(32, -1) for v in layer_grads(sums)], 1), bits)
    first = extra.first(mate(small[1]), [small[0, 1], small[0, 0, 1], small[0, 0, 0]])
    got_a0, got_du0, first, got_d1, got_u1, got_a1, grad = stage(got_a0, got_du0, first, got_d1, got_u1, got_a1, grad)
    second, first, fourth = stage(a0.second(got_a0), first, du0.fourth(got_du0))

    got_a0, got_x, got_du0 = step(2, second), step(3, first), step(0, fourth)
    shares = [u1.last(got_u1), a1.last(got_a1)]
    got_a0, got_x, got_du0, shares = stage(got_a0, got_x, got_du0, shares)
    third, second, got_du0 = stage(a0.third(got_a0), extra.second(got_x), got_du0)

    got_a0, got_x = step(1, third), step(2, second)
    done = du0.last(got_du0)
    downs = jnp.stack([done[:PIECE].reshape(-1), d1.last(got_d1).reshape(-1)])
    up1, attn1, up0 = shares_of([*shares, done[PIECE:]], bits)
    got_a0, got_x, up1, attn1, up0, downs = stage(got_a0, got_x, up1, attn1, up0, downs)
    fourth, third = stage(a0.fourth(got_a0), extra.third(got_x))

    got_a0, got_x = step(0, fourth), step(1, third)
    ups = jnp.stack([up0.reshape(-1), up1.reshape(-1)])
    got_a0, got_x, ups = stage(got_a0, got_x, ups)
    (attn0,) = shares_of([a0.last(got_a0)], bits)
    mine = extra.last(step(0, extra.fourth(got_x)))
    return (
        output,
        grad,
        jnp.stack([v[:, : 3 * D].reshape(-1) for v in (attn0, attn1)]),
        jnp.stack([v[:, 3 * D :].reshape(-1) for v in (attn0, attn1)]),
        ups,
        downs,
        mine[: gains.shape[0]],
        mine[gains.shape[0] :],
    )


def solution(mesh):
    both, flat, rows = P(AXES), P(None, AXES), P(AXES, None)
    return jax.shard_map(
        body,
        mesh=mesh,
        in_specs=(rows, both, flat, flat, flat, flat, both, both, rows),
        out_specs=(rows, rows, flat, flat, flat, flat, both, both),
        check_vma=False,
    )
```

```python
import functools

import jax
import jax.numpy as jnp
import numpy as np
from jax import lax
from jax.experimental import pallas as pl
from jax.experimental.pallas import tpu as pltpu
from jax.sharding import PartitionSpec as P

D = 640
HEADS = 20
HEAD_DIM = 32
FF = 2560
LAYERS = 2
EPSILON = 1e-05
MASKED = -1e9
LANES = 128
GROUPS = D // LANES
PER_GROUP = LANES // HEAD_DIM
BLOCKS = FF // D
EARLY, LATE = (0, 3), (3, 2)
PIECE = 80
VECS = 16
AXES = ("wide", "narrow")
WHOLE, WHOLE_ROWS = (4, 2, PIECE, FF), (4, 2, 2, 2, PIECE, D)
SLACK = 8 * 1024 * 1024
f32, bf16 = jnp.float32, jnp.bfloat16

GAIN_A, GAIN_F, SHIFT_A, BIAS_QKV, BIAS_OUT, SHIFT_F, BIAS_UP, BIAS_DOWN = 0, 1, 2, 3, 6, 7, 8, 12


def rotary_tables(length):
    half = HEAD_DIM // 2
    inverse = 1.0 / 10000.0 ** (np.arange(half) * (2.0 / HEAD_DIM))
    angles = np.arange(length)[:, None] * inverse[None, :]
    cos, sine = np.cos(angles), np.sin(angles)
    none = np.zeros_like(sine)
    ahead = np.tile(np.concatenate([-sine, none], 1), (1, PER_GROUP))
    behind = np.tile(np.concatenate([none, sine], 1), (1, PER_GROUP))
    wide = np.stack([np.tile(cos, (1, 2 * PER_GROUP)), ahead, behind]).astype(np.float32)
    return jnp.asarray(wide), jnp.asarray(np.stack([cos.T, sine.T]).astype(np.float32))


def dot(left, right):
    return jnp.dot(left, right, preferred_element_type=f32)


def dot_nt(left, right):
    return lax.dot_general(left, right, (((1,), (1,)), ((), ())), preferred_element_type=f32)


def dot_tn(left, right):
    return lax.dot_general(left, right, (((0,), (0,)), ((), ())), preferred_element_type=f32)


def rotated(value, table):
    half = HEAD_DIM // 2
    return value * table[0] + pltpu.roll(value, LANES - half, 1) * table[1] + pltpu.roll(value, half, 1) * table[2]


def rotated_back(value, table):
    half = HEAD_DIM // 2
    first, second = value[:half], value[half:]
    return jnp.concatenate([first * table[0] + second * table[1], second * table[0] - first * table[1]], 0)


def unit_of(value):
    centered = value - jnp.mean(value, -1, keepdims=True)
    inverse = lax.rsqrt(jnp.mean(centered * centered, -1, keepdims=True) + EPSILON)
    return centered * inverse, inverse


def norm_back(grad, unit, inverse, gain):
    scaled = grad * gain
    return inverse * (scaled - jnp.mean(scaled, -1, keepdims=True) - unit * jnp.mean(scaled * unit, -1, keepdims=True))


def column_sum(value):
    return jnp.sum(value, 0, keepdims=True)


def gelu_parts(value):
    scaled = jnp.abs(value) * 0.7071067811865476
    t = 1.0 / (1.0 + 0.3275911 * scaled)
    bell = jnp.exp(-scaled * scaled)
    series = t * (0.127414796 + t * (-0.142248368 + t * (0.7107068705 + t * (-0.7265760135 + t * 0.5307027145))))
    tail = series * bell
    return jnp.where(value >= 0.0, 1.0 - tail, tail), bell * 0.3989422804014327


def row_loop(length, step, body):
    def run(i, carry):
        body(pl.ds(pl.multiple_of(i * step, step), step), i)
        return carry

    lax.fori_loop(0, length // step, run, 0)


def owner_of(coords, kn, kb, ka, k2, k1):
    n = coords[3] ^ kn
    z = coords[0] ^ (2 * k1 + k2 + n * (k2 - k1))
    return z, coords[1] ^ (kb + n * (ka - kb)), coords[2] ^ (ka + n * (kb - ka)), n


PLACES = [(ka, k2, k1) for ka in range(2) for k2 in range(2) for k1 in range(2)]


class Assembly:
    def __init__(self, coords, by_rows, pieces, offset, whole, sems):
        self.by_rows, self.whole, self.sems = by_rows, whole, sems
        self.any = pieces[0].at[0, :, pl.ds(offset, PIECE)]
        for kb in range(2):
            for kn in range(2):
                n = coords[3] ^ kn
                b = (coords[1] + n * (coords[2] - coords[1])) ^ kb
                for a in range(2):
                    target = self.target(a + n * (b - a), b + n * (a - b), n)
                    pltpu.make_async_copy(pieces[2 * kb + kn].at[a, :, pl.ds(offset, PIECE)], *target).start()

    def target(self, x, y, n):
        to = (y, x, n) if self.by_rows else (y, slice(None), pl.ds(pl.multiple_of((2 * x + n) * D, D), D))
        return self.whole.at[(slice(None), *to)], self.sems.at[4 * x + 2 * n + y]

    def wait(self, quarters=(0, 1, 2, 3)):
        for quarter in quarters:
            for y in range(2):
                pltpu.make_async_copy(self.any, *self.target(quarter // 2, y, quarter % 2)).wait()


def head_masks():
    lane = lax.broadcasted_iota(jnp.int32, (1, LANES), 1)
    return [(lane // HEAD_DIM == head).astype(f32).astype(bf16) for head in range(PER_GROUP)]


def masked_tail(length, live):
    row = lax.broadcasted_iota(jnp.int32, (length, LANES), 0)
    lane = lax.broadcasted_iota(jnp.int32, (length, LANES), 1)
    keys = jnp.where((lane == 0) & (row >= live), MASKED, 0.0).astype(bf16)
    row = lax.broadcasted_iota(jnp.int32, (LANES, length), 0)
    return keys, jnp.where(row == 0, 1.0, 0.0).astype(bf16)


def attn_fwd_kernel(plan, coords, x_ref, vec_ref, table_ref, *refs):
    count = len(plan)
    pieces, refs = refs[: 4 * count], refs[4 * count :]
    at_ref, qt_ref, kv_ref, ot_ref, lse_ref, m_ref, b_ref, bt_ref, *refs = refs
    wholes, refs = refs[:count], refs[count:]
    a_ref, q_ref, key_ref, query_ref, sems = refs
    length = x_ref.shape[0]
    jobs = [
        Assembly(coords, by_rows, pieces[4 * i : 4 * i + 4], offset, wholes[i], sems.at[i])
        for i, (offset, by_rows) in enumerate(plan)
    ]
    w_ref = wholes[0]

    def norm(rows, _):
        unit, _ = unit_of(x_ref[rows, :].astype(f32))
        a_ref[rows, :] = (unit * vec_ref[GAIN_A : GAIN_A + 1, :] + vec_ref[SHIFT_A : SHIFT_A + 1, :]).astype(bf16)

    row_loop(length, 128, norm)
    normed = a_ref[...]
    at_ref[...] = normed.T
    for part in range(3):
        jobs[0].wait([part])
        out = dot(normed, w_ref[:, :, :, part * D : (part + 1) * D].reshape(D, D)) + vec_ref[BIAS_QKV + part : BIAS_QKV + part + 1, :]
        if part == 0:
            out = out * HEAD_DIM**-0.5
        for group in range(GROUPS):
            lanes = slice(group * LANES, (group + 1) * LANES)
            piece = out[:, lanes]
            if part < 2:
                piece = rotated(piece, table_ref)
            if part == 0:
                qt_ref[lanes, :] = piece.astype(bf16).T
            else:
                kv_ref[:, (part - 1) * D + group * LANES : (part - 1) * D + (group + 1) * LANES] = piece.astype(bf16)
    masks = head_masks()
    tail, query_ref[LANES:, :] = masked_tail(length, coords[4])
    for head in range(PER_GROUP):
        key_ref[head, :, LANES:] = tail
    ones = jnp.ones((16, length), bf16)

    def group_step(group, carry):
        rows = pl.ds(pl.multiple_of(group * LANES, LANES), LANES)
        query_ref[:LANES, :] = qt_ref[rows, :]
        values = kv_ref[:, pl.ds(pl.multiple_of(D + group * LANES, LANES), LANES)].T
        for head in range(PER_GROUP):
            key_ref[head, :, :LANES] = kv_ref[:, rows] * masks[head]
        every = dot(key_ref[...].reshape(PER_GROUP * length, 2 * LANES), query_ref[...])
        for head in range(PER_GROUP):
            scores = every[head * length : (head + 1) * length]
            top = jnp.max(scores, 0, keepdims=True)
            probs = jnp.exp(scores - top).astype(bf16)
            wide = jnp.concatenate([values[head * HEAD_DIM : (head + 1) * HEAD_DIM], ones], 0)
            out = dot(wide, probs)
            total = out[HEAD_DIM : HEAD_DIM + 1]
            to = pl.ds(pl.multiple_of(group * LANES + head * HEAD_DIM, HEAD_DIM), HEAD_DIM)
            ot_ref[to, :] = (out[:HEAD_DIM] / total).astype(bf16)
            lse_ref[pl.ds(group * PER_GROUP + head, 1), :] = top + jnp.log(total)
        return carry

    for group in range(GROUPS):
        group_step(group, 0)
    jobs[0].wait([3])
    q_ref[...] = ot_ref[...].T
    m_ref[...] = x_ref[...].astype(f32) + (dot(q_ref[...], w_ref[:, :, :, 3 * D :].reshape(D, D)) + vec_ref[BIAS_OUT : BIAS_OUT + 1, :])

    def after(rows, _):
        unit, _ = unit_of(m_ref[rows, :])
        b_ref[rows, :] = (unit * vec_ref[GAIN_F : GAIN_F + 1, :] + vec_ref[SHIFT_F : SHIFT_F + 1, :]).astype(bf16)

    row_loop(length, 128, after)
    bt_ref[...] = b_ref[...].T
    for job in jobs[1:]:
        job.wait()


def assemble_kernel(offset, by_rows, coords, *refs):
    Assembly(coords, by_rows, refs[:4], offset, refs[4], refs[5]).wait()


def ffn_fwd_kernel(offsets, last, coords, m_ref, b_ref, vec_ref, *refs):
    offset, offset_down = offsets
    if offset is None:
        up_ref, down_ref, y_ref, zt_ref, slope_ref, *rest = refs
    elif offset_down is None:
        down_ref, *pieces, y_ref, zt_ref, slope_ref, up_ref = refs[:9]
        rest = refs[9:]
    else:
        *pieces, y_ref, zt_ref, slope_ref, up_ref, down_ref = refs[:9]
        rest = refs[9:]
    z_ref = y_ref if last else rest[0]
    sems = rest[-1] if rest else None
    if offset is not None:
        job = Assembly(coords, False, pieces, offset, up_ref, sems.at[0])
    if offset_down is not None:
        job_down = Assembly(coords, True, pieces, offset_down, down_ref, sems.at[1])
    normed = b_ref[...]
    for block in range(BLOCKS):
        if offset is not None:
            job.wait([block])
        columns = slice(block * D, (block + 1) * D)
        part = up_ref[:, columns] if offset is None else up_ref[:, :, :, columns].reshape(D, D)
        pre = dot(normed, part) + vec_ref[BIAS_UP + block : BIAS_UP + block + 1, :]
        cdf, bell = gelu_parts(pre)
        z_ref[:, columns] = (pre * cdf).astype(bf16)
        slope_ref[:, columns] = (cdf + pre * bell).astype(bf16)
        zt_ref[columns, :] = z_ref[:, columns].T
    if offset_down is not None:
        job_down.wait()
    if not last:
        y_ref[...] = m_ref[...] + (dot(z_ref[...], down_ref[...].reshape(FF, D)) + vec_ref[BIAS_DOWN : BIAS_DOWN + 1, :])


def ffn_out_kernel(coords, m_ref, z_ref, vec_ref, down_ref, y_ref):
    out = m_ref[...] + (dot(z_ref[...], down_ref[...]) + vec_ref[BIAS_DOWN : BIAS_DOWN + 1, :])
    row = lax.broadcasted_iota(jnp.int32, (m_ref.shape[0], 1), 0)
    y_ref[...] = jnp.where(row < coords[4], out, 0.0).astype(bf16)


def ffn_bwd_kernel(top, coords, g_ref, slope_ref, m_ref, vec_ref, up_ref, down_ref, *refs):
    gb_ref, gu_ref, gm_ref, gmb_ref, sums_ref = refs
    length = m_ref.shape[0]
    sums_ref[...] = jnp.zeros_like(sums_ref)

    def add(row, value):
        sums_ref[row : row + 1, :] += column_sum(value)

    grad = g_ref[...].astype(f32)
    if top:
        row = lax.broadcasted_iota(jnp.int32, (length, 1), 0)
        grad = jnp.where(row < coords[4], grad, 0.0)
    low = grad.astype(bf16)
    gb_ref[...] = low
    add(BIAS_DOWN, low.astype(f32))
    for block in range(BLOCKS):
        columns = slice(block * D, (block + 1) * D)
        part = (dot_nt(low, down_ref[columns, :]) * slope_ref[:, columns].astype(f32)).astype(bf16)
        gu_ref[:, columns] = part
        add(BIAS_UP + block, part.astype(f32))
    gm_ref[...] = dot_nt(gu_ref[...], up_ref[...])

    def after(rows, i):
        normed_grad = gm_ref[rows, :]
        unit, inverse = unit_of(m_ref[rows, :])
        add(GAIN_F, normed_grad * unit)
        add(SHIFT_F, normed_grad)
        grad = g_ref[rows, :].astype(f32)
        if top:
            row = lax.broadcasted_iota(jnp.int32, (128, 1), 0) + i * 128
            grad = jnp.where(row < coords[4], grad, 0.0)
        middle = grad + norm_back(normed_grad, unit, inverse, vec_ref[GAIN_F : GAIN_F + 1, :])
        gm_ref[rows, :] = middle
        low = middle.astype(bf16)
        gmb_ref[rows, :] = low
        add(BIAS_OUT, low.astype(f32))

    row_loop(length, 128, after)


def attn_bwd_kernel(groups, coords, gmb_ref, qt_ref, kv_ref, ot_ref, lse_ref, table_ref, w_ref, *refs):
    start, count = groups
    gp_ref, *flip_ref, go_ref, key_ref, query_ref = refs
    length = gmb_ref.shape[0]
    low = gmb_ref[...]
    if flip_ref:
        flip_ref[0][...] = low.T
    go_ref[...] = dot_nt(w_ref[start * LANES : (start + count) * LANES, 3 * D :], low).astype(bf16)
    masks = head_masks()
    tail, query_ref[LANES:, :] = masked_tail(length, coords[4])
    for head in range(PER_GROUP):
        key_ref[head, :, LANES:] = tail

    def group_step(i, carry):
        group = i + start
        rows = pl.ds(pl.multiple_of(group * LANES, LANES), LANES)
        query, grad = qt_ref[rows, :], go_ref[pl.ds(pl.multiple_of(i * LANES, LANES), LANES), :]
        query_ref[:LANES, :] = query
        keys = kv_ref[:, rows]
        values = kv_ref[:, pl.ds(pl.multiple_of(D + group * LANES, LANES), LANES)]
        flipped = keys.T
        products = grad.astype(f32) * ot_ref[rows, :].astype(f32)
        for head in range(PER_GROUP):
            key_ref[head, :, :LANES] = keys * masks[head]
        for head in range(PER_GROUP):
            part = slice(head * HEAD_DIM, (head + 1) * HEAD_DIM)
            delta = column_sum(products[part])
            probs = jnp.exp(dot(key_ref[head], query_ref[...]) - lse_ref[pl.ds(group * PER_GROUP + head, 1), :])
            scores = (probs * (dot(values * masks[head], grad) - delta)).astype(bf16)
            dv = dot_nt(grad[part], probs.astype(bf16))
            dk = dot_nt(query[part], scores)
            dq = dot(flipped[part], scores)
            to = pl.ds(pl.multiple_of(i * LANES + head * HEAD_DIM, HEAD_DIM), HEAD_DIM)
            dq = rotated_back(dq.astype(bf16).astype(f32), table_ref) * HEAD_DIM**-0.5
            dk = rotated_back(dk.astype(bf16).astype(f32), table_ref)
            for part, value in enumerate((dq, dk, dv)):
                gp_ref[part, to, :] = value.astype(bf16)
        return carry

    lax.fori_loop(0, count, group_step, 0)


def attn_after_kernel(early_ref, late_ref, gm_ref, x_ref, vec_ref, w_ref, *refs):
    gx_ref, sums_ref, ga_ref = refs
    length = x_ref.shape[0]
    sums_ref[...] = jnp.zeros_like(sums_ref)

    def add(row, value):
        sums_ref[row : row + 1, :] += column_sum(value)

    ones = jnp.ones((16, length), bf16)
    total = 0.0
    for part in range(3):
        for ref, (start, count) in ((early_ref, EARLY), (late_ref, LATE)):
            columns = slice(start * LANES, (start + count) * LANES)
            sums_ref[BIAS_QKV + part : BIAS_QKV + part + 1, columns] = dot_nt(ones, ref[part])[:1]
            total = total + dot(w_ref[:, part * D + start * LANES : part * D + (start + count) * LANES], ref[part])
    ga_ref[...] = total.T

    def after(rows, _):
        normed_grad = ga_ref[rows, :]
        unit, inverse = unit_of(x_ref[rows, :].astype(f32))
        add(GAIN_A, normed_grad * unit)
        add(SHIFT_A, normed_grad)
        out = gm_ref[rows, :] + norm_back(normed_grad, unit, inverse, vec_ref[GAIN_A : GAIN_A + 1, :])
        gx_ref[rows, :] = out.astype(gx_ref.dtype)

    row_loop(length, 128, after)


def grads_kernel(items, inputs, phase, coords, *refs):
    ins, outs, (left_ref, whole_ref) = refs[:inputs], refs[inputs:-2], refs[-2:]

    def put(value, kb, ka, k2, k1, to):
        to = slice(to, to + value.shape[0])
        if phase:
            outs[0][kb, ka, k2, k1, to] = value
        elif kb:
            outs[0][ka, k2, k1, to] = value
        elif ka:
            outs[1][k2, k1, to] = value
        else:
            outs[2][k2, k1, to] = value

    for kind, lefts, right, to in items:
        if kind == "down":
            for kb in range(2):
                for place, (ka, k2, k1) in enumerate(PLACES):
                    z, y, x, n = owner_of(coords, phase, kb, ka, k2, k1)
                    start = pl.multiple_of((8 * z + 4 * y + 2 * x + n) * PIECE, PIECE)
                    left_ref[place * PIECE : (place + 1) * PIECE, :] = ins[lefts[0]][pl.ds(start, PIECE), :]
                whole = dot(left_ref[...], ins[right][...]).astype(bf16)
                for place, (ka, k2, k1) in enumerate(PLACES):
                    put(whole[place * PIECE : (place + 1) * PIECE], kb, ka, k2, k1, to)
        else:
            for kx in range(2):
                quarter = 2 * (coords[2] ^ kx) + (coords[3] ^ phase)
                n = coords[3] ^ phase
                for ky in range(2):
                    for kz in range(4):
                        k2, k1 = kz // 2, kz % 2
                        z = coords[0] ^ (2 * k1 + k2 + n * (k2 - k1))
                        start = pl.multiple_of((2 * z + (coords[1] ^ ky)) * PIECE, PIECE)
                        to_row = (4 * ky + kz) * PIECE
                        if kind == "up":
                            part = ins[lefts[0]][pl.ds(start, PIECE), :]
                        else:
                            part = jnp.where(quarter == 3, ins[lefts[1]][pl.ds(start, PIECE), :], ins[lefts[0]][pl.ds(start, PIECE), :])
                        left_ref[to_row : to_row + PIECE, :] = part
                if kind == "attn":

                    @pl.when(quarter == 3)
                    def _(right=right):
                        whole_ref[...] = dot_nt(left_ref[...], ins[right][...]).astype(bf16)

                    @pl.when(quarter < 3)
                    def _(right=right, quarter=quarter):
                        part = jnp.minimum(quarter, 2)
                        for i, (start, count) in ((2, EARLY), (1, LATE)):
                            columns = slice(start * LANES, (start + count) * LANES)
                            whole_ref[:, columns] = dot_nt(left_ref[...], ins[right - i][part]).astype(bf16)

                else:
                    columns = pl.ds(pl.multiple_of(quarter * D, D), D)
                    whole_ref[...] = dot(left_ref[...], ins[right][:, columns]).astype(bf16)

                def write(swapped, kx=kx, to=to):
                    for ky in range(2):
                        for kz in range(4):
                            start = (4 * ky + kz) * PIECE
                            ka, kb = (ky, kx) if swapped else (kx, ky)
                            put(whole_ref[start : start + PIECE, :], kb, ka, kz // 2, kz % 2, to)

                pl.when(n == 0)(functools.partial(write, False))
                pl.when(n == 1)(functools.partial(write, True))


def call(kernel, ins, outs, scratch, name, flops, exps=0):
    moved = sum(a.size * a.dtype.itemsize for a, _ in ins) + sum(int(np.prod(s)) * jnp.dtype(t).itemsize for s, t in outs)
    limit = SLACK + sum(int(np.prod(t.shape)) * t.dtype.itemsize for t in scratch if t.memory_space == V)
    return pl.pallas_call(
        kernel,
        out_shape=[jax.ShapeDtypeStruct(s, t) for s, t in outs],
        in_specs=[pl.BlockSpec(memory_space=space) for _, space in ins],
        out_specs=[pl.BlockSpec(memory_space=pltpu.VMEM)] * len(outs),
        scratch_shapes=scratch,
        compiler_params=pltpu.CompilerParams(vmem_limit_bytes=limit),
        cost_estimate=pl.CostEstimate(flops=int(flops), bytes_accessed=int(moved), transcendentals=int(exps)),
        name=name,
    )(*[a for a, _ in ins])


V, S, H = pltpu.VMEM, pltpu.SMEM, pl.ANY
SEMS = pltpu.SemaphoreType.DMA


def attn_fwd(coords, x, vec, table, weights):
    n = x.shape[0]
    ins = [(coords, S), (x, V), (vec, V), (table[0], V)] + [(p, H) for w in weights for p in w[0]]
    outs = [((D, n), bf16), ((D, n), bf16), ((n, 2 * D), bf16), ((D, n), bf16), ((24, n), f32)]
    outs += [((n, D), f32), ((n, D), bf16), ((D, n), bf16)]
    outs += [(WHOLE_ROWS if w[2] else WHOLE, bf16) for w in weights]
    scratch = [V((n, D), bf16), V((n, D), bf16), V((PER_GROUP, n, 2 * LANES), bf16), V((2 * LANES, n), bf16)]
    scratch.append(SEMS((len(weights), 8)))
    kernel = functools.partial(attn_fwd_kernel, [w[1:] for w in weights])
    out = call(kernel, ins, outs, scratch, "attn_fwd", 2 * n * D * FF + 4 * n * n * D, HEADS * n * n)
    return dict(zip(("at", "qt", "kv", "ot", "lse", "m", "b", "bt"), out[:8], strict=True)) | {"x": x}, [w.reshape((FF, D) if w.ndim == 6 else (D, FF)) for w in out[8:]]


def assemble(coords, weight):
    pieces, offset, by_rows = weight
    outs = [(WHOLE_ROWS if by_rows else WHOLE, bf16)]
    ins = [(coords, S)] + [(p, H) for p in pieces]
    out = call(functools.partial(assemble_kernel, offset, by_rows), ins, outs, [SEMS((8,))], "assemble", 0)[0]
    return out.reshape((FF, D) if by_rows else (D, FF))


def ffn_fwd(coords, kept, vec, up, down, last):
    n = kept["m"].shape[0]
    parts = [isinstance(w, tuple) for w in (up, down)]
    ins = [(coords, S), (kept["m"], V), (kept["b"], V), (vec, V)]
    ins += [(w, V) for w, part in zip((up, down), parts) if not part]
    ins += [(p, H) for p in up[0]] if parts[0] else []
    outs = [((n, FF), bf16) if last else ((n, D), f32), ((FF, n), bf16), ((n, FF), bf16)]
    outs += [(shape, bf16) for shape, part in zip((WHOLE, WHOLE_ROWS), parts) if part]
    scratch = ([] if last else [V((n, FF), bf16)]) + ([SEMS((2, 8))] if parts[0] else [])
    offsets = [w[1] if part else None for w, part in zip((up, down), parts)]
    kernel = functools.partial(ffn_fwd_kernel, offsets, last)
    y, zt, slope, *more = call(kernel, ins, outs, scratch, "ffn_fwd", 4 * n * D * FF, 2 * n * FF)
    up = more[0].reshape(D, FF) if parts[0] else up
    down = more[1].reshape(FF, D) if parts[1] else down
    return y, {"zt": zt, "slope": slope}, up, down


def ffn_out(coords, kept, hidden, vec, down):
    ins = [(coords, S)] + [(a, V) for a in (kept["m"], hidden, vec, down)]
    return call(ffn_out_kernel, ins, [(kept["m"].shape, bf16)], [], "ffn_out", 2 * hidden.size * D)[0]


def ffn_bwd(coords, g, kept, vec, up, down, top):
    n = g.shape[0]
    ins = [(coords, S)] + [(a, V) for a in (g, kept["slope"], kept["m"], vec, up, down)]
    outs = [((n, D), bf16), ((n, FF), bf16), ((n, D), f32), ((n, D), bf16), ((VECS, D), f32)]
    out = call(functools.partial(ffn_bwd_kernel, top), ins, outs, [], "ffn_bwd", 4 * n * D * FF, 0)
    return dict(zip(("gb", "gu", "gm", "gmb", "sums"), out, strict=True))


def attn_bwd(coords, gmb, kept, table, weight, groups):
    n = gmb.shape[0]
    ins = [(coords, S)] + [(a, V) for a in (gmb, kept["qt"], kept["kv"], kept["ot"], kept["lse"], table[1], weight)]
    rows = groups[1] * LANES
    scratch = [V((rows, n), bf16), V((PER_GROUP, n, 2 * LANES), bf16), V((2 * LANES, n), bf16)]
    outs = [((3, rows, n), bf16)] + ([((D, n), bf16)] if groups == LATE else [])
    flops = 2 * n * D * rows + 10 * n * n * rows
    kernel = functools.partial(attn_bwd_kernel, groups)
    return call(kernel, ins, outs, scratch, "attn_bwd", flops, HEADS * n * n)


def attn_after(back, kept, vec, weight, last):
    n = back["gm"].shape[0]
    ins = [(a, V) for a in (back["early"], back["late"], back["gm"], kept["x"], vec, weight)]
    outs = [((n, D), bf16 if last else f32), ((VECS, D), f32)]
    return call(attn_after_kernel, ins, outs, [V((n, D), f32)], "attn_after", 6 * n * D * D, 0)


def grads(coords, items, phase):
    arrays, plan, flops, rows = [], [], 0, 0
    for kind, lefts, right, height in items:
        index = list(range(len(arrays), len(arrays) + len(lefts)))
        arrays += [*lefts, right]
        plan.append((kind, index, len(arrays) - 1, rows))
        rows += height
        flops += 2 * arrays[0].shape[1] * D * D * 2
    leads = [(2, 2, 2, 2)] if phase else [(2, 2, 2), (2, 2), (2, 2)]
    outs = [((*lead, rows, D), bf16) for lead in leads]
    kernel = functools.partial(grads_kernel, plan, len(arrays), phase)
    ins = [(coords, S)] + [(a, V) for a in arrays]
    return call(kernel, ins, outs, [V((D, arrays[0].shape[1]), bf16), V((D, D), bf16)], "grads", flops, 0)


def mate(value):
    return lax.ppermute(value, "narrow", [(0, 1), (1, 0)])


def step(link, value):
    masks = ((8, 4, 1, 2)[link], (4, 8, 2, 1)[link])
    pairs = [(2 * w + n, 2 * (w ^ masks[n]) + n) for w in range(16) for n in range(2)]
    return lax.ppermute(value, AXES, pairs)


def relative(values, bits):
    for place_of, bit in enumerate(reversed(bits)):
        flip = 1 << place_of
        values = [jnp.where(bit > 0, values[i ^ flip], values[i]) for i in range(len(values))]
    return values


def add(*terms):
    return functools.reduce(lambda p, q: p + q, [t.astype(f32) for t in terms])


def regroup(parts, bits):
    mine = relative(parts, bits)
    return relative([mine[0]] + [lax.ppermute(mine[k], AXES, [(i, i ^ k) for i in range(32)]) for k in (1, 2, 3)], bits)


def vector_tables(gains, biases):
    gains = gains.astype(f32).reshape(LAYERS, 2, D)
    biases = biases.astype(f32).reshape(LAYERS, 11, D)
    return jnp.concatenate([gains, biases, jnp.zeros((LAYERS, VECS - 13, D), f32)], 1)


NAMES = ("down", "up", "attn")
LOTS = ((("down", 1),), (("up", 1),), (("attn", 1),), (("down", 0), ("up", 0)), (("attn", 0),))


def whole_weight(matrix, by_rows):
    if by_rows:
        cut = jnp.transpose(matrix.reshape(4, 2, 2, 2, PIECE, D), (3, 1, 2, 0, 4, 5))
    else:
        cut = jnp.transpose(matrix.reshape(4, 2, PIECE, 2, 2, D), (4, 1, 3, 0, 2, 5))
    cut = [cut[0], jnp.swapaxes(cut[1], 0, 1)]
    return [cut[kn][kb] for kb in range(2) for kn in range(2)], 0, by_rows


def whole_grad(core, rest, rows, by_rows):
    near = jnp.stack([jnp.stack([rest[2], rest[1]]), rest[0]])
    cut = jnp.stack([jnp.transpose(near, (1, 0, 3, 2, 4, 5)), core])[..., rows, :]
    if by_rows:
        return jnp.transpose(cut, (3, 4, 2, 1, 0, 5, 6)).reshape(FF, D)
    return jnp.transpose(cut, (3, 4, 2, 5, 1, 0, 6)).reshape(D, FF)


def fetch_plain(w_qkv, w_out, w_up, w_down, gains, biases):
    def whole(value, rows):
        return lax.all_gather(value, AXES, axis=0, tiled=True).reshape(rows, -1)

    weights = {}
    for l in range(LAYERS):
        attn = jnp.concatenate([whole(w_qkv[l], D), whole(w_out[l], D)], 1)
        weights["attn", l] = whole_weight(attn, False)
        weights["up", l] = whole_weight(whole(w_up[l], D), False)
        weights["down", l] = whole_weight(whole(w_down[l], FF), True)
    return weights, vector_tables(whole(gains, 1)[0], whole(biases, 1)[0])


class Lot:
    def first(self, core, rest):
        self.core, self.rest = core, rest
        return add(rest[0], core[1]).astype(bf16)

    def second(self, got):
        self.got = got
        return add(self.rest[1], self.core[0, 1], got[1]).astype(bf16)

    def third(self, got):
        total = add(self.rest[2], self.core[0, 0], self.got[0], got)
        self.total = total[0]
        return total[1].astype(bf16)

    def fourth(self, got):
        total = add(self.total, got)
        self.total = total[0]
        return total[1].astype(bf16)

    def last(self, got):
        return add(self.total, got)


def stage(*groups):
    flat, tree = jax.tree.flatten(groups)
    return jax.tree.unflatten(tree, lax.optimization_barrier(flat))


def device_bits():
    wide = lax.axis_index("wide")
    return [(wide >> 3) & 1, (wide >> 2) & 1, (wide >> 1) & 1, wide & 1, lax.axis_index("narrow")]


def coordinates(values):
    return jnp.stack([jnp.asarray(v, jnp.int32) for v in values])


def layer_grads(sums):
    both = jnp.stack(sums)
    return both[:, :2].reshape(-1), both[:, 2:13].reshape(-1)


def gradient_blocks(coords, lot, kept, back, phase):
    items = []
    for name, l in LOTS[lot]:
        if name == "attn":
            items.append((name, [kept[l]["at"], kept[l]["ot"], back[l]["early"], back[l]["late"]], back[l]["flip"], PIECE))
        elif name == "up":
            items.append((name, [kept[l]["bt"]], back[l]["gu"], PIECE))
        else:
            items.append((name, [kept[l]["zt"]], back[l]["gb"], PIECE))
    outs = grads(coords, items, phase)
    return outs[0] if phase else outs


def shares_of(parts, bits):
    rows = D // 32
    cut = jnp.stack(parts)
    whole = jnp.concatenate(regroup([cut[:, s * rows : (s + 1) * rows] for s in range(4)], bits[3:]), 2)
    return [whole[i] for i in range(len(parts))]


def body(tokens, lengths, w_qkv, w_out, w_up, w_down, gains, biases, cotangent):
    args = (tokens, lengths, w_qkv, w_out, w_up, w_down, gains, biases, cotangent)
    if lax.axis_size("wide") == 16 and lax.axis_size("narrow") == 2:
        return staged(*args)
    return plain(*args)


def plain(tokens, lengths, w_qkv, w_out, w_up, w_down, gains, biases, cotangent):
    length = tokens.shape[0] // lengths.shape[0]
    coords = coordinates([0, 0, 0, 0, lengths[0]])
    table = rotary_tables(length)
    weights, vectors = fetch_plain(w_qkv, w_out, w_up, w_down, gains, biases)
    kept, back, wholes, x = [], [{}, {}], [], tokens
    for l in range(LAYERS):
        held, whole = attn_fwd(coords, x, vectors[l], table, [weights[name, l] for name in ("attn", "up", "down")])
        x, more, *_ = ffn_fwd(coords, held, vectors[l], whole[1], whole[2], l == LAYERS - 1)
        kept.append(held | more)
        wholes.append(whole)
    output = ffn_out(coords, kept[-1], x, vectors[-1], wholes[-1][2])
    grad, sums = cotangent, [None] * LAYERS
    for l in reversed(range(LAYERS)):
        last = l == 0
        back[l] = ffn_bwd(coords, grad, kept[l], vectors[l], wholes[l][1], wholes[l][2], not last)
        (back[l]["early"],) = attn_bwd(coords, back[l]["gmb"], kept[l], table, wholes[l][0], EARLY)
        back[l]["late"], back[l]["flip"] = attn_bwd(coords, back[l]["gmb"], kept[l], table, wholes[l][0], LATE)
        grad, more = attn_after(back[l], kept[l], vectors[l], wholes[l][0], last)
        sums[l] = back[l]["sums"] + more
    matrices = {}
    for lot, keys in enumerate(LOTS):
        core, rest = [gradient_blocks(coords, lot, kept, back, phase) for phase in (1, 0)]
        for i, key in enumerate(keys):
            rows = slice(i * PIECE, (i + 1) * PIECE)
            matrices[key] = whole_grad(core, rest, rows, key[0] == "down").astype(f32)
    outs = []
    for name, begin, end in (("attn", 0, 3 * D), ("attn", 3 * D, FF), ("up", 0, FF), ("down", 0, D)):
        cut = jnp.stack([matrices[name, l][:, begin:end].reshape(-1) for l in range(LAYERS)])
        outs.append(lax.psum_scatter(cut, AXES, scatter_dimension=1, tiled=True))
    outs += [lax.psum_scatter(v, AXES, scatter_dimension=0, tiled=True) for v in layer_grads(sums)]
    return (output, grad, *outs)


def turned(value, bits):
    value = value.reshape(2, 2, 2, 2, 2, -1)
    for axis, bit in enumerate(bits):
        value = jnp.where(bit > 0, jnp.flip(value, axis), value)
    cores = [jnp.transpose(value, order) for order in ((4, 2, 3, 1, 0, 5), (4, 3, 2, 0, 1, 5))]
    own = jnp.where(bits[4] > 0, cores[1][0], cores[0][0])
    other = jnp.where(bits[4] > 0, cores[0][1], cores[1][1])
    return jnp.stack([own, other])


def ordered(bit, own, got):
    return jnp.stack([jnp.where(bit > 0, got, own), jnp.where(bit > 0, own, got)])


def staged(tokens, lengths, w_qkv, w_out, w_up, w_down, gains, biases, cotangent):
    length = tokens.shape[0] // lengths.shape[0]
    bits = device_bits()
    coords = coordinates([lax.axis_index("wide") >> 2, *bits[2:], lengths[0]])
    table = rotary_tables(length)
    rows = D // 32
    weights, whole = {}, {}

    z1, z0, y, x, n = bits
    third, fourth = jnp.where(n > 0, y, x), jnp.where(n > 0, x, y)

    def link0(value):
        return ordered(jnp.where(n > 0, z0, z1), value, step(0, value))

    def link1(value):
        return value, step(1, value)

    def by_z(pair):
        own, got = pair
        blocks = []
        for high in range(2):
            for low in range(2):
                core0 = jnp.where(z0 == low, own[high], got[high])
                blocks.append(jnp.where(n > 0, jnp.where(z1 == high, own[low], got[low]), core0))
        return jnp.stack(blocks)

    def link2(value):
        return ordered(third, value, step(2, value))

    def arrived(keys, *pieces):
        offset = 0
        for key, height in keys:
            weights[key] = (list(pieces), offset, key[0] == "down")
            offset += height

    small = jnp.concatenate([gains, biases])
    width = small.shape[0]
    c0 = jnp.concatenate([w_down[0].reshape(PIECE, D), jnp.zeros((16, D), bf16).at[0, :width].set(small)])
    c0, w_qkv, w_out, w_up = stage(c0, w_qkv, w_out, w_up)
    t0 = link0(c0)
    flat = []
    for l in range(LAYERS):
        flat.append(jnp.concatenate([w_qkv[l].reshape(rows, 3 * D), w_out[l].reshape(rows, D)], 1))
        flat.append(w_up[l].reshape(rows, FF))
    flat = jnp.stack(flat)
    parts = [flat[:, :, s * D : (s + 1) * D] for s in range(4)]
    t0, parts = stage(t0, parts)
    u0 = link1(t0)
    c1, up0, attn1, up1 = jnp.concatenate(regroup(parts, bits[3:]), 1)
    c2, c3 = jnp.concatenate([up0, attn1]), jnp.concatenate([w_down[1].reshape(PIECE, D), up1])
    zz0, c1, c2, c3 = stage(by_z(u0), c1, c2, c3)
    near0, t12 = stage(link2(zz0), link0(jnp.concatenate([c1, c2])))
    t1, t2 = t12[:, :PIECE], t12[:, PIECE:]
    far0, mate0, u1 = step(3, near0), mate(near0), link1(t1)
    far0, mate0, zz1, t2 = stage(far0, mate0, by_z(u1), t2)
    near1, far_mate0, u2, t3 = link2(zz1), mate(far0), link1(t2), link0(c3)
    near1, far_mate0, t3 = stage(near1, far_mate0, t3)
    zz2 = by_z(u2)
    arrived(((("down", 0), PIECE),), near0, mate0, far0, far_mate0)
    far1, mate1, near2, u3 = step(3, near1), mate(near1), link2(zz2), link1(t3)
    whole["down", 0] = assemble(coords, weights["down", 0])
    own, other = [], []
    for first, second, to in ((near0, far0, own), (mate0, far_mate0, other)):
        turn = n if to is own else 1 - n
        both = ordered(jnp.where(turn > 0, x, y), first[:, :, PIECE, :width], second[:, :, PIECE, :width])
        to.append(jnp.where(turn > 0, jnp.transpose(both, (2, 1, 0, 3)), jnp.transpose(both, (2, 0, 1, 3))))
    both = ordered(n, own[0], other[0])
    both = jnp.transpose(both, (1, 2, 3, 0, 4)).reshape(32, width)
    vectors = vector_tables(both[:, : gains.shape[0]].reshape(-1), both[:, gains.shape[0] :].reshape(-1))
    far1, mate1, near2, zz3, vectors, whole = stage(far1, mate1, near2, by_z(u3), vectors, whole)
    far_mate1, near2, zz3 = stage(mate(far1), near2, zz3)
    arrived(((("attn", 0), PIECE),), near1, mate1, far1, far_mate1)
    kept, back = [None, None], [None, None]
    far2, mate2 = step(3, near2), mate(near2)
    kept[0], got = attn_fwd(coords, tokens, vectors[0], table, [weights["attn", 0]])
    whole["attn", 0] = got[0]
    far2, mate2, kept[0] = stage(far2, mate2, kept[0])
    far_mate2, kept[0], zz3 = stage(mate(far2), kept[0], zz3)
    arrived(((("up", 0), PIECE), (("attn", 1), PIECE)), near2, mate2, far2, far_mate2)
    got3 = step(2, zz3)
    h, more, whole["up", 0], _ = ffn_fwd(coords, kept[0], vectors[0], weights["up", 0], whole["down", 0], False)
    kept[0] |= more
    got3, h = stage(got3, h)
    near3, h = stage(ordered(third, zz3, got3), h)
    far3, mate3 = step(3, near3), mate(near3)
    kept[1], got = attn_fwd(coords, h, vectors[1], table, [weights["attn", 1]])
    whole["attn", 1] = got[0]
    far3, mate3, kept[1] = stage(far3, mate3, kept[1])
    arrived(((("down", 1), PIECE), (("up", 1), PIECE)), near3, mate3, far3, mate(far3))
    hidden, more, whole["up", 1], whole["down", 1] = ffn_fwd(
        coords, kept[1], vectors[1], weights["up", 1], weights["down", 1], True
    )
    kept[1] |= more

    d1, u1, a1, du0, a0, extra = [Lot() for _ in range(6)]

    def blocks(lot, phase):
        return gradient_blocks(coords, lot, kept, back, phase)

    live = jnp.arange(length, dtype=jnp.int32)[:, None] < lengths[0]
    back[1] = {"gb": jnp.where(live, cotangent, jnp.zeros((), bf16))}
    core, back[1] = stage(blocks(0, 1), back[1])
    first, cotangent = stage(d1.first(mate(core), blocks(0, 0)), cotangent)

    got_d1 = step(3, first)
    back[1] |= ffn_bwd(coords, cotangent, kept[1], vectors[1], whole["up", 1], whole["down", 1], True)
    got_d1, core, back[1] = stage(got_d1, blocks(1, 1), back[1])
    second, core, back[1] = stage(d1.second(got_d1), core, back[1])

    got_d1 = step(2, second)
    core, rest = stage(mate(core), blocks(1, 0))
    first, back[1] = stage(u1.first(core, rest), back[1])

    got_u1 = step(3, first)
    (back[1]["early"],) = attn_bwd(coords, back[1]["gmb"], kept[1], table, whole["attn", 1], EARLY)
    got_u1, got_d1, back[1] = stage(got_u1, got_d1, back[1])
    second, third, back[1] = stage(u1.second(got_u1), d1.third(got_d1), back[1])

    got_u1, got_d1 = step(2, second), step(1, third)
    back[1]["late"], back[1]["flip"] = attn_bwd(coords, back[1]["gmb"], kept[1], table, whole["attn", 1], LATE)
    got_u1, got_d1, core, back[1] = stage(got_u1, got_d1, blocks(2, 1), back[1])
    third, fourth, core, back[1] = stage(u1.third(got_u1), d1.fourth(got_d1), core, back[1])

    got_u1, got_d1 = step(1, third), step(0, fourth)
    core, rest = stage(mate(core), blocks(2, 0))
    first, back[1] = stage(a1.first(core, rest), back[1])

    got_a1 = step(3, first)
    grad, more = attn_after(back[1], kept[1], vectors[1], whole["attn", 1], False)
    sums = [None, back[1]["sums"] + more]
    back[0] = ffn_bwd(coords, grad, kept[0], vectors[0], whole["up", 0], whole["down", 0], False)
    got_a1, got_u1, got_d1, core, back[0] = stage(got_a1, got_u1, got_d1, blocks(3, 1), back[0])
    second, fourth, core, back[0] = stage(a1.second(got_a1), u1.fourth(got_u1), core, back[0])

    got_a1, got_u1, core, rest = stage(step(2, second), step(0, fourth), mate(core), blocks(3, 0))
    first, third, back[0] = stage(du0.first(core, rest), a1.third(got_a1), back[0])

    got_du0, got_a1 = step(3, first), step(1, third)
    (back[0]["early"],) = attn_bwd(coords, back[0]["gmb"], kept[0], table, whole["attn", 0], EARLY)
    back[0]["late"], back[0]["flip"] = attn_bwd(coords, back[0]["gmb"], kept[0], table, whole["attn", 0], LATE)
    got_du0, got_a1, back[0] = stage(got_du0, got_a1, back[0])
    second, fourth, back[0], hidden = stage(du0.second(got_du0), a1.fourth(got_a1), back[0], hidden)

    got_du0, got_a1 = step(2, second), step(0, fourth)
    core = blocks(4, 1)
    grad, more = attn_after(back[0], kept[0], vectors[0], whole["attn", 0], True)
    sums[0] = back[0]["sums"] + more
    output = ffn_out(coords, kept[1], hidden, vectors[1], whole["down", 1])
    got_du0, got_a1, core, grad, sums, back[0], output = stage(got_du0, got_a1, core, grad, sums, back[0], output)
    third, core, back[0] = stage(du0.third(got_du0), core, back[0])

    got_du0 = step(1, third)
    core, rest = stage(mate(core), blocks(4, 0))
    first, sums = stage(a0.first(core, rest), sums)

    got_a0 = step(3, first)
    small = turned(jnp.concatenate([v.reshape(32, -1) for v in layer_grads(sums)], 1), bits)
    first = extra.first(mate(small[1]), [small[0, 1], small[0, 0, 1], small[0, 0, 0]])
    got_a0, got_du0, first, got_d1, got_u1, got_a1, grad = stage(got_a0, got_du0, first, got_d1, got_u1, got_a1, grad)
    second, first, fourth = stage(a0.second(got_a0), first, du0.fourth(got_du0))

    got_a0, got_x, got_du0 = step(2, second), step(3, first), step(0, fourth)
    shares = [u1.last(got_u1), a1.last(got_a1)]
    got_a0, got_x, got_du0, shares = stage(got_a0, got_x, got_du0, shares)
    third, second, got_du0 = stage(a0.third(got_a0), extra.second(got_x), got_du0)

    got_a0, got_x = step(1, third), step(2, second)
    done = du0.last(got_du0)
    downs = jnp.stack([done[:PIECE].reshape(-1), d1.last(got_d1).reshape(-1)])
    up1, attn1, up0 = shares_of([*shares, done[PIECE:]], bits)
    got_a0, got_x, up1, attn1, up0, downs = stage(got_a0, got_x, up1, attn1, up0, downs)
    fourth, third = stage(a0.fourth(got_a0), extra.third(got_x))

    got_a0, got_x = step(0, fourth), step(1, third)
    ups = jnp.stack([up0.reshape(-1), up1.reshape(-1)])
    got_a0, got_x, ups = stage(got_a0, got_x, ups)
    (attn0,) = shares_of([a0.last(got_a0)], bits)
    mine = extra.last(step(0, extra.fourth(got_x)))
    return (
        output,
        grad,
        jnp.stack([v[:, : 3 * D].reshape(-1) for v in (attn0, attn1)]),
        jnp.stack([v[:, 3 * D :].reshape(-1) for v in (attn0, attn1)]),
        ups,
        downs,
        mine[: gains.shape[0]],
        mine[gains.shape[0] :],
    )


def solution(mesh):
    both, flat, rows = P(AXES), P(None, AXES), P(AXES, None)
    return jax.shard_map(
        body,
        mesh=mesh,
        in_specs=(rows, both, flat, flat, flat, flat, both, both, rows),
        out_specs=(rows, rows, flat, flat, flat, flat, both, both),
        check_vma=False,
    )
```

```python
import functools

import jax
import jax.numpy as jnp
import numpy as np
from jax import lax
from jax.experimental import pallas as pl
from jax.experimental.pallas import tpu as pltpu
from jax.sharding import PartitionSpec as P

D = 640
HEADS = 20
HEAD_DIM = 32
FF = 2560
LAYERS = 2
EPSILON = 1e-05
MASKED = -1e9
LANES = 128
GROUPS = D // LANES
PER_GROUP = LANES // HEAD_DIM
BLOCKS = FF // D
EARLY, LATE = (0, 3), (3, 2)
PIECE = 80
VECS = 16
AXES = ("wide", "narrow")
WHOLE, WHOLE_ROWS = (4, 2, PIECE, FF), (4, 2, 2, 2, PIECE, D)
SLACK = 8 * 1024 * 1024
f32, bf16 = jnp.float32, jnp.bfloat16

GAIN_A, GAIN_F, SHIFT_A, BIAS_QKV, BIAS_OUT, SHIFT_F, BIAS_UP, BIAS_DOWN = 0, 1, 2, 3, 6, 7, 8, 12


def rotary_tables(length):
    half = HEAD_DIM // 2
    inverse = 1.0 / 10000.0 ** (np.arange(half) * (2.0 / HEAD_DIM))
    angles = np.arange(length)[:, None] * inverse[None, :]
    cos, sine = np.cos(angles), np.sin(angles)
    none = np.zeros_like(sine)
    ahead = np.tile(np.concatenate([-sine, none], 1), (1, PER_GROUP))
    behind = np.tile(np.concatenate([none, sine], 1), (1, PER_GROUP))
    wide = np.stack([np.tile(cos, (1, 2 * PER_GROUP)), ahead, behind]).astype(np.float32)
    return jnp.asarray(wide), jnp.asarray(np.stack([cos.T, sine.T]).astype(np.float32))


def dot(left, right):
    return jnp.dot(left, right, preferred_element_type=f32)


def dot_nt(left, right):
    return lax.dot_general(left, right, (((1,), (1,)), ((), ())), preferred_element_type=f32)


def dot_tn(left, right):
    return lax.dot_general(left, right, (((0,), (0,)), ((), ())), preferred_element_type=f32)


def rotated(value, table):
    half = HEAD_DIM // 2
    return value * table[0] + pltpu.roll(value, LANES - half, 1) * table[1] + pltpu.roll(value, half, 1) * table[2]


def rotated_back(value, table):
    half = HEAD_DIM // 2
    first, second = value[:half], value[half:]
    return jnp.concatenate([first * table[0] + second * table[1], second * table[0] - first * table[1]], 0)


def unit_of(value):
    centered = value - jnp.mean(value, -1, keepdims=True)
    inverse = lax.rsqrt(jnp.mean(centered * centered, -1, keepdims=True) + EPSILON)
    return centered * inverse, inverse


def norm_back(grad, unit, inverse, gain):
    scaled = grad * gain
    return inverse * (scaled - jnp.mean(scaled, -1, keepdims=True) - unit * jnp.mean(scaled * unit, -1, keepdims=True))


def column_sum(value):
    return jnp.sum(value, 0, keepdims=True)


def gelu_parts(value):
    scaled = jnp.abs(value) * 0.7071067811865476
    t = 1.0 / (1.0 + 0.3275911 * scaled)
    bell = jnp.exp(-scaled * scaled)
    series = t * (0.127414796 + t * (-0.142248368 + t * (0.7107068705 + t * (-0.7265760135 + t * 0.5307027145))))
    tail = series * bell
    return jnp.where(value >= 0.0, 1.0 - tail, tail), bell * 0.3989422804014327


def row_loop(length, step, body):
    def run(i, carry):
        body(pl.ds(pl.multiple_of(i * step, step), step), i)
        return carry

    lax.fori_loop(0, length // step, run, 0)


def owner_of(coords, kn, kb, ka, k2, k1):
    n = coords[3] ^ kn
    z = coords[0] ^ (2 * k1 + k2 + n * (k2 - k1))
    return z, coords[1] ^ (kb + n * (ka - kb)), coords[2] ^ (ka + n * (kb - ka)), n


PLACES = [(ka, k2, k1) for ka in range(2) for k2 in range(2) for k1 in range(2)]


class Assembly:
    def __init__(self, coords, by_rows, pieces, offset, whole, sems):
        self.by_rows, self.whole, self.sems = by_rows, whole, sems
        self.any = pieces[0].at[0, :, pl.ds(offset, PIECE)]
        for kb in range(2):
            for kn in range(2):
                n = coords[3] ^ kn
                b = (coords[1] + n * (coords[2] - coords[1])) ^ kb
                for a in range(2):
                    target = self.target(a + n * (b - a), b + n * (a - b), n)
                    pltpu.make_async_copy(pieces[2 * kb + kn].at[a, :, pl.ds(offset, PIECE)], *target).start()

    def target(self, x, y, n):
        to = (y, x, n) if self.by_rows else (y, slice(None), pl.ds(pl.multiple_of((2 * x + n) * D, D), D))
        return self.whole.at[(slice(None), *to)], self.sems.at[4 * x + 2 * n + y]

    def wait(self, quarters=(0, 1, 2, 3)):
        for quarter in quarters:
            for y in range(2):
                pltpu.make_async_copy(self.any, *self.target(quarter // 2, y, quarter % 2)).wait()


def head_masks():
    lane = lax.broadcasted_iota(jnp.int32, (1, LANES), 1)
    return [(lane // HEAD_DIM == head).astype(f32).astype(bf16) for head in range(PER_GROUP)]


def masked_tail(length, live):
    row = lax.broadcasted_iota(jnp.int32, (length, LANES), 0)
    lane = lax.broadcasted_iota(jnp.int32, (length, LANES), 1)
    keys = jnp.where((lane == 0) & (row >= live), MASKED, 0.0).astype(bf16)
    row = lax.broadcasted_iota(jnp.int32, (LANES, length), 0)
    return keys, jnp.where(row == 0, 1.0, 0.0).astype(bf16)


def attn_fwd_kernel(plan, coords, x_ref, vec_ref, table_ref, *refs):
    count = len(plan)
    pieces, refs = refs[: 4 * count], refs[4 * count :]
    at_ref, qt_ref, kv_ref, ot_ref, lse_ref, m_ref, b_ref, bt_ref, *refs = refs
    wholes, refs = refs[:count], refs[count:]
    a_ref, q_ref, key_ref, query_ref, sems = refs
    length = x_ref.shape[0]
    jobs = [
        Assembly(coords, by_rows, pieces[4 * i : 4 * i + 4], offset, wholes[i], sems.at[i])
        for i, (offset, by_rows) in enumerate(plan)
    ]
    w_ref = wholes[0]

    def norm(rows, _):
        unit, _ = unit_of(x_ref[rows, :].astype(f32))
        a_ref[rows, :] = (unit * vec_ref[GAIN_A : GAIN_A + 1, :] + vec_ref[SHIFT_A : SHIFT_A + 1, :]).astype(bf16)

    row_loop(length, 128, norm)
    normed = a_ref[...]
    at_ref[...] = normed.T
    for part in range(3):
        jobs[0].wait([part])
        out = dot(normed, w_ref[:, :, :, part * D : (part + 1) * D].reshape(D, D)) + vec_ref[BIAS_QKV + part : BIAS_QKV + part + 1, :]
        if part == 0:
            out = out * HEAD_DIM**-0.5
        for group in range(GROUPS):
            lanes = slice(group * LANES, (group + 1) * LANES)
            piece = out[:, lanes]
            if part < 2:
                piece = rotated(piece, table_ref)
            if part == 0:
                qt_ref[lanes, :] = piece.astype(bf16).T
            else:
                kv_ref[:, (part - 1) * D + group * LANES : (part - 1) * D + (group + 1) * LANES] = piece.astype(bf16)
    masks = head_masks()
    tail, query_ref[LANES:, :] = masked_tail(length, coords[4])
    for head in range(PER_GROUP):
        key_ref[head, :, LANES:] = tail
    ones = jnp.ones((16, length), bf16)

    def group_step(group, carry):
        rows = pl.ds(pl.multiple_of(group * LANES, LANES), LANES)
        query_ref[:LANES, :] = qt_ref[rows, :]
        values = kv_ref[:, pl.ds(pl.multiple_of(D + group * LANES, LANES), LANES)].T
        for head in range(PER_GROUP):
            key_ref[head, :, :LANES] = kv_ref[:, rows] * masks[head]
        every = dot(key_ref[...].reshape(PER_GROUP * length, 2 * LANES), query_ref[...])
        for head in range(PER_GROUP):
            scores = every[head * length : (head + 1) * length]
            top = jnp.max(scores, 0, keepdims=True)
            probs = jnp.exp(scores - top).astype(bf16)
            wide = jnp.concatenate([values[head * HEAD_DIM : (head + 1) * HEAD_DIM], ones], 0)
            out = dot(wide, probs)
            total = out[HEAD_DIM : HEAD_DIM + 1]
            to = pl.ds(pl.multiple_of(group * LANES + head * HEAD_DIM, HEAD_DIM), HEAD_DIM)
            ot_ref[to, :] = (out[:HEAD_DIM] / total).astype(bf16)
            lse_ref[pl.ds(group * PER_GROUP + head, 1), :] = top + jnp.log(total)
        return carry

    for group in range(GROUPS):
        group_step(group, 0)
    jobs[0].wait([3])
    q_ref[...] = ot_ref[...].T
    m_ref[...] = x_ref[...].astype(f32) + (dot(q_ref[...], w_ref[:, :, :, 3 * D :].reshape(D, D)) + vec_ref[BIAS_OUT : BIAS_OUT + 1, :])

    def after(rows, _):
        unit, _ = unit_of(m_ref[rows, :])
        b_ref[rows, :] = (unit * vec_ref[GAIN_F : GAIN_F + 1, :] + vec_ref[SHIFT_F : SHIFT_F + 1, :]).astype(bf16)

    row_loop(length, 128, after)
    bt_ref[...] = b_ref[...].T
    for job in jobs[1:]:
        job.wait()


def assemble_kernel(offset, by_rows, coords, *refs):
    Assembly(coords, by_rows, refs[:4], offset, refs[4], refs[5]).wait()


def ffn_fwd_kernel(offsets, last, coords, m_ref, b_ref, vec_ref, *refs):
    offset, offset_down = offsets
    if offset is None:
        up_ref, down_ref, y_ref, zt_ref, slope_ref, *rest = refs
    elif offset_down is None:
        down_ref, *pieces, y_ref, zt_ref, slope_ref, up_ref = refs[:9]
        rest = refs[9:]
    else:
        *pieces, y_ref, zt_ref, slope_ref, up_ref, down_ref = refs[:9]
        rest = refs[9:]
    z_ref = y_ref if last else rest[0]
    sems = rest[-1] if rest else None
    if offset is not None:
        job = Assembly(coords, False, pieces, offset, up_ref, sems.at[0])
    if offset_down is not None:
        job_down = Assembly(coords, True, pieces, offset_down, down_ref, sems.at[1])
    normed = b_ref[...]
    for block in range(BLOCKS):
        if offset is not None:
            job.wait([block])
        columns = slice(block * D, (block + 1) * D)
        part = up_ref[:, columns] if offset is None else up_ref[:, :, :, columns].reshape(D, D)
        pre = dot(normed, part) + vec_ref[BIAS_UP + block : BIAS_UP + block + 1, :]
        cdf, bell = gelu_parts(pre)
        z_ref[:, columns] = (pre * cdf).astype(bf16)
        slope_ref[:, columns] = (cdf + pre * bell).astype(bf16)
        zt_ref[columns, :] = z_ref[:, columns].T
    if offset_down is not None:
        job_down.wait()
    if not last:
        y_ref[...] = m_ref[...] + (dot(z_ref[...], down_ref[...].reshape(FF, D)) + vec_ref[BIAS_DOWN : BIAS_DOWN + 1, :])


def ffn_out_kernel(coords, m_ref, z_ref, vec_ref, down_ref, y_ref):
    out = m_ref[...] + (dot(z_ref[...], down_ref[...]) + vec_ref[BIAS_DOWN : BIAS_DOWN + 1, :])
    row = lax.broadcasted_iota(jnp.int32, (m_ref.shape[0], 1), 0)
    y_ref[...] = jnp.where(row < coords[4], out, 0.0).astype(bf16)


def ffn_bwd_kernel(top, coords, g_ref, slope_ref, m_ref, vec_ref, up_ref, down_ref, *refs):
    gb_ref, gu_ref, gm_ref, gmb_ref, sums_ref = refs
    length = m_ref.shape[0]
    sums_ref[...] = jnp.zeros_like(sums_ref)

    def add(row, value):
        sums_ref[row : row + 1, :] += column_sum(value)

    grad = g_ref[...].astype(f32)
    if top:
        row = lax.broadcasted_iota(jnp.int32, (length, 1), 0)
        grad = jnp.where(row < coords[4], grad, 0.0)
    low = grad.astype(bf16)
    gb_ref[...] = low
    add(BIAS_DOWN, low.astype(f32))
    for block in range(BLOCKS):
        columns = slice(block * D, (block + 1) * D)
        part = (dot_nt(low, down_ref[columns, :]) * slope_ref[:, columns].astype(f32)).astype(bf16)
        gu_ref[:, columns] = part
        add(BIAS_UP + block, part.astype(f32))
    gm_ref[...] = dot_nt(gu_ref[...], up_ref[...])

    def after(rows, i):
        normed_grad = gm_ref[rows, :]
        unit, inverse = unit_of(m_ref[rows, :])
        add(GAIN_F, normed_grad * unit)
        add(SHIFT_F, normed_grad)
        grad = g_ref[rows, :].astype(f32)
        if top:
            row = lax.broadcasted_iota(jnp.int32, (128, 1), 0) + i * 128
            grad = jnp.where(row < coords[4], grad, 0.0)
        middle = grad + norm_back(normed_grad, unit, inverse, vec_ref[GAIN_F : GAIN_F + 1, :])
        gm_ref[rows, :] = middle
        low = middle.astype(bf16)
        gmb_ref[rows, :] = low
        add(BIAS_OUT, low.astype(f32))

    row_loop(length, 128, after)


def attn_bwd_kernel(groups, coords, gmb_ref, qt_ref, kv_ref, ot_ref, lse_ref, table_ref, w_ref, *refs):
    start, count = groups
    gp_ref, *flip_ref, go_ref, key_ref, query_ref = refs
    length = gmb_ref.shape[0]
    low = gmb_ref[...]
    if flip_ref:
        flip_ref[0][...] = low.T
    go_ref[...] = dot_nt(w_ref[start * LANES : (start + count) * LANES, 3 * D :], low).astype(bf16)
    masks = head_masks()
    tail, query_ref[LANES:, :] = masked_tail(length, coords[4])
    for head in range(PER_GROUP):
        key_ref[head, :, LANES:] = tail

    def group_step(i, carry):
        group = i + start
        rows = pl.ds(pl.multiple_of(group * LANES, LANES), LANES)
        query, grad = qt_ref[rows, :], go_ref[pl.ds(pl.multiple_of(i * LANES, LANES), LANES), :]
        query_ref[:LANES, :] = query
        keys = kv_ref[:, rows]
        values = kv_ref[:, pl.ds(pl.multiple_of(D + group * LANES, LANES), LANES)]
        flipped = keys.T
        products = grad.astype(f32) * ot_ref[rows, :].astype(f32)
        for head in range(PER_GROUP):
            key_ref[head, :, :LANES] = keys * masks[head]
        for head in range(PER_GROUP):
            part = slice(head * HEAD_DIM, (head + 1) * HEAD_DIM)
            delta = column_sum(products[part])
            probs = jnp.exp(dot(key_ref[head], query_ref[...]) - lse_ref[pl.ds(group * PER_GROUP + head, 1), :])
            scores = (probs * (dot(values * masks[head], grad) - delta)).astype(bf16)
            dv = dot_nt(grad[part], probs.astype(bf16))
            dk = dot_nt(query[part], scores)
            dq = dot(flipped[part], scores)
            to = pl.ds(pl.multiple_of(i * LANES + head * HEAD_DIM, HEAD_DIM), HEAD_DIM)
            dq = rotated_back(dq.astype(bf16).astype(f32), table_ref) * HEAD_DIM**-0.5
            dk = rotated_back(dk.astype(bf16).astype(f32), table_ref)
            for part, value in enumerate((dq, dk, dv)):
                gp_ref[part, to, :] = value.astype(bf16)
        return carry

    lax.fori_loop(0, count, group_step, 0)


def attn_after_kernel(early_ref, late_ref, gm_ref, x_ref, vec_ref, w_ref, *refs):
    gx_ref, sums_ref, ga_ref = refs
    length = x_ref.shape[0]
    sums_ref[...] = jnp.zeros_like(sums_ref)

    def add(row, value):
        sums_ref[row : row + 1, :] += column_sum(value)

    ones = jnp.ones((16, length), bf16)
    total = 0.0
    for part in range(3):
        for ref, (start, count) in ((early_ref, EARLY), (late_ref, LATE)):
            columns = slice(start * LANES, (start + count) * LANES)
            sums_ref[BIAS_QKV + part : BIAS_QKV + part + 1, columns] = dot_nt(ones, ref[part])[:1]
            total = total + dot(w_ref[:, part * D + start * LANES : part * D + (start + count) * LANES], ref[part])
    ga_ref[...] = total.T

    def after(rows, _):
        normed_grad = ga_ref[rows, :]
        unit, inverse = unit_of(x_ref[rows, :].astype(f32))
        add(GAIN_A, normed_grad * unit)
        add(SHIFT_A, normed_grad)
        out = gm_ref[rows, :] + norm_back(normed_grad, unit, inverse, vec_ref[GAIN_A : GAIN_A + 1, :])
        gx_ref[rows, :] = out.astype(gx_ref.dtype)

    row_loop(length, 128, after)


def grads_kernel(items, inputs, phase, coords, *refs):
    ins, outs, (left_ref, whole_ref) = refs[:inputs], refs[inputs:-2], refs[-2:]

    def put(value, kb, ka, k2, k1, to):
        to = slice(to, to + value.shape[0])
        if phase:
            outs[0][kb, ka, k2, k1, to] = value
        elif kb:
            outs[0][ka, k2, k1, to] = value
        elif ka:
            outs[1][k2, k1, to] = value
        else:
            outs[2][k2, k1, to] = value

    for kind, lefts, right, to in items:
        if kind == "down":
            for kb in range(2):
                for place, (ka, k2, k1) in enumerate(PLACES):
                    z, y, x, n = owner_of(coords, phase, kb, ka, k2, k1)
                    start = pl.multiple_of((8 * z + 4 * y + 2 * x + n) * PIECE, PIECE)
                    left_ref[place * PIECE : (place + 1) * PIECE, :] = ins[lefts[0]][pl.ds(start, PIECE), :]
                whole = dot(left_ref[...], ins[right][...]).astype(bf16)
                for place, (ka, k2, k1) in enumerate(PLACES):
                    put(whole[place * PIECE : (place + 1) * PIECE], kb, ka, k2, k1, to)
        else:
            for kx in range(2):
                quarter = 2 * (coords[2] ^ kx) + (coords[3] ^ phase)
                n = coords[3] ^ phase
                for ky in range(2):
                    for kz in range(4):
                        k2, k1 = kz // 2, kz % 2
                        z = coords[0] ^ (2 * k1 + k2 + n * (k2 - k1))
                        start = pl.multiple_of((2 * z + (coords[1] ^ ky)) * PIECE, PIECE)
                        to_row = (4 * ky + kz) * PIECE
                        if kind == "up":
                            part = ins[lefts[0]][pl.ds(start, PIECE), :]
                        else:
                            part = jnp.where(quarter == 3, ins[lefts[1]][pl.ds(start, PIECE), :], ins[lefts[0]][pl.ds(start, PIECE), :])
                        left_ref[to_row : to_row + PIECE, :] = part
                if kind == "attn":

                    @pl.when(quarter == 3)
                    def _(right=right):
                        whole_ref[...] = dot_nt(left_ref[...], ins[right][...]).astype(bf16)

                    @pl.when(quarter < 3)
                    def _(right=right, quarter=quarter):
                        part = jnp.minimum(quarter, 2)
                        for i, (start, count) in ((2, EARLY), (1, LATE)):
                            columns = slice(start * LANES, (start + count) * LANES)
                            whole_ref[:, columns] = dot_nt(left_ref[...], ins[right - i][part]).astype(bf16)

                else:
                    columns = pl.ds(pl.multiple_of(quarter * D, D), D)
                    whole_ref[...] = dot(left_ref[...], ins[right][:, columns]).astype(bf16)

                def write(swapped, kx=kx, to=to):
                    for ky in range(2):
                        for kz in range(4):
                            start = (4 * ky + kz) * PIECE
                            ka, kb = (ky, kx) if swapped else (kx, ky)
                            put(whole_ref[start : start + PIECE, :], kb, ka, kz // 2, kz % 2, to)

                pl.when(n == 0)(functools.partial(write, False))
                pl.when(n == 1)(functools.partial(write, True))


def call(kernel, ins, outs, scratch, name, flops, exps=0):
    moved = sum(a.size * a.dtype.itemsize for a, _ in ins) + sum(int(np.prod(s)) * jnp.dtype(t).itemsize for s, t in outs)
    limit = SLACK + sum(int(np.prod(t.shape)) * t.dtype.itemsize for t in scratch if t.memory_space == V)
    return pl.pallas_call(
        kernel,
        out_shape=[jax.ShapeDtypeStruct(s, t) for s, t in outs],
        in_specs=[pl.BlockSpec(memory_space=space) for _, space in ins],
        out_specs=[pl.BlockSpec(memory_space=pltpu.VMEM)] * len(outs),
        scratch_shapes=scratch,
        compiler_params=pltpu.CompilerParams(vmem_limit_bytes=limit),
        cost_estimate=pl.CostEstimate(flops=int(flops), bytes_accessed=int(moved), transcendentals=int(exps)),
        name=name,
    )(*[a for a, _ in ins])


V, S, H = pltpu.VMEM, pltpu.SMEM, pl.ANY
SEMS = pltpu.SemaphoreType.DMA


def attn_fwd(coords, x, vec, table, weights):
    n = x.shape[0]
    ins = [(coords, S), (x, V), (vec, V), (table[0], V)] + [(p, H) for w in weights for p in w[0]]
    outs = [((D, n), bf16), ((D, n), bf16), ((n, 2 * D), bf16), ((D, n), bf16), ((24, n), f32)]
    outs += [((n, D), f32), ((n, D), bf16), ((D, n), bf16)]
    outs += [(WHOLE_ROWS if w[2] else WHOLE, bf16) for w in weights]
    scratch = [V((n, D), bf16), V((n, D), bf16), V((PER_GROUP, n, 2 * LANES), bf16), V((2 * LANES, n), bf16)]
    scratch.append(SEMS((len(weights), 8)))
    kernel = functools.partial(attn_fwd_kernel, [w[1:] for w in weights])
    out = call(kernel, ins, outs, scratch, "attn_fwd", 2 * n * D * FF + 4 * n * n * D, HEADS * n * n)
    return dict(zip(("at", "qt", "kv", "ot", "lse", "m", "b", "bt"), out[:8], strict=True)) | {"x": x}, [w.reshape((FF, D) if w.ndim == 6 else (D, FF)) for w in out[8:]]


def assemble(coords, weight):
    pieces, offset, by_rows = weight
    outs = [(WHOLE_ROWS if by_rows else WHOLE, bf16)]
    ins = [(coords, S)] + [(p, H) for p in pieces]
    out = call(functools.partial(assemble_kernel, offset, by_rows), ins, outs, [SEMS((8,))], "assemble", 0)[0]
    return out.reshape((FF, D) if by_rows else (D, FF))


def ffn_fwd(coords, kept, vec, up, down, last):
    n = kept["m"].shape[0]
    parts = [isinstance(w, tuple) for w in (up, down)]
    ins = [(coords, S), (kept["m"], V), (kept["b"], V), (vec, V)]
    ins += [(w, V) for w, part in zip((up, down), parts) if not part]
    ins += [(p, H) for p in up[0]] if parts[0] else []
    outs = [((n, FF), bf16) if last else ((n, D), f32), ((FF, n), bf16), ((n, FF), bf16)]
    outs += [(shape, bf16) for shape, part in zip((WHOLE, WHOLE_ROWS), parts) if part]
    scratch = ([] if last else [V((n, FF), bf16)]) + ([SEMS((2, 8))] if parts[0] else [])
    offsets = [w[1] if part else None for w, part in zip((up, down), parts)]
    kernel = functools.partial(ffn_fwd_kernel, offsets, last)
    y, zt, slope, *more = call(kernel, ins, outs, scratch, "ffn_fwd", 4 * n * D * FF, 2 * n * FF)
    up = more[0].reshape(D, FF) if parts[0] else up
    down = more[1].reshape(FF, D) if parts[1] else down
    return y, {"zt": zt, "slope": slope}, up, down


def ffn_out(coords, kept, hidden, vec, down):
    ins = [(coords, S)] + [(a, V) for a in (kept["m"], hidden, vec, down)]
    return call(ffn_out_kernel, ins, [(kept["m"].shape, bf16)], [], "ffn_out", 2 * hidden.size * D)[0]


def ffn_bwd(coords, g, kept, vec, up, down, top):
    n = g.shape[0]
    ins = [(coords, S)] + [(a, V) for a in (g, kept["slope"], kept["m"], vec, up, down)]
    outs = [((n, D), bf16), ((n, FF), bf16), ((n, D), f32), ((n, D), bf16), ((VECS, D), f32)]
    out = call(functools.partial(ffn_bwd_kernel, top), ins, outs, [], "ffn_bwd", 4 * n * D * FF, 0)
    return dict(zip(("gb", "gu", "gm", "gmb", "sums"), out, strict=True))


def attn_bwd(coords, gmb, kept, table, weight, groups):
    n = gmb.shape[0]
    ins = [(coords, S)] + [(a, V) for a in (gmb, kept["qt"], kept["kv"], kept["ot"], kept["lse"], table[1], weight)]
    rows = groups[1] * LANES
    scratch = [V((rows, n), bf16), V((PER_GROUP, n, 2 * LANES), bf16), V((2 * LANES, n), bf16)]
    outs = [((3, rows, n), bf16)] + ([((D, n), bf16)] if groups == LATE else [])
    flops = 2 * n * D * rows + 10 * n * n * rows
    kernel = functools.partial(attn_bwd_kernel, groups)
    return call(kernel, ins, outs, scratch, "attn_bwd", flops, HEADS * n * n)


def attn_after(back, kept, vec, weight, last):
    n = back["gm"].shape[0]
    ins = [(a, V) for a in (back["early"], back["late"], back["gm"], kept["x"], vec, weight)]
    outs = [((n, D), bf16 if last else f32), ((VECS, D), f32)]
    return call(attn_after_kernel, ins, outs, [V((n, D), f32)], "attn_after", 6 * n * D * D, 0)


def grads(coords, items, phase):
    arrays, plan, flops, rows = [], [], 0, 0
    for kind, lefts, right, height in items:
        index = list(range(len(arrays), len(arrays) + len(lefts)))
        arrays += [*lefts, right]
        plan.append((kind, index, len(arrays) - 1, rows))
        rows += height
        flops += 2 * arrays[0].shape[1] * D * D * 2
    leads = [(2, 2, 2, 2)] if phase else [(2, 2, 2), (2, 2), (2, 2)]
    outs = [((*lead, rows, D), bf16) for lead in leads]
    kernel = functools.partial(grads_kernel, plan, len(arrays), phase)
    ins = [(coords, S)] + [(a, V) for a in arrays]
    return call(kernel, ins, outs, [V((D, arrays[0].shape[1]), bf16), V((D, D), bf16)], "grads", flops, 0)


def mate(value):
    return lax.ppermute(value, "narrow", [(0, 1), (1, 0)])


def step(link, value):
    masks = ((8, 4, 1, 2)[link], (4, 8, 2, 1)[link])
    pairs = [(2 * w + n, 2 * (w ^ masks[n]) + n) for w in range(16) for n in range(2)]
    return lax.ppermute(value, AXES, pairs)


def relative(values, bits):
    for place_of, bit in enumerate(reversed(bits)):
        flip = 1 << place_of
        values = [jnp.where(bit > 0, values[i ^ flip], values[i]) for i in range(len(values))]
    return values


def add(*terms):
    return functools.reduce(lambda p, q: p + q, [t.astype(f32) for t in terms])


def regroup(parts, bits):
    mine = relative(parts, bits)
    return relative([mine[0]] + [lax.ppermute(mine[k], AXES, [(i, i ^ k) for i in range(32)]) for k in (1, 2, 3)], bits)


def vector_tables(gains, biases):
    gains = gains.astype(f32).reshape(LAYERS, 2, D)
    biases = biases.astype(f32).reshape(LAYERS, 11, D)
    return jnp.concatenate([gains, biases, jnp.zeros((LAYERS, VECS - 13, D), f32)], 1)


NAMES = ("down", "up", "attn")
LOTS = ((("down", 1),), (("up", 1),), (("attn", 1),), (("down", 0), ("up", 0)), (("attn", 0),))


def whole_weight(matrix, by_rows):
    if by_rows:
        cut = jnp.transpose(matrix.reshape(4, 2, 2, 2, PIECE, D), (3, 1, 2, 0, 4, 5))
    else:
        cut = jnp.transpose(matrix.reshape(4, 2, PIECE, 2, 2, D), (4, 1, 3, 0, 2, 5))
    cut = [cut[0], jnp.swapaxes(cut[1], 0, 1)]
    return [cut[kn][kb] for kb in range(2) for kn in range(2)], 0, by_rows


def whole_grad(core, rest, rows, by_rows):
    near = jnp.stack([jnp.stack([rest[2], rest[1]]), rest[0]])
    cut = jnp.stack([jnp.transpose(near, (1, 0, 3, 2, 4, 5)), core])[..., rows, :]
    if by_rows:
        return jnp.transpose(cut, (3, 4, 2, 1, 0, 5, 6)).reshape(FF, D)
    return jnp.transpose(cut, (3, 4, 2, 5, 1, 0, 6)).reshape(D, FF)


def fetch_plain(w_qkv, w_out, w_up, w_down, gains, biases):
    def whole(value, rows):
        return lax.all_gather(value[None], AXES, axis=1, tiled=True).reshape(rows, -1)

    weights = {}
    for l in range(LAYERS):
        attn = jnp.concatenate([whole(w_qkv[l], D), whole(w_out[l], D)], 1)
        weights["attn", l] = whole_weight(attn, False)
        weights["up", l] = whole_weight(whole(w_up[l], D), False)
        weights["down", l] = whole_weight(whole(w_down[l], FF), True)
    return weights, vector_tables(whole(gains, 1)[0], whole(biases, 1)[0])


class Lot:
    def first(self, core, rest):
        self.core, self.rest = core, rest
        return add(rest[0], core[1]).astype(bf16)

    def second(self, got):
        self.got = got
        return add(self.rest[1], self.core[0, 1], got[1]).astype(bf16)

    def third(self, got):
        total = add(self.rest[2], self.core[0, 0], self.got[0], got)
        self.total = total[0]
        return total[1].astype(bf16)

    def fourth(self, got):
        total = add(self.total, got)
        self.total = total[0]
        return total[1].astype(bf16)

    def last(self, got):
        return add(self.total, got)


def stage(*groups):
    flat, tree = jax.tree.flatten(groups)
    return jax.tree.unflatten(tree, lax.optimization_barrier(flat))


def device_bits():
    wide = lax.axis_index("wide")
    return [(wide >> 3) & 1, (wide >> 2) & 1, (wide >> 1) & 1, wide & 1, lax.axis_index("narrow")]


def coordinates(values):
    return jnp.stack([jnp.asarray(v, jnp.int32) for v in values])


def layer_grads(sums):
    both = jnp.stack(sums)
    return both[:, :2].reshape(-1), both[:, 2:13].reshape(-1)


def gradient_blocks(coords, lot, kept, back, phase):
    items = []
    for name, l in LOTS[lot]:
        if name == "attn":
            items.append((name, [kept[l]["at"], kept[l]["ot"], back[l]["early"], back[l]["late"]], back[l]["flip"], PIECE))
        elif name == "up":
            items.append((name, [kept[l]["bt"]], back[l]["gu"], PIECE))
        else:
            items.append((name, [kept[l]["zt"]], back[l]["gb"], PIECE))
    outs = grads(coords, items, phase)
    return outs[0] if phase else outs


def shares_of(parts, bits):
    rows = D // 32
    cut = jnp.stack(parts)
    whole = jnp.concatenate(regroup([cut[:, s * rows : (s + 1) * rows] for s in range(4)], bits[3:]), 2)
    return [whole[i] for i in range(len(parts))]


def body(tokens, lengths, w_qkv, w_out, w_up, w_down, gains, biases, cotangent):
    args = (tokens, lengths, w_qkv, w_out, w_up, w_down, gains, biases, cotangent)
    if lax.axis_size("wide") == 16 and lax.axis_size("narrow") == 2:
        return staged(*args)
    return plain(*args)


def plain(tokens, lengths, w_qkv, w_out, w_up, w_down, gains, biases, cotangent):
    length = tokens.shape[0] // lengths.shape[0]
    coords = coordinates([0, 0, 0, 0, lengths[0]])
    table = rotary_tables(length)
    weights, vectors = fetch_plain(w_qkv, w_out, w_up, w_down, gains, biases)
    kept, back, wholes, x = [], [{}, {}], [], tokens
    for l in range(LAYERS):
        held, whole = attn_fwd(coords, x, vectors[l], table, [weights[name, l] for name in ("attn", "up", "down")])
        x, more, *_ = ffn_fwd(coords, held, vectors[l], whole[1], whole[2], l == LAYERS - 1)
        kept.append(held | more)
        wholes.append(whole)
    output = ffn_out(coords, kept[-1], x, vectors[-1], wholes[-1][2])
    grad, sums = cotangent, [None] * LAYERS
    for l in reversed(range(LAYERS)):
        last = l == 0
        back[l] = ffn_bwd(coords, grad, kept[l], vectors[l], wholes[l][1], wholes[l][2], not last)
        (back[l]["early"],) = attn_bwd(coords, back[l]["gmb"], kept[l], table, wholes[l][0], EARLY)
        back[l]["late"], back[l]["flip"] = attn_bwd(coords, back[l]["gmb"], kept[l], table, wholes[l][0], LATE)
        grad, more = attn_after(back[l], kept[l], vectors[l], wholes[l][0], last)
        sums[l] = back[l]["sums"] + more
    matrices = {}
    for lot, keys in enumerate(LOTS):
        core, rest = [gradient_blocks(coords, lot, kept, back, phase) for phase in (1, 0)]
        for i, key in enumerate(keys):
            rows = slice(i * PIECE, (i + 1) * PIECE)
            matrices[key] = whole_grad(core, rest, rows, key[0] == "down").astype(f32)
    devices = lax.axis_size(AXES)
    parts = []
    for name, begin, end in (("attn", 0, 3 * D), ("attn", 3 * D, FF), ("up", 0, FF), ("down", 0, D)):
        parts += [matrices[name, l][:, begin:end].reshape(devices, -1) for l in range(LAYERS)]
    parts += [v.reshape(devices, -1) for v in layer_grads(sums)]
    summed = lax.psum_scatter(jnp.concatenate(parts, 1), AXES, scatter_dimension=0, tiled=True)[0]
    ends = np.cumsum([p.shape[1] for p in parts])
    cut = [summed[end - p.shape[1] : end] for end, p in zip(ends, parts, strict=True)]
    outs = [jnp.stack(cut[i : i + LAYERS]) for i in range(0, 4 * LAYERS, LAYERS)] + cut[4 * LAYERS :]
    return (output, grad, *outs)


def turned(value, bits):
    value = value.reshape(2, 2, 2, 2, 2, -1)
    for axis, bit in enumerate(bits):
        value = jnp.where(bit > 0, jnp.flip(value, axis), value)
    cores = [jnp.transpose(value, order) for order in ((4, 2, 3, 1, 0, 5), (4, 3, 2, 0, 1, 5))]
    own = jnp.where(bits[4] > 0, cores[1][0], cores[0][0])
    other = jnp.where(bits[4] > 0, cores[0][1], cores[1][1])
    return jnp.stack([own, other])


def ordered(bit, own, got):
    return jnp.stack([jnp.where(bit > 0, got, own), jnp.where(bit > 0, own, got)])


def staged(tokens, lengths, w_qkv, w_out, w_up, w_down, gains, biases, cotangent):
    length = tokens.shape[0] // lengths.shape[0]
    bits = device_bits()
    coords = coordinates([lax.axis_index("wide") >> 2, *bits[2:], lengths[0]])
    table = rotary_tables(length)
    rows = D // 32
    weights, whole = {}, {}

    z1, z0, y, x, n = bits
    third, fourth = jnp.where(n > 0, y, x), jnp.where(n > 0, x, y)

    def link0(value):
        return ordered(jnp.where(n > 0, z0, z1), value, step(0, value))

    def link1(value):
        return value, step(1, value)

    def by_z(pair):
        own, got = pair
        blocks = []
        for high in range(2):
            for low in range(2):
                core0 = jnp.where(z0 == low, own[high], got[high])
                blocks.append(jnp.where(n > 0, jnp.where(z1 == high, own[low], got[low]), core0))
        return jnp.stack(blocks)

    def link2(value):
        return ordered(third, value, step(2, value))

    def arrived(keys, *pieces):
        offset = 0
        for key, height in keys:
            weights[key] = (list(pieces), offset, key[0] == "down")
            offset += height

    small = jnp.concatenate([gains, biases])
    width = small.shape[0]
    c0 = jnp.concatenate([w_down[0].reshape(PIECE, D), jnp.zeros((16, D), bf16).at[0, :width].set(small)])
    c0, w_qkv, w_out, w_up = stage(c0, w_qkv, w_out, w_up)
    t0 = link0(c0)
    flat = []
    for l in range(LAYERS):
        flat.append(jnp.concatenate([w_qkv[l].reshape(rows, 3 * D), w_out[l].reshape(rows, D)], 1))
        flat.append(w_up[l].reshape(rows, FF))
    flat = jnp.stack(flat)
    parts = [flat[:, :, s * D : (s + 1) * D] for s in range(4)]
    t0, parts = stage(t0, parts)
    u0 = link1(t0)
    c1, up0, attn1, up1 = jnp.concatenate(regroup(parts, bits[3:]), 1)
    c2, c3 = jnp.concatenate([up0, attn1]), jnp.concatenate([w_down[1].reshape(PIECE, D), up1])
    zz0, c1, c2, c3 = stage(by_z(u0), c1, c2, c3)
    near0, t12 = stage(link2(zz0), link0(jnp.concatenate([c1, c2])))
    t1, t2 = t12[:, :PIECE], t12[:, PIECE:]
    far0, mate0, u1 = step(3, near0), mate(near0), link1(t1)
    far0, mate0, zz1, t2 = stage(far0, mate0, by_z(u1), t2)
    near1, far_mate0, u2, t3 = link2(zz1), mate(far0), link1(t2), link0(c3)
    near1, far_mate0, t3 = stage(near1, far_mate0, t3)
    zz2 = by_z(u2)
    arrived(((("down", 0), PIECE),), near0, mate0, far0, far_mate0)
    far1, mate1, near2, u3 = step(3, near1), mate(near1), link2(zz2), link1(t3)
    whole["down", 0] = assemble(coords, weights["down", 0])
    own, other = [], []
    for first, second, to in ((near0, far0, own), (mate0, far_mate0, other)):
        turn = n if to is own else 1 - n
        both = ordered(jnp.where(turn > 0, x, y), first[:, :, PIECE, :width], second[:, :, PIECE, :width])
        to.append(jnp.where(turn > 0, jnp.transpose(both, (2, 1, 0, 3)), jnp.transpose(both, (2, 0, 1, 3))))
    both = ordered(n, own[0], other[0])
    both = jnp.transpose(both, (1, 2, 3, 0, 4)).reshape(32, width)
    vectors = vector_tables(both[:, : gains.shape[0]].reshape(-1), both[:, gains.shape[0] :].reshape(-1))
    far1, mate1, near2, zz3, vectors, whole = stage(far1, mate1, near2, by_z(u3), vectors, whole)
    far_mate1, near2, zz3 = stage(mate(far1), near2, zz3)
    arrived(((("attn", 0), PIECE),), near1, mate1, far1, far_mate1)
    kept, back = [None, None], [None, None]
    far2, mate2 = step(3, near2), mate(near2)
    kept[0], got = attn_fwd(coords, tokens, vectors[0], table, [weights["attn", 0]])
    whole["attn", 0] = got[0]
    far2, mate2, kept[0] = stage(far2, mate2, kept[0])
    far_mate2, kept[0], zz3 = stage(mate(far2), kept[0], zz3)
    arrived(((("up", 0), PIECE), (("attn", 1), PIECE)), near2, mate2, far2, far_mate2)
    got3 = step(2, zz3)
    h, more, whole["up", 0], _ = ffn_fwd(coords, kept[0], vectors[0], weights["up", 0], whole["down", 0], False)
    kept[0] |= more
    got3, h = stage(got3, h)
    near3, h = stage(ordered(third, zz3, got3), h)
    far3, mate3 = step(3, near3), mate(near3)
    kept[1], got = attn_fwd(coords, h, vectors[1], table, [weights["attn", 1]])
    whole["attn", 1] = got[0]
    far3, mate3, kept[1] = stage(far3, mate3, kept[1])
    arrived(((("down", 1), PIECE), (("up", 1), PIECE)), near3, mate3, far3, mate(far3))
    hidden, more, whole["up", 1], whole["down", 1] = ffn_fwd(
        coords, kept[1], vectors[1], weights["up", 1], weights["down", 1], True
    )
    kept[1] |= more

    d1, u1, a1, du0, a0, extra = [Lot() for _ in range(6)]

    def blocks(lot, phase):
        return gradient_blocks(coords, lot, kept, back, phase)

    live = jnp.arange(length, dtype=jnp.int32)[:, None] < lengths[0]
    back[1] = {"gb": jnp.where(live, cotangent, jnp.zeros((), bf16))}
    core, back[1] = stage(blocks(0, 1), back[1])
    first, cotangent = stage(d1.first(mate(core), blocks(0, 0)), cotangent)

    got_d1 = step(3, first)
    back[1] |= ffn_bwd(coords, cotangent, kept[1], vectors[1], whole["up", 1], whole["down", 1], True)
    got_d1, core, back[1] = stage(got_d1, blocks(1, 1), back[1])
    second, core, back[1] = stage(d1.second(got_d1), core, back[1])

    got_d1 = step(2, second)
    core, rest = stage(mate(core), blocks(1, 0))
    first, back[1] = stage(u1.first(core, rest), back[1])

    got_u1 = step(3, first)
    (back[1]["early"],) = attn_bwd(coords, back[1]["gmb"], kept[1], table, whole["attn", 1], EARLY)
    got_u1, got_d1, back[1] = stage(got_u1, got_d1, back[1])
    second, third, back[1] = stage(u1.second(got_u1), d1.third(got_d1), back[1])

    got_u1, got_d1 = step(2, second), step(1, third)
    back[1]["late"], back[1]["flip"] = attn_bwd(coords, back[1]["gmb"], kept[1], table, whole["attn", 1], LATE)
    got_u1, got_d1, core, back[1] = stage(got_u1, got_d1, blocks(2, 1), back[1])
    third, fourth, core, back[1] = stage(u1.third(got_u1), d1.fourth(got_d1), core, back[1])

    got_u1, got_d1 = step(1, third), step(0, fourth)
    core, rest = stage(mate(core), blocks(2, 0))
    first, back[1] = stage(a1.first(core, rest), back[1])

    got_a1 = step(3, first)
    grad, more = attn_after(back[1], kept[1], vectors[1], whole["attn", 1], False)
    sums = [None, back[1]["sums"] + more]
    back[0] = ffn_bwd(coords, grad, kept[0], vectors[0], whole["up", 0], whole["down", 0], False)
    got_a1, got_u1, got_d1, core, back[0] = stage(got_a1, got_u1, got_d1, blocks(3, 1), back[0])
    second, fourth, core, back[0] = stage(a1.second(got_a1), u1.fourth(got_u1), core, back[0])

    got_a1, got_u1, core, rest = stage(step(2, second), step(0, fourth), mate(core), blocks(3, 0))
    first, third, back[0] = stage(du0.first(core, rest), a1.third(got_a1), back[0])

    got_du0, got_a1 = step(3, first), step(1, third)
    (back[0]["early"],) = attn_bwd(coords, back[0]["gmb"], kept[0], table, whole["attn", 0], EARLY)
    back[0]["late"], back[0]["flip"] = attn_bwd(coords, back[0]["gmb"], kept[0], table, whole["attn", 0], LATE)
    got_du0, got_a1, back[0] = stage(got_du0, got_a1, back[0])
    second, fourth, back[0], hidden = stage(du0.second(got_du0), a1.fourth(got_a1), back[0], hidden)

    got_du0, got_a1 = step(2, second), step(0, fourth)
    core = blocks(4, 1)
    grad, more = attn_after(back[0], kept[0], vectors[0], whole["attn", 0], True)
    sums[0] = back[0]["sums"] + more
    output = ffn_out(coords, kept[1], hidden, vectors[1], whole["down", 1])
    got_du0, got_a1, core, grad, sums, back[0], output = stage(got_du0, got_a1, core, grad, sums, back[0], output)
    third, core, back[0] = stage(du0.third(got_du0), core, back[0])

    got_du0 = step(1, third)
    core, rest = stage(mate(core), blocks(4, 0))
    first, sums = stage(a0.first(core, rest), sums)

    got_a0 = step(3, first)
    small = turned(jnp.concatenate([v.reshape(32, -1) for v in layer_grads(sums)], 1), bits)
    first = extra.first(mate(small[1]), [small[0, 1], small[0, 0, 1], small[0, 0, 0]])
    got_a0, got_du0, first, got_d1, got_u1, got_a1, grad = stage(got_a0, got_du0, first, got_d1, got_u1, got_a1, grad)
    second, first, fourth = stage(a0.second(got_a0), first, du0.fourth(got_du0))

    got_a0, got_x, got_du0 = step(2, second), step(3, first), step(0, fourth)
    shares = [u1.last(got_u1), a1.last(got_a1)]
    got_a0, got_x, got_du0, shares = stage(got_a0, got_x, got_du0, shares)
    third, second, got_du0 = stage(a0.third(got_a0), extra.second(got_x), got_du0)

    got_a0, got_x = step(1, third), step(2, second)
    done = du0.last(got_du0)
    downs = jnp.stack([done[:PIECE].reshape(-1), d1.last(got_d1).reshape(-1)])
    up1, attn1, up0 = shares_of([*shares, done[PIECE:]], bits)
    got_a0, got_x, up1, attn1, up0, downs = stage(got_a0, got_x, up1, attn1, up0, downs)
    fourth, third = stage(a0.fourth(got_a0), extra.third(got_x))

    got_a0, got_x = step(0, fourth), step(1, third)
    ups = jnp.stack([up0.reshape(-1), up1.reshape(-1)])
    got_a0, got_x, ups = stage(got_a0, got_x, ups)
    (attn0,) = shares_of([a0.last(got_a0)], bits)
    mine = extra.last(step(0, extra.fourth(got_x)))
    return (
        output,
        grad,
        jnp.stack([v[:, : 3 * D].reshape(-1) for v in (attn0, attn1)]),
        jnp.stack([v[:, 3 * D :].reshape(-1) for v in (attn0, attn1)]),
        ups,
        downs,
        mine[: gains.shape[0]],
        mine[gains.shape[0] :],
    )


def solution(mesh):
    both, flat, rows = P(AXES), P(None, AXES), P(AXES, None)
    return jax.shard_map(
        body,
        mesh=mesh,
        in_specs=(rows, both, flat, flat, flat, flat, both, both, rows),
        out_specs=(rows, rows, flat, flat, flat, flat, both, both),
        check_vma=False,
    )
```

```python
import functools

import jax
import jax.numpy as jnp
import numpy as np
from jax import lax
from jax.experimental import pallas as pl
from jax.experimental.pallas import tpu as pltpu
from jax.sharding import PartitionSpec as P

D = 640
HEADS = 20
HEAD_DIM = 32
FF = 2560
LAYERS = 2
EPSILON = 1e-05
MASKED = -1e9
LANES = 128
GROUPS = D // LANES
PER_GROUP = LANES // HEAD_DIM
BLOCKS = FF // D
EARLY, LATE = (0, 3), (3, 2)
PIECE = 80
VECS = 16
AXES = ("wide", "narrow")
WHOLE, WHOLE_ROWS = (4, 2, PIECE, FF), (4, 2, 2, 2, PIECE, D)
SLACK = 8 * 1024 * 1024
f32, bf16 = jnp.float32, jnp.bfloat16

GAIN_A, GAIN_F, SHIFT_A, BIAS_QKV, BIAS_OUT, SHIFT_F, BIAS_UP, BIAS_DOWN = 0, 1, 2, 3, 6, 7, 8, 12


def rotary_tables(length):
    half = HEAD_DIM // 2
    inverse = 1.0 / 10000.0 ** (np.arange(half) * (2.0 / HEAD_DIM))
    angles = np.arange(length)[:, None] * inverse[None, :]
    cos, sine = np.cos(angles), np.sin(angles)
    none = np.zeros_like(sine)
    ahead = np.tile(np.concatenate([-sine, none], 1), (1, PER_GROUP))
    behind = np.tile(np.concatenate([none, sine], 1), (1, PER_GROUP))
    wide = np.stack([np.tile(cos, (1, 2 * PER_GROUP)), ahead, behind]).astype(np.float32)
    return jnp.asarray(wide), jnp.asarray(np.stack([cos.T, sine.T]).astype(np.float32))


def dot(left, right):
    return jnp.dot(left, right, preferred_element_type=f32)


def dot_nt(left, right):
    return lax.dot_general(left, right, (((1,), (1,)), ((), ())), preferred_element_type=f32)


def dot_tn(left, right):
    return lax.dot_general(left, right, (((0,), (0,)), ((), ())), preferred_element_type=f32)


def rotated(value, table):
    half = HEAD_DIM // 2
    return value * table[0] + pltpu.roll(value, LANES - half, 1) * table[1] + pltpu.roll(value, half, 1) * table[2]


def rotated_back(value, table):
    half = HEAD_DIM // 2
    first, second = value[:half], value[half:]
    return jnp.concatenate([first * table[0] + second * table[1], second * table[0] - first * table[1]], 0)


def unit_of(value):
    centered = value - jnp.mean(value, -1, keepdims=True)
    inverse = lax.rsqrt(jnp.mean(centered * centered, -1, keepdims=True) + EPSILON)
    return centered * inverse, inverse


def norm_back(grad, unit, inverse, gain):
    scaled = grad * gain
    return inverse * (scaled - jnp.mean(scaled, -1, keepdims=True) - unit * jnp.mean(scaled * unit, -1, keepdims=True))


def column_sum(value):
    return jnp.sum(value, 0, keepdims=True)


def gelu_parts(value):
    scaled = jnp.abs(value) * 0.7071067811865476
    t = 1.0 / (1.0 + 0.3275911 * scaled)
    bell = jnp.exp(-scaled * scaled)
    series = t * (0.127414796 + t * (-0.142248368 + t * (0.7107068705 + t * (-0.7265760135 + t * 0.5307027145))))
    tail = series * bell
    return jnp.where(value >= 0.0, 1.0 - tail, tail), bell * 0.3989422804014327


def row_loop(length, step, body):
    def run(i, carry):
        body(pl.ds(pl.multiple_of(i * step, step), step), i)
        return carry

    lax.fori_loop(0, length // step, run, 0)


def owner_of(coords, kn, kb, ka, k2, k1):
    n = coords[3] ^ kn
    z = coords[0] ^ (2 * k1 + k2 + n * (k2 - k1))
    return z, coords[1] ^ (kb + n * (ka - kb)), coords[2] ^ (ka + n * (kb - ka)), n


PLACES = [(ka, k2, k1) for ka in range(2) for k2 in range(2) for k1 in range(2)]


class Assembly:
    def __init__(self, coords, by_rows, pieces, offset, whole, sems):
        self.by_rows, self.whole, self.sems = by_rows, whole, sems
        self.any = pieces[0].at[0, :, pl.ds(offset, PIECE)]
        for kb in range(2):
            for kn in range(2):
                n = coords[3] ^ kn
                b = (coords[1] + n * (coords[2] - coords[1])) ^ kb
                for a in range(2):
                    target = self.target(a + n * (b - a), b + n * (a - b), n)
                    pltpu.make_async_copy(pieces[2 * kb + kn].at[a, :, pl.ds(offset, PIECE)], *target).start()

    def target(self, x, y, n):
        to = (y, x, n) if self.by_rows else (y, slice(None), pl.ds(pl.multiple_of((2 * x + n) * D, D), D))
        return self.whole.at[(slice(None), *to)], self.sems.at[4 * x + 2 * n + y]

    def wait(self, quarters=(0, 1, 2, 3)):
        for quarter in quarters:
            for y in range(2):
                pltpu.make_async_copy(self.any, *self.target(quarter // 2, y, quarter % 2)).wait()


def head_masks():
    lane = lax.broadcasted_iota(jnp.int32, (1, LANES), 1)
    return [(lane // HEAD_DIM == head).astype(f32).astype(bf16) for head in range(PER_GROUP)]


def masked_tail(length, live):
    row = lax.broadcasted_iota(jnp.int32, (length, LANES), 0)
    lane = lax.broadcasted_iota(jnp.int32, (length, LANES), 1)
    keys = jnp.where((lane == 0) & (row >= live), MASKED, 0.0).astype(bf16)
    row = lax.broadcasted_iota(jnp.int32, (LANES, length), 0)
    return keys, jnp.where(row == 0, 1.0, 0.0).astype(bf16)


def attn_fwd_kernel(plan, coords, x_ref, vec_ref, table_ref, *refs):
    count = len(plan)
    pieces, refs = refs[: 4 * count], refs[4 * count :]
    at_ref, qt_ref, kv_ref, ot_ref, lse_ref, m_ref, b_ref, bt_ref, *refs = refs
    wholes, refs = refs[:count], refs[count:]
    a_ref, q_ref, key_ref, query_ref, sems = refs
    length = x_ref.shape[0]
    jobs = [
        Assembly(coords, by_rows, pieces[4 * i : 4 * i + 4], offset, wholes[i], sems.at[i])
        for i, (offset, by_rows) in enumerate(plan)
    ]
    w_ref = wholes[0]

    def norm(rows, _):
        unit, _ = unit_of(x_ref[rows, :].astype(f32))
        a_ref[rows, :] = (unit * vec_ref[GAIN_A : GAIN_A + 1, :] + vec_ref[SHIFT_A : SHIFT_A + 1, :]).astype(bf16)

    row_loop(length, 128, norm)
    normed = a_ref[...]
    at_ref[...] = normed.T
    for part in range(3):
        jobs[0].wait([part])
        out = dot(normed, w_ref[:, :, :, part * D : (part + 1) * D].reshape(D, D)) + vec_ref[BIAS_QKV + part : BIAS_QKV + part + 1, :]
        if part == 0:
            out = out * HEAD_DIM**-0.5
        for group in range(GROUPS):
            lanes = slice(group * LANES, (group + 1) * LANES)
            piece = out[:, lanes]
            if part < 2:
                piece = rotated(piece, table_ref)
            if part == 0:
                qt_ref[lanes, :] = piece.astype(bf16).T
            else:
                kv_ref[:, (part - 1) * D + group * LANES : (part - 1) * D + (group + 1) * LANES] = piece.astype(bf16)
    masks = head_masks()
    tail, query_ref[LANES:, :] = masked_tail(length, coords[4])
    for head in range(PER_GROUP):
        key_ref[head, :, LANES:] = tail
    ones = jnp.ones((16, length), bf16)

    def group_step(group, carry):
        rows = pl.ds(pl.multiple_of(group * LANES, LANES), LANES)
        query_ref[:LANES, :] = qt_ref[rows, :]
        values = kv_ref[:, pl.ds(pl.multiple_of(D + group * LANES, LANES), LANES)].T
        for head in range(PER_GROUP):
            key_ref[head, :, :LANES] = kv_ref[:, rows] * masks[head]
        every = dot(key_ref[...].reshape(PER_GROUP * length, 2 * LANES), query_ref[...])
        for head in range(PER_GROUP):
            scores = every[head * length : (head + 1) * length]
            top = jnp.max(scores, 0, keepdims=True)
            probs = jnp.exp(scores - top).astype(bf16)
            wide = jnp.concatenate([values[head * HEAD_DIM : (head + 1) * HEAD_DIM], ones], 0)
            out = dot(wide, probs)
            total = out[HEAD_DIM : HEAD_DIM + 1]
            to = pl.ds(pl.multiple_of(group * LANES + head * HEAD_DIM, HEAD_DIM), HEAD_DIM)
            ot_ref[to, :] = (out[:HEAD_DIM] / total).astype(bf16)
            lse_ref[pl.ds(group * PER_GROUP + head, 1), :] = top + jnp.log(total)
        return carry

    for group in range(GROUPS):
        group_step(group, 0)
    jobs[0].wait([3])
    q_ref[...] = ot_ref[...].T
    m_ref[...] = x_ref[...].astype(f32) + (dot(q_ref[...], w_ref[:, :, :, 3 * D :].reshape(D, D)) + vec_ref[BIAS_OUT : BIAS_OUT + 1, :])

    def after(rows, _):
        unit, _ = unit_of(m_ref[rows, :])
        b_ref[rows, :] = (unit * vec_ref[GAIN_F : GAIN_F + 1, :] + vec_ref[SHIFT_F : SHIFT_F + 1, :]).astype(bf16)

    row_loop(length, 128, after)
    bt_ref[...] = b_ref[...].T
    for job in jobs[1:]:
        job.wait()


def assemble_kernel(offset, by_rows, coords, *refs):
    Assembly(coords, by_rows, refs[:4], offset, refs[4], refs[5]).wait()


def ffn_fwd_kernel(offsets, last, coords, m_ref, b_ref, vec_ref, *refs):
    offset, offset_down = offsets
    if offset is None:
        up_ref, down_ref, y_ref, zt_ref, slope_ref, *rest = refs
    elif offset_down is None:
        down_ref, *pieces, y_ref, zt_ref, slope_ref, up_ref = refs[:9]
        rest = refs[9:]
    else:
        *pieces, y_ref, zt_ref, slope_ref, up_ref, down_ref = refs[:9]
        rest = refs[9:]
    z_ref = y_ref if last else rest[0]
    sems = rest[-1] if rest else None
    if offset is not None:
        job = Assembly(coords, False, pieces, offset, up_ref, sems.at[0])
    if offset_down is not None:
        job_down = Assembly(coords, True, pieces, offset_down, down_ref, sems.at[1])
    normed = b_ref[...]
    for block in range(BLOCKS):
        if offset is not None:
            job.wait([block])
        columns = slice(block * D, (block + 1) * D)
        part = up_ref[:, columns] if offset is None else up_ref[:, :, :, columns].reshape(D, D)
        pre = dot(normed, part) + vec_ref[BIAS_UP + block : BIAS_UP + block + 1, :]
        cdf, bell = gelu_parts(pre)
        z_ref[:, columns] = (pre * cdf).astype(bf16)
        slope_ref[:, columns] = (cdf + pre * bell).astype(bf16)
        zt_ref[columns, :] = z_ref[:, columns].T
    if offset_down is not None:
        job_down.wait()
    if not last:
        y_ref[...] = m_ref[...] + (dot(z_ref[...], down_ref[...].reshape(FF, D)) + vec_ref[BIAS_DOWN : BIAS_DOWN + 1, :])


def ffn_out_kernel(coords, m_ref, z_ref, vec_ref, down_ref, y_ref):
    out = m_ref[...] + (dot(z_ref[...], down_ref[...]) + vec_ref[BIAS_DOWN : BIAS_DOWN + 1, :])
    row = lax.broadcasted_iota(jnp.int32, (m_ref.shape[0], 1), 0)
    y_ref[...] = jnp.where(row < coords[4], out, 0.0).astype(bf16)


def ffn_bwd_kernel(top, coords, g_ref, slope_ref, m_ref, vec_ref, up_ref, down_ref, *refs):
    gb_ref, gu_ref, gm_ref, gmb_ref, sums_ref = refs
    length = m_ref.shape[0]
    sums_ref[...] = jnp.zeros_like(sums_ref)

    def add(row, value):
        sums_ref[row : row + 1, :] += column_sum(value)

    grad = g_ref[...].astype(f32)
    if top:
        row = lax.broadcasted_iota(jnp.int32, (length, 1), 0)
        grad = jnp.where(row < coords[4], grad, 0.0)
    low = grad.astype(bf16)
    gb_ref[...] = low
    add(BIAS_DOWN, low.astype(f32))
    for block in range(BLOCKS):
        columns = slice(block * D, (block + 1) * D)
        part = (dot_nt(low, down_ref[columns, :]) * slope_ref[:, columns].astype(f32)).astype(bf16)
        gu_ref[:, columns] = part
        add(BIAS_UP + block, part.astype(f32))
    gm_ref[...] = dot_nt(gu_ref[...], up_ref[...])

    def after(rows, i):
        normed_grad = gm_ref[rows, :]
        unit, inverse = unit_of(m_ref[rows, :])
        add(GAIN_F, normed_grad * unit)
        add(SHIFT_F, normed_grad)
        grad = g_ref[rows, :].astype(f32)
        if top:
            row = lax.broadcasted_iota(jnp.int32, (128, 1), 0) + i * 128
            grad = jnp.where(row < coords[4], grad, 0.0)
        middle = grad + norm_back(normed_grad, unit, inverse, vec_ref[GAIN_F : GAIN_F + 1, :])
        gm_ref[rows, :] = middle
        low = middle.astype(bf16)
        gmb_ref[rows, :] = low
        add(BIAS_OUT, low.astype(f32))

    row_loop(length, 128, after)


def attn_bwd_kernel(groups, coords, gmb_ref, qt_ref, kv_ref, ot_ref, lse_ref, table_ref, w_ref, *refs):
    start, count = groups
    gp_ref, *flip_ref, go_ref, key_ref, query_ref = refs
    length = gmb_ref.shape[0]
    low = gmb_ref[...]
    if flip_ref:
        flip_ref[0][...] = low.T
    go_ref[...] = dot_nt(w_ref[start * LANES : (start + count) * LANES, 3 * D :], low).astype(bf16)
    masks = head_masks()
    tail, query_ref[LANES:, :] = masked_tail(length, coords[4])
    for head in range(PER_GROUP):
        key_ref[head, :, LANES:] = tail

    def group_step(i, carry):
        group = i + start
        rows = pl.ds(pl.multiple_of(group * LANES, LANES), LANES)
        query, grad = qt_ref[rows, :], go_ref[pl.ds(pl.multiple_of(i * LANES, LANES), LANES), :]
        query_ref[:LANES, :] = query
        keys = kv_ref[:, rows]
        values = kv_ref[:, pl.ds(pl.multiple_of(D + group * LANES, LANES), LANES)]
        flipped = keys.T
        products = grad.astype(f32) * ot_ref[rows, :].astype(f32)
        for head in range(PER_GROUP):
            key_ref[head, :, :LANES] = keys * masks[head]
        for head in range(PER_GROUP):
            part = slice(head * HEAD_DIM, (head + 1) * HEAD_DIM)
            delta = column_sum(products[part])
            probs = jnp.exp(dot(key_ref[head], query_ref[...]) - lse_ref[pl.ds(group * PER_GROUP + head, 1), :])
            scores = (probs * (dot(values * masks[head], grad) - delta)).astype(bf16)
            dv = dot_nt(grad[part], probs.astype(bf16))
            dk = dot_nt(query[part], scores)
            dq = dot(flipped[part], scores)
            to = pl.ds(pl.multiple_of(i * LANES + head * HEAD_DIM, HEAD_DIM), HEAD_DIM)
            dq = rotated_back(dq.astype(bf16).astype(f32), table_ref) * HEAD_DIM**-0.5
            dk = rotated_back(dk.astype(bf16).astype(f32), table_ref)
            for part, value in enumerate((dq, dk, dv)):
                gp_ref[part, to, :] = value.astype(bf16)
        return carry

    lax.fori_loop(0, count, group_step, 0)


def attn_after_kernel(early_ref, late_ref, gm_ref, x_ref, vec_ref, w_ref, *refs):
    gx_ref, sums_ref, ga_ref = refs
    length = x_ref.shape[0]
    sums_ref[...] = jnp.zeros_like(sums_ref)

    def add(row, value):
        sums_ref[row : row + 1, :] += column_sum(value)

    ones = jnp.ones((16, length), bf16)
    total = 0.0
    for part in range(3):
        for ref, (start, count) in ((early_ref, EARLY), (late_ref, LATE)):
            columns = slice(start * LANES, (start + count) * LANES)
            sums_ref[BIAS_QKV + part : BIAS_QKV + part + 1, columns] = dot_nt(ones, ref[part])[:1]
            total = total + dot(w_ref[:, part * D + start * LANES : part * D + (start + count) * LANES], ref[part])
    ga_ref[...] = total.T

    def after(rows, _):
        normed_grad = ga_ref[rows, :]
        unit, inverse = unit_of(x_ref[rows, :].astype(f32))
        add(GAIN_A, normed_grad * unit)
        add(SHIFT_A, normed_grad)
        out = gm_ref[rows, :] + norm_back(normed_grad, unit, inverse, vec_ref[GAIN_A : GAIN_A + 1, :])
        gx_ref[rows, :] = out.astype(gx_ref.dtype)

    row_loop(length, 128, after)


def grads_kernel(items, inputs, phase, coords, *refs):
    ins, outs, (left_ref, whole_ref) = refs[:inputs], refs[inputs:-2], refs[-2:]

    def put(value, kb, ka, k2, k1, to):
        to = slice(to, to + value.shape[0])
        if phase:
            outs[0][kb, ka, k2, k1, to] = value
        elif kb:
            outs[0][ka, k2, k1, to] = value
        elif ka:
            outs[1][k2, k1, to] = value
        else:
            outs[2][k2, k1, to] = value

    for kind, lefts, right, to in items:
        if kind == "down":
            for kb in range(2):
                for place, (ka, k2, k1) in enumerate(PLACES):
                    z, y, x, n = owner_of(coords, phase, kb, ka, k2, k1)
                    start = pl.multiple_of((8 * z + 4 * y + 2 * x + n) * PIECE, PIECE)
                    left_ref[place * PIECE : (place + 1) * PIECE, :] = ins[lefts[0]][pl.ds(start, PIECE), :]
                whole = dot(left_ref[...], ins[right][...]).astype(bf16)
                for place, (ka, k2, k1) in enumerate(PLACES):
                    put(whole[place * PIECE : (place + 1) * PIECE], kb, ka, k2, k1, to)
        else:
            for kx in range(2):
                quarter = 2 * (coords[2] ^ kx) + (coords[3] ^ phase)
                n = coords[3] ^ phase
                for ky in range(2):
                    for kz in range(4):
                        k2, k1 = kz // 2, kz % 2
                        z = coords[0] ^ (2 * k1 + k2 + n * (k2 - k1))
                        start = pl.multiple_of((2 * z + (coords[1] ^ ky)) * PIECE, PIECE)
                        to_row = (4 * ky + kz) * PIECE
                        if kind == "up":
                            part = ins[lefts[0]][pl.ds(start, PIECE), :]
                        else:
                            part = jnp.where(quarter == 3, ins[lefts[1]][pl.ds(start, PIECE), :], ins[lefts[0]][pl.ds(start, PIECE), :])
                        left_ref[to_row : to_row + PIECE, :] = part
                if kind == "attn":

                    @pl.when(quarter == 3)
                    def _(right=right):
                        whole_ref[...] = dot_nt(left_ref[...], ins[right][...]).astype(bf16)

                    @pl.when(quarter < 3)
                    def _(right=right, quarter=quarter):
                        part = jnp.minimum(quarter, 2)
                        for i, (start, count) in ((2, EARLY), (1, LATE)):
                            columns = slice(start * LANES, (start + count) * LANES)
                            whole_ref[:, columns] = dot_nt(left_ref[...], ins[right - i][part]).astype(bf16)

                else:
                    columns = pl.ds(pl.multiple_of(quarter * D, D), D)
                    whole_ref[...] = dot(left_ref[...], ins[right][:, columns]).astype(bf16)

                def write(swapped, kx=kx, to=to):
                    for ky in range(2):
                        for kz in range(4):
                            start = (4 * ky + kz) * PIECE
                            ka, kb = (ky, kx) if swapped else (kx, ky)
                            put(whole_ref[start : start + PIECE, :], kb, ka, kz // 2, kz % 2, to)

                pl.when(n == 0)(functools.partial(write, False))
                pl.when(n == 1)(functools.partial(write, True))


def call(kernel, ins, outs, scratch, name, flops, exps=0):
    moved = sum(a.size * a.dtype.itemsize for a, _ in ins) + sum(int(np.prod(s)) * jnp.dtype(t).itemsize for s, t in outs)
    limit = SLACK + sum(int(np.prod(t.shape)) * t.dtype.itemsize for t in scratch if t.memory_space == V)
    return pl.pallas_call(
        kernel,
        out_shape=[jax.ShapeDtypeStruct(s, t) for s, t in outs],
        in_specs=[pl.BlockSpec(memory_space=space) for _, space in ins],
        out_specs=[pl.BlockSpec(memory_space=pltpu.VMEM)] * len(outs),
        scratch_shapes=scratch,
        compiler_params=pltpu.CompilerParams(vmem_limit_bytes=limit),
        cost_estimate=pl.CostEstimate(flops=int(flops), bytes_accessed=int(moved), transcendentals=int(exps)),
        name=name,
    )(*[a for a, _ in ins])


V, S, H = pltpu.VMEM, pltpu.SMEM, pl.ANY
SEMS = pltpu.SemaphoreType.DMA


def attn_fwd(coords, x, vec, table, weights):
    n = x.shape[0]
    ins = [(coords, S), (x, V), (vec, V), (table[0], V)] + [(p, H) for w in weights for p in w[0]]
    outs = [((D, n), bf16), ((D, n), bf16), ((n, 2 * D), bf16), ((D, n), bf16), ((24, n), f32)]
    outs += [((n, D), f32), ((n, D), bf16), ((D, n), bf16)]
    outs += [(WHOLE_ROWS if w[2] else WHOLE, bf16) for w in weights]
    scratch = [V((n, D), bf16), V((n, D), bf16), V((PER_GROUP, n, 2 * LANES), bf16), V((2 * LANES, n), bf16)]
    scratch.append(SEMS((len(weights), 8)))
    kernel = functools.partial(attn_fwd_kernel, [w[1:] for w in weights])
    out = call(kernel, ins, outs, scratch, "attn_fwd", 2 * n * D * FF + 4 * n * n * D, HEADS * n * n)
    return dict(zip(("at", "qt", "kv", "ot", "lse", "m", "b", "bt"), out[:8], strict=True)) | {"x": x}, [w.reshape((FF, D) if w.ndim == 6 else (D, FF)) for w in out[8:]]


def assemble(coords, weight):
    pieces, offset, by_rows = weight
    outs = [(WHOLE_ROWS if by_rows else WHOLE, bf16)]
    ins = [(coords, S)] + [(p, H) for p in pieces]
    out = call(functools.partial(assemble_kernel, offset, by_rows), ins, outs, [SEMS((8,))], "assemble", 0)[0]
    return out.reshape((FF, D) if by_rows else (D, FF))


def ffn_fwd(coords, kept, vec, up, down, last):
    n = kept["m"].shape[0]
    parts = [isinstance(w, tuple) for w in (up, down)]
    ins = [(coords, S), (kept["m"], V), (kept["b"], V), (vec, V)]
    ins += [(w, V) for w, part in zip((up, down), parts) if not part]
    ins += [(p, H) for p in up[0]] if parts[0] else []
    outs = [((n, FF), bf16) if last else ((n, D), f32), ((FF, n), bf16), ((n, FF), bf16)]
    outs += [(shape, bf16) for shape, part in zip((WHOLE, WHOLE_ROWS), parts) if part]
    scratch = ([] if last else [V((n, FF), bf16)]) + ([SEMS((2, 8))] if parts[0] else [])
    offsets = [w[1] if part else None for w, part in zip((up, down), parts)]
    kernel = functools.partial(ffn_fwd_kernel, offsets, last)
    y, zt, slope, *more = call(kernel, ins, outs, scratch, "ffn_fwd", 4 * n * D * FF, 2 * n * FF)
    up = more[0].reshape(D, FF) if parts[0] else up
    down = more[1].reshape(FF, D) if parts[1] else down
    return y, {"zt": zt, "slope": slope}, up, down


def ffn_out(coords, kept, hidden, vec, down):
    ins = [(coords, S)] + [(a, V) for a in (kept["m"], hidden, vec, down)]
    return call(ffn_out_kernel, ins, [(kept["m"].shape, bf16)], [], "ffn_out", 2 * hidden.size * D)[0]


def ffn_bwd(coords, g, kept, vec, up, down, top):
    n = g.shape[0]
    ins = [(coords, S)] + [(a, V) for a in (g, kept["slope"], kept["m"], vec, up, down)]
    outs = [((n, D), bf16), ((n, FF), bf16), ((n, D), f32), ((n, D), bf16), ((VECS, D), f32)]
    out = call(functools.partial(ffn_bwd_kernel, top), ins, outs, [], "ffn_bwd", 4 * n * D * FF, 0)
    return dict(zip(("gb", "gu", "gm", "gmb", "sums"), out, strict=True))


def attn_bwd(coords, gmb, kept, table, weight, groups):
    n = gmb.shape[0]
    ins = [(coords, S)] + [(a, V) for a in (gmb, kept["qt"], kept["kv"], kept["ot"], kept["lse"], table[1], weight)]
    rows = groups[1] * LANES
    scratch = [V((rows, n), bf16), V((PER_GROUP, n, 2 * LANES), bf16), V((2 * LANES, n), bf16)]
    outs = [((3, rows, n), bf16)] + ([((D, n), bf16)] if groups == LATE else [])
    flops = 2 * n * D * rows + 10 * n * n * rows
    kernel = functools.partial(attn_bwd_kernel, groups)
    return call(kernel, ins, outs, scratch, "attn_bwd", flops, HEADS * n * n)


def attn_after(back, kept, vec, weight, last):
    n = back["gm"].shape[0]
    ins = [(a, V) for a in (back["early"], back["late"], back["gm"], kept["x"], vec, weight)]
    outs = [((n, D), bf16 if last else f32), ((VECS, D), f32)]
    return call(attn_after_kernel, ins, outs, [V((n, D), f32)], "attn_after", 6 * n * D * D, 0)


def grads(coords, items, phase):
    arrays, plan, flops, rows = [], [], 0, 0
    for kind, lefts, right, height in items:
        index = list(range(len(arrays), len(arrays) + len(lefts)))
        arrays += [*lefts, right]
        plan.append((kind, index, len(arrays) - 1, rows))
        rows += height
        flops += 2 * arrays[0].shape[1] * D * D * 2
    leads = [(2, 2, 2, 2)] if phase else [(2, 2, 2), (2, 2), (2, 2)]
    outs = [((*lead, rows, D), bf16) for lead in leads]
    kernel = functools.partial(grads_kernel, plan, len(arrays), phase)
    ins = [(coords, S)] + [(a, V) for a in arrays]
    return call(kernel, ins, outs, [V((D, arrays[0].shape[1]), bf16), V((D, D), bf16)], "grads", flops, 0)


def mate(value):
    return lax.ppermute(value, "narrow", [(0, 1), (1, 0)])


def step(link, value):
    masks = ((8, 4, 1, 2)[link], (4, 8, 2, 1)[link])
    pairs = [(2 * w + n, 2 * (w ^ masks[n]) + n) for w in range(16) for n in range(2)]
    return lax.ppermute(value, AXES, pairs)


def relative(values, bits):
    for place_of, bit in enumerate(reversed(bits)):
        flip = 1 << place_of
        values = [jnp.where(bit > 0, values[i ^ flip], values[i]) for i in range(len(values))]
    return values


def add(*terms):
    return functools.reduce(lambda p, q: p + q, [t.astype(f32) for t in terms])


def regroup(parts, bits):
    mine = relative(parts, bits)
    return relative([mine[0]] + [lax.ppermute(mine[k], AXES, [(i, i ^ k) for i in range(32)]) for k in (1, 2, 3)], bits)


def vector_tables(gains, biases):
    gains = gains.astype(f32).reshape(LAYERS, 2, D)
    biases = biases.astype(f32).reshape(LAYERS, 11, D)
    return jnp.concatenate([gains, biases, jnp.zeros((LAYERS, VECS - 13, D), f32)], 1)


NAMES = ("down", "up", "attn")
LOTS = ((("down", 1),), (("up", 1),), (("attn", 1),), (("down", 0), ("up", 0)), (("attn", 0),))


def whole_weight(matrix, by_rows):
    if by_rows:
        cut = jnp.transpose(matrix.reshape(4, 2, 2, 2, PIECE, D), (3, 1, 2, 0, 4, 5))
    else:
        cut = jnp.transpose(matrix.reshape(4, 2, PIECE, 2, 2, D), (4, 1, 3, 0, 2, 5))
    cut = [cut[0], jnp.swapaxes(cut[1], 0, 1)]
    return [cut[kn][kb] for kb in range(2) for kn in range(2)], 0, by_rows


def whole_grad(core, rest, rows, by_rows):
    near = jnp.stack([jnp.stack([rest[2], rest[1]]), rest[0]])
    cut = jnp.stack([jnp.transpose(near, (1, 0, 3, 2, 4, 5)), core])[..., rows, :]
    if by_rows:
        return jnp.transpose(cut, (3, 4, 2, 1, 0, 5, 6)).reshape(FF, D)
    return jnp.transpose(cut, (3, 4, 2, 5, 1, 0, 6)).reshape(D, FF)


def fetch_plain(w_qkv, w_out, w_up, w_down, gains, biases):
    def whole(value, rows):
        return lax.all_gather(value[None], AXES, axis=1, tiled=True).reshape(rows, -1)

    weights = {}
    for l in range(LAYERS):
        attn = jnp.concatenate([whole(w_qkv[l], D), whole(w_out[l], D)], 1)
        weights["attn", l] = whole_weight(attn, False)
        weights["up", l] = whole_weight(whole(w_up[l], D), False)
        weights["down", l] = whole_weight(whole(w_down[l], FF), True)
    return weights, vector_tables(whole(gains, 1)[0], whole(biases, 1)[0])


class Lot:
    def first(self, core, rest):
        self.core, self.rest = core, rest
        return add(rest[0], core[1]).astype(bf16)

    def second(self, got):
        self.got = got
        return add(self.rest[1], self.core[0, 1], got[1]).astype(bf16)

    def third(self, got):
        total = add(self.rest[2], self.core[0, 0], self.got[0], got)
        self.total = total[0]
        return total[1].astype(bf16)

    def fourth(self, got):
        total = add(self.total, got)
        self.total = total[0]
        return total[1].astype(bf16)

    def last(self, got):
        return add(self.total, got)


def stage(*groups):
    flat, tree = jax.tree.flatten(groups)
    return jax.tree.unflatten(tree, lax.optimization_barrier(flat))


def device_bits():
    wide = lax.axis_index("wide")
    return [(wide >> 3) & 1, (wide >> 2) & 1, (wide >> 1) & 1, wide & 1, lax.axis_index("narrow")]


def coordinates(values):
    return jnp.stack([jnp.asarray(v, jnp.int32) for v in values])


def layer_grads(sums):
    both = jnp.stack(sums)
    return both[:, :2].reshape(-1), both[:, 2:13].reshape(-1)


def gradient_blocks(coords, lot, kept, back, phase):
    items = []
    for name, l in LOTS[lot]:
        if name == "attn":
            items.append((name, [kept[l]["at"], kept[l]["ot"], back[l]["early"], back[l]["late"]], back[l]["flip"], PIECE))
        elif name == "up":
            items.append((name, [kept[l]["bt"]], back[l]["gu"], PIECE))
        else:
            items.append((name, [kept[l]["zt"]], back[l]["gb"], PIECE))
    outs = grads(coords, items, phase)
    return outs[0] if phase else outs


def shares_of(parts, bits):
    rows = D // 32
    cut = jnp.stack(parts)
    whole = jnp.concatenate(regroup([cut[:, s * rows : (s + 1) * rows] for s in range(4)], bits[3:]), 2)
    return [whole[i] for i in range(len(parts))]


def body(tokens, lengths, w_qkv, w_out, w_up, w_down, gains, biases, cotangent):
    args = (tokens, lengths, w_qkv, w_out, w_up, w_down, gains, biases, cotangent)
    if lax.axis_size("wide") == 16 and lax.axis_size("narrow") == 2:
        return staged(*args)
    return plain(*args)


def plain(tokens, lengths, w_qkv, w_out, w_up, w_down, gains, biases, cotangent):
    length = tokens.shape[0] // lengths.shape[0]
    coords = coordinates([0, 0, 0, 0, lengths[0]])
    table = rotary_tables(length)
    weights, vectors = fetch_plain(w_qkv, w_out, w_up, w_down, gains, biases)
    kept, back, wholes, x = [], [{}, {}], [], tokens
    for l in range(LAYERS):
        held, whole = attn_fwd(coords, x, vectors[l], table, [weights[name, l] for name in ("attn", "up", "down")])
        x, more, *_ = ffn_fwd(coords, held, vectors[l], whole[1], whole[2], l == LAYERS - 1)
        kept.append(held | more)
        wholes.append(whole)
    output = ffn_out(coords, kept[-1], x, vectors[-1], wholes[-1][2])
    grad, sums = cotangent, [None] * LAYERS
    for l in reversed(range(LAYERS)):
        last = l == 0
        back[l] = ffn_bwd(coords, grad, kept[l], vectors[l], wholes[l][1], wholes[l][2], not last)
        (back[l]["early"],) = attn_bwd(coords, back[l]["gmb"], kept[l], table, wholes[l][0], EARLY)
        back[l]["late"], back[l]["flip"] = attn_bwd(coords, back[l]["gmb"], kept[l], table, wholes[l][0], LATE)
        grad, more = attn_after(back[l], kept[l], vectors[l], wholes[l][0], last)
        sums[l] = back[l]["sums"] + more
    matrices = {}
    for lot, keys in enumerate(LOTS):
        core, rest = [gradient_blocks(coords, lot, kept, back, phase) for phase in (1, 0)]
        for i, key in enumerate(keys):
            rows = slice(i * PIECE, (i + 1) * PIECE)
            matrices[key] = whole_grad(core, rest, rows, key[0] == "down").astype(f32)
    devices = lax.axis_size(AXES)
    parts = []
    for name, begin, end in (("attn", 0, 3 * D), ("attn", 3 * D, FF), ("up", 0, FF), ("down", 0, D)):
        parts += [matrices[name, l][:, begin:end].reshape(devices, -1) for l in range(LAYERS)]
    parts += [v.reshape(devices, -1) for v in layer_grads(sums)]
    summed = lax.psum_scatter(jnp.concatenate(parts, 1), AXES, scatter_dimension=0, tiled=True)[0]
    ends = np.cumsum([p.shape[1] for p in parts])
    cut = [summed[end - p.shape[1] : end] for end, p in zip(ends, parts, strict=True)]
    outs = [jnp.stack(cut[i : i + LAYERS]) for i in range(0, 4 * LAYERS, LAYERS)] + cut[4 * LAYERS :]
    return (output, grad, *outs)


def turned(value, bits):
    value = value.reshape(2, 2, 2, 2, 2, -1)
    for axis, bit in enumerate(bits):
        value = jnp.where(bit > 0, jnp.flip(value, axis), value)
    cores = [jnp.transpose(value, order) for order in ((4, 2, 3, 1, 0, 5), (4, 3, 2, 0, 1, 5))]
    own = jnp.where(bits[4] > 0, cores[1][0], cores[0][0])
    other = jnp.where(bits[4] > 0, cores[0][1], cores[1][1])
    return jnp.stack([own, other])


def ordered(bit, own, got):
    return jnp.stack([jnp.where(bit > 0, got, own), jnp.where(bit > 0, own, got)])


def staged(tokens, lengths, w_qkv, w_out, w_up, w_down, gains, biases, cotangent):
    length = tokens.shape[0] // lengths.shape[0]
    bits = device_bits()
    coords = coordinates([lax.axis_index("wide") >> 2, *bits[2:], lengths[0]])
    table = rotary_tables(length)
    rows = D // 32
    weights, whole = {}, {}

    z1, z0, y, x, n = bits
    third, fourth = jnp.where(n > 0, y, x), jnp.where(n > 0, x, y)

    def link0(value):
        return ordered(jnp.where(n > 0, z0, z1), value, step(0, value))

    def link1(value):
        return value, step(1, value)

    def by_z(pair):
        own, got = pair
        blocks = []
        for high in range(2):
            for low in range(2):
                core0 = jnp.where(z0 == low, own[high], got[high])
                blocks.append(jnp.where(n > 0, jnp.where(z1 == high, own[low], got[low]), core0))
        return jnp.stack(blocks)

    def link2(value):
        return ordered(third, value, step(2, value))

    def arrived(keys, *pieces):
        offset = 0
        for key, height in keys:
            weights[key] = (list(pieces), offset, key[0] == "down")
            offset += height

    small = jnp.concatenate([gains, biases])
    width = small.shape[0]
    c0 = jnp.concatenate([w_down[0].reshape(PIECE, D), jnp.zeros((16, D), bf16).at[0, :width].set(small)])
    c0, w_qkv, w_out, w_up = stage(c0, w_qkv, w_out, w_up)
    t0 = link0(c0)
    flat = []
    for l in range(LAYERS):
        flat.append(jnp.concatenate([w_qkv[l].reshape(rows, 3 * D), w_out[l].reshape(rows, D)], 1))
        flat.append(w_up[l].reshape(rows, FF))
    flat = jnp.stack(flat)
    parts = [flat[:, :, s * D : (s + 1) * D] for s in range(4)]
    t0, parts = stage(t0, parts)
    u0 = link1(t0)
    c1, up0, attn1, up1 = jnp.concatenate(regroup(parts, bits[3:]), 1)
    c2, c3 = jnp.concatenate([up0, attn1]), jnp.concatenate([w_down[1].reshape(PIECE, D), up1])
    zz0, c1, c2, c3 = stage(by_z(u0), c1, c2, c3)
    near0, t12 = stage(link2(zz0), link0(jnp.concatenate([c1, c2])))
    t1, t2 = t12[:, :PIECE], t12[:, PIECE:]
    far0, mate0, u1 = step(3, near0), mate(near0), link1(t1)
    far0, mate0, zz1, t2 = stage(far0, mate0, by_z(u1), t2)
    near1, far_mate0, u2, t3 = link2(zz1), mate(far0), link1(t2), link0(c3)
    near1, far_mate0, t3 = stage(near1, far_mate0, t3)
    zz2 = by_z(u2)
    arrived(((("down", 0), PIECE),), near0, mate0, far0, far_mate0)
    far1, mate1, near2, u3 = step(3, near1), mate(near1), link2(zz2), link1(t3)
    whole["down", 0] = assemble(coords, weights["down", 0])
    own, other = [], []
    for first, second, to in ((near0, far0, own), (mate0, far_mate0, other)):
        turn = n if to is own else 1 - n
        both = ordered(jnp.where(turn > 0, x, y), first[:, :, PIECE, :width], second[:, :, PIECE, :width])
        to.append(jnp.where(turn > 0, jnp.transpose(both, (2, 1, 0, 3)), jnp.transpose(both, (2, 0, 1, 3))))
    both = ordered(n, own[0], other[0])
    both = jnp.transpose(both, (1, 2, 3, 0, 4)).reshape(32, width)
    vectors = vector_tables(both[:, : gains.shape[0]].reshape(-1), both[:, gains.shape[0] :].reshape(-1))
    far1, mate1, near2, zz3, vectors, whole = stage(far1, mate1, near2, by_z(u3), vectors, whole)
    far_mate1, near2, zz3 = stage(mate(far1), near2, zz3)
    arrived(((("attn", 0), PIECE),), near1, mate1, far1, far_mate1)
    kept, back = [None, None], [None, None]
    far2, mate2 = step(3, near2), mate(near2)
    kept[0], got = attn_fwd(coords, tokens, vectors[0], table, [weights["attn", 0]])
    whole["attn", 0] = got[0]
    far2, mate2, kept[0] = stage(far2, mate2, kept[0])
    far_mate2, kept[0], zz3 = stage(mate(far2), kept[0], zz3)
    arrived(((("up", 0), PIECE), (("attn", 1), PIECE)), near2, mate2, far2, far_mate2)
    got3 = step(2, zz3)
    h, more, whole["up", 0], _ = ffn_fwd(coords, kept[0], vectors[0], weights["up", 0], whole["down", 0], False)
    kept[0] |= more
    got3, h = stage(got3, h)
    near3, h = stage(ordered(third, zz3, got3), h)
    far3, mate3 = step(3, near3), mate(near3)
    kept[1], got = attn_fwd(coords, h, vectors[1], table, [weights["attn", 1]])
    whole["attn", 1] = got[0]
    far3, mate3, kept[1] = stage(far3, mate3, kept[1])
    arrived(((("down", 1), PIECE), (("up", 1), PIECE)), near3, mate3, far3, mate(far3))
    hidden, more, whole["up", 1], whole["down", 1] = ffn_fwd(
        coords, kept[1], vectors[1], weights["up", 1], weights["down", 1], True
    )
    kept[1] |= more

    d1, u1, a1, du0, a0, extra = [Lot() for _ in range(6)]

    def blocks(lot, phase):
        return gradient_blocks(coords, lot, kept, back, phase)

    live = jnp.arange(length, dtype=jnp.int32)[:, None] < lengths[0]
    back[1] = {"gb": jnp.where(live, cotangent, jnp.zeros((), bf16))}
    core, back[1] = stage(blocks(0, 1), back[1])
    first, cotangent = stage(d1.first(mate(core), blocks(0, 0)), cotangent)

    got_d1 = step(3, first)
    back[1] |= ffn_bwd(coords, cotangent, kept[1], vectors[1], whole["up", 1], whole["down", 1], True)
    got_d1, core, back[1] = stage(got_d1, blocks(1, 1), back[1])
    second, core, back[1] = stage(d1.second(got_d1), core, back[1])

    got_d1 = step(2, second)
    core, rest = stage(mate(core), blocks(1, 0))
    first, back[1] = stage(u1.first(core, rest), back[1])

    got_u1 = step(3, first)
    (back[1]["early"],) = attn_bwd(coords, back[1]["gmb"], kept[1], table, whole["attn", 1], EARLY)
    got_u1, got_d1, back[1] = stage(got_u1, got_d1, back[1])
    second, third, back[1] = stage(u1.second(got_u1), d1.third(got_d1), back[1])

    got_u1, got_d1 = step(2, second), step(1, third)
    back[1]["late"], back[1]["flip"] = attn_bwd(coords, back[1]["gmb"], kept[1], table, whole["attn", 1], LATE)
    got_u1, got_d1, core, back[1] = stage(got_u1, got_d1, blocks(2, 1), back[1])
    third, fourth, core, back[1] = stage(u1.third(got_u1), d1.fourth(got_d1), core, back[1])

    got_u1, got_d1 = step(1, third), step(0, fourth)
    core, rest = stage(mate(core), blocks(2, 0))
    first, back[1] = stage(a1.first(core, rest), back[1])

    got_a1 = step(3, first)
    grad, more = attn_after(back[1], kept[1], vectors[1], whole["attn", 1], False)
    sums = [None, back[1]["sums"] + more]
    back[0] = ffn_bwd(coords, grad, kept[0], vectors[0], whole["up", 0], whole["down", 0], False)
    got_a1, got_u1, got_d1, core, back[0] = stage(got_a1, got_u1, got_d1, blocks(3, 1), back[0])
    second, fourth, core, back[0] = stage(a1.second(got_a1), u1.fourth(got_u1), core, back[0])

    got_a1, got_u1, core, rest = stage(step(2, second), step(0, fourth), mate(core), blocks(3, 0))
    first, third, back[0], hidden = stage(du0.first(core, rest), a1.third(got_a1), back[0], hidden)

    got_du0, got_a1 = step(3, first), step(1, third)
    (back[0]["early"],) = attn_bwd(coords, back[0]["gmb"], kept[0], table, whole["attn", 0], EARLY)
    back[0]["late"], back[0]["flip"] = attn_bwd(coords, back[0]["gmb"], kept[0], table, whole["attn", 0], LATE)
    output = ffn_out(coords, kept[1], hidden, vectors[1], whole["down", 1])
    got_du0, got_a1, back[0], output = stage(got_du0, got_a1, back[0], output)
    second, fourth, back[0] = stage(du0.second(got_du0), a1.fourth(got_a1), back[0])

    got_du0, got_a1 = step(2, second), step(0, fourth)
    core = blocks(4, 1)
    grad, more = attn_after(back[0], kept[0], vectors[0], whole["attn", 0], True)
    sums[0] = back[0]["sums"] + more
    got_du0, got_a1, core, grad, sums, back[0] = stage(got_du0, got_a1, core, grad, sums, back[0])
    third, core, back[0] = stage(du0.third(got_du0), core, back[0])

    got_du0 = step(1, third)
    core, rest = stage(mate(core), blocks(4, 0))
    first, sums = stage(a0.first(core, rest), sums)

    got_a0 = step(3, first)
    small = turned(jnp.concatenate([v.reshape(32, -1) for v in layer_grads(sums)], 1), bits)
    first = extra.first(mate(small[1]), [small[0, 1], small[0, 0, 1], small[0, 0, 0]])
    got_a0, got_du0, first, got_d1, got_u1, got_a1, grad = stage(got_a0, got_du0, first, got_d1, got_u1, got_a1, grad)
    second, first, fourth = stage(a0.second(got_a0), first, du0.fourth(got_du0))

    got_a0, got_x, got_du0 = step(2, second), step(3, first), step(0, fourth)
    shares = [u1.last(got_u1), a1.last(got_a1)]
    got_a0, got_x, got_du0, shares = stage(got_a0, got_x, got_du0, shares)
    third, second, got_du0 = stage(a0.third(got_a0), extra.second(got_x), got_du0)

    got_a0, got_x = step(1, third), step(2, second)
    done = du0.last(got_du0)
    downs = jnp.stack([done[:PIECE].reshape(-1), d1.last(got_d1).reshape(-1)])
    up1, attn1, up0 = shares_of([*shares, done[PIECE:]], bits)
    got_a0, got_x, up1, attn1, up0, downs = stage(got_a0, got_x, up1, attn1, up0, downs)
    fourth, third = stage(a0.fourth(got_a0), extra.third(got_x))

    got_a0, got_x = step(0, fourth), step(1, third)
    ups = jnp.stack([up0.reshape(-1), up1.reshape(-1)])
    got_a0, got_x, ups = stage(got_a0, got_x, ups)
    (attn0,) = shares_of([a0.last(got_a0)], bits)
    mine = extra.last(step(0, extra.fourth(got_x)))
    return (
        output,
        grad,
        jnp.stack([v[:, : 3 * D].reshape(-1) for v in (attn0, attn1)]),
        jnp.stack([v[:, 3 * D :].reshape(-1) for v in (attn0, attn1)]),
        ups,
        downs,
        mine[: gains.shape[0]],
        mine[gains.shape[0] :],
    )


def solution(mesh):
    both, flat, rows = P(AXES), P(None, AXES), P(AXES, None)
    return jax.shard_map(
        body,
        mesh=mesh,
        in_specs=(rows, both, flat, flat, flat, flat, both, both, rows),
        out_specs=(rows, rows, flat, flat, flat, flat, both, both),
        check_vma=False,
    )
```
